128 devices in a mesh: prompt: 8 (over z, core), seq: 16 (over x, y).
Axes of the slice: x: 4, y: 4, z: 4, core: 2. Of those that a mesh axis runs over, the one named last changes fastest.
Arguments:
- tokens: bfloat16 [8, 2048, 2048], P('prompt', 'seq'), may hold values from -6 to 6
- span_lengths: int32 [8], P('prompt'), may hold values from 512 to 2048, as said below
- state_slots: int32 [8], P('prompt'), may hold values from 0 to 7
- expert_ids: int32 [8, 2048, 10], P('prompt', 'seq'), may hold values from 0 to 255, all different within a row; in each aligned block of 128 rows (0 to 127, 128 to 255, ..., all dimensions but the last counted through in order) at most 8 rows name the same one
- state_pool: float32 [8, 32, 128, 128], P(None, 'seq'), may hold values from -3 to 3
- attn_gain: float32 [2048], replicated, may hold values from 0.5 to 1.5
- w_query: bfloat16 [2048, 2048], P(None, 'seq'), may hold values from -0.125 to 0.125
- w_key: bfloat16 [2048, 2048], P(None, 'seq'), may hold values from -0.125 to 0.125
- w_value: bfloat16 [2048, 4096], P(None, 'seq'), may hold values from -0.125 to 0.125
- w_zgate: bfloat16 [2048, 4096], P(None, 'seq'), may hold values from -0.125 to 0.125
- w_heads: bfloat16 [2048, 2, 32], P(None, None, 'seq'), may hold values from -0.125 to 0.125
- decay_rate: float32 [32], P('seq'), may hold values from 0.00048828125 to 0.1
- head_gain: float32 [128], replicated, may hold values from 0.25 to 2.5
- w_output: bfloat16 [4096, 2048], P('seq'), may hold values from -0.09375 to 0.09375
- moe_gain: float32 [2048], replicated, may hold values from 0.5 to 1.5
- router: bfloat16 [2048, 256], replicated
- w_expert_in: bfloat16 [256, 2048, 1024], P(('prompt', 'seq')), may hold values from -0.125 to 0.125
- w_expert_out: bfloat16 [256, 512, 2048], P(('prompt', 'seq')), may hold values from -0.25 to 0.25
Outputs:
- attended: bfloat16 [8, 2048, 2048], P('prompt', 'seq')
- expert_out: bfloat16 [8, 2048, 2048], P('prompt', 'seq')
- new_states: float32 [8, 32, 128, 128], P('prompt', 'seq')
The draws below stay inside these ranges and needn't reach their ends.
Inputs may be any that keep to these rules, and one draw needn't show every extreme that they name: `span_lengths`: each prompt's live tokens are its first slots; at least one prompt fills all 2048 slots. `expert_ids`: among the rows of one device no expert is named by more than 8 rows; padded slots are routed too.
All inputs are finite; a program needn't handle non-finite values.
Results may differ from the reference program's by a relative error of at most 0.03.
Values may be sent and summed in bfloat16 or wider, within the bound.
A program may use at most 128 MiB of HBM per device.

```python
import math
import jax
import jax.numpy as jnp
import numpy as np
from jax import lax

D = 2048
HK = 16
HV = 32
DH = 128
FFE = 512
TOP = 10
EXPERTS = 256
CAP = 8
BLK = 256
SLOTS = 8
TOK_DEV = 128
PROMPTS = 8
SPAN = 2048
N_PROMPT = 8
N_SEQ = 16


def draw_span_lengths(key, part):
    key = jax.random.fold_in(key, 5)
    first, second = jax.random.split(key)
    drawn = jax.random.randint(first, (PROMPTS,), SPAN // 4, SPAN + 1)
    full = jax.random.randint(second, (), 0, PROMPTS)
    return jnp.where(jnp.arange(PROMPTS) == full, SPAN, drawn).astype(jnp.int32)


def draw_router(key, part):
    key = jax.random.fold_in(key, 11)
    first = jax.random.fold_in(key, 0)
    base = jax.random.normal(first, (D, EXPERTS), jnp.float32) * D ** (-0.5)
    return (base * 0.5).astype(jnp.bfloat16)


def place_ends(values, rng, smallest, top_value):
    longest = values.shape.index(max(values.shape))
    spots = []
    for shift in (0, 1):
        where = [jax.random.randint(jax.random.fold_in(rng, axis), (), 0, length) for axis, length in enumerate(values.shape)]
        where[longest] = (where[longest] + shift) % values.shape[longest]
        spots.append(tuple(where))
    return values.at[spots[0]].set(smallest).at[spots[1]].set(top_value)


def level_of(rng, shape, pieces, smallest, top_value):
    def one(position, parts):
        steps = jax.random.uniform(jax.random.fold_in(jax.random.fold_in(rng, 6), position), (parts,), jnp.float32, smallest / len(pieces), top_value / len(pieces))
        return jnp.repeat(jnp.exp(steps), shape[position] // parts).reshape((-1,) + (1,) * (len(shape) - position - 1))

    factor_of = one(*pieces[0])
    for cut in pieces[1:]:
        factor_of = factor_of * one(*cut)
    return factor_of


def deal_out(stream_key, own, number, rows, amount, top, reach, slope):
    sequence = jax.random.permutation(stream_key, amount)
    packed, ordinary = shares(amount, rows * top, reach, slope, True), shares(amount, rows * top, reach, slope, False)
    places = jnp.arange(amount)

    def named(sizes, rotation):
        used = int((sizes > 0).sum())
        fixed = max(1, used // 4)
        moved = fixed + (places - fixed + rotation * (used - fixed)) % max(1, amount - fixed)
        return jnp.zeros((amount,), jnp.int32).at[sequence[jnp.where(places < fixed, places, moved)]].set(jnp.asarray(sizes, jnp.int32))

    sizes = jnp.where(number % 4 == 0, named(packed, number // 4), named(ordinary, number - number // 4 - 1))
    mixed = jax.random.permutation(jax.random.fold_in(own, 3), amount)
    giver, taker = mixed[0:amount // 2 * 2:2], mixed[1:amount // 2 * 2:2]
    slack = jnp.minimum(sizes[giver] - 1, reach - sizes[taker]) // 2
    slack = jnp.where((giver == sequence[0]) | (taker == sequence[0]) | (sizes[taker] == 0), 0, jnp.maximum(slack, 0))
    moved = jax.random.randint(jax.random.fold_in(own, 4), (amount // 2,), 0, 1 << 20) % (slack + 1)
    sizes = sizes.at[giver].add(-moved).at[taker].add(moved)
    labels = jnp.searchsorted(jnp.cumsum(sizes), jnp.arange(rows * top), side="right").astype(jnp.int32)
    table = labels.reshape(top, rows).T
    table = table[jax.random.permutation(jax.random.fold_in(own, 1), rows)]
    rotation = jax.random.randint(jax.random.fold_in(own, 2), (rows, 1), 0, top)
    return jnp.take_along_axis(table, (jnp.arange(top)[None, :] + rotation) % top, axis=1)


def shares(count, total, reach, slope, full):
    loads = [(1 << 20) // math.isqrt(standing ** slope) + 1 for standing in range(1, count + 1)]
    largest = reach if full else min(reach, max(-(-total // count), total * loads[0] // sum(loads)))
    least = 1 if total - largest >= count - 1 else 0
    given, rest = [largest] + [least] * (count - 1), total - largest - least * (count - 1)
    while rest > 0:
        movable = [i for i in range(1, count) if given[i] < largest] or [i for i in range(1, count) if given[i] < reach]
        mass, budget = sum([loads[i] for i in movable]), rest
        for i in movable:
            addition = min(reach - given[i], max(1, budget * loads[i] // mass), rest)
            given[i] = given[i] + addition
            rest = rest - addition
    return np.array(given)


def scatter_about(key, extent, scale, limit, cuts=(), kind=jnp.bfloat16):
    entries = jax.random.normal(key, extent, jnp.float32) * scale
    if len(cuts) > 0:
        entries = level_of(key, extent, cuts, -0.22, 0.18) * entries
    return jnp.clip(entries, min=-limit, max=limit).astype(kind)


def setup_inputs(seed: int = 0) -> dict:
    key_list = jax.random.split(jax.random.key(seed), 19)
    tokens = scatter_about(key_list[0], (PROMPTS, SPAN, D), 1.0, 6.0, ((0, 8), (1, 16)))
    span_lengths = draw_span_lengths(jax.random.fold_in(key_list[18], 71), 0)
    state_slots = place_ends(jax.random.randint(key_list[2], (PROMPTS,), 0, SLOTS), jax.random.fold_in(key_list[2], 1), 0, SLOTS - 1).astype(jnp.int32)
    expert_ids_keys = jax.random.split(jax.random.fold_in(key_list[3], 1), PROMPTS * SPAN // TOK_DEV)
    expert_ids_turns = jax.random.permutation(jax.random.fold_in(key_list[3], 3), PROMPTS * SPAN // TOK_DEV)
    expert_ids = jax.vmap(lambda own, number: deal_out(jax.random.fold_in(key_list[3], 2), own, number, TOK_DEV, EXPERTS, TOP, CAP, 2))(expert_ids_keys, expert_ids_turns).reshape((PROMPTS, SPAN, TOP))
    state_pool = scatter_about(key_list[4], (SLOTS, HV, DH, DH), 0.5, 3.0, ((1, 16),), jnp.float32)
    attn_gain = jnp.clip(1.0 + 0.1 * jax.random.normal(key_list[5], (D,), jnp.float32), 0.5, 1.5)
    w_query = scatter_about(key_list[6], (D, HK * DH), D ** -0.5, 0.125, ((1, 16),))
    w_key = scatter_about(key_list[7], (D, HK * DH), D ** -0.5, 0.125, ((1, 16),))
    w_value = scatter_about(key_list[8], (D, HV * DH), D ** -0.5, 0.125, ((1, 16),))
    w_zgate = scatter_about(key_list[9], (D, HV * DH), D ** -0.5, 0.125, ((1, 16),))
    w_heads = scatter_about(key_list[10], (D, 2, HV), D ** -0.5, 0.125, ((2, 16),))
    decay_rate = jnp.clip(jnp.exp(math.log(0.1) - 5.322034 * jax.random.uniform(key_list[11], (HV,), jnp.float32) ** level_of(key_list[11], (HV,), ((0, 16),), -0.2, 0.2)), 0.00048828125, 0.1)
    head_gain = jnp.clip(jnp.exp(jax.random.uniform(key_list[12], (DH,), jnp.float32, math.log(0.25), math.log(2.5))), 0.25, 2.5)
    w_output = scatter_about(key_list[13], (HV * DH, D), (HV * DH) ** -0.5, 0.09375, ((0, 16),))
    moe_gain = jnp.clip(1.0 + 0.1 * jax.random.normal(key_list[14], (D,), jnp.float32), 0.5, 1.5)
    router = draw_router(jax.random.fold_in(key_list[18], 71), 0)
    w_expert_in = scatter_about(key_list[16], (EXPERTS, D, 2 * FFE), D ** -0.5, 0.125, ((0, 128),))
    w_expert_out = scatter_about(key_list[17], (EXPERTS, FFE, D), FFE ** -0.5, 0.25, ((0, 128),))
    return dict(tokens=tokens, span_lengths=span_lengths, state_slots=state_slots, expert_ids=expert_ids, state_pool=state_pool, attn_gain=attn_gain, w_query=w_query, w_key=w_key, w_value=w_value, w_zgate=w_zgate, w_heads=w_heads, decay_rate=decay_rate, head_gain=head_gain, w_output=w_output, moe_gain=moe_gain, router=router, w_expert_in=w_expert_in, w_expert_out=w_expert_out)


EPS = 1e-06

def rms_scale(values, gain):
    mean = lax.optimization_barrier(jnp.mean(values * values, axis=-1, keepdims=True))
    return values * lax.rsqrt(mean + EPS) * gain

def unit_rows(values):
    return values * lax.rsqrt(lax.optimization_barrier(jnp.sum(values * values, axis=-1, keepdims=True)) + EPS)

def block_prepare(query, keys, values, beta, logdec, size):
    span, heads, width = query.shape
    count = span // size

    def blocks(array):
        return jnp.swapaxes(array.reshape((count, size, heads) + array.shape[2:]), 1, 2)
    query, keys, values, beta, logdec = (blocks(query), blocks(keys), blocks(values), blocks(beta), blocks(logdec))
    highest = lax.Precision.HIGHEST
    cumul = jnp.cumsum(logdec, axis=-1)
    diff = cumul[..., :, None] - cumul[..., None, :]
    rows_iota = lax.broadcasted_iota(jnp.int32, (size, size), 0)
    cols_iota = lax.broadcasted_iota(jnp.int32, (size, size), 1)
    decay = jnp.exp(jnp.minimum(diff, 0.0))
    strict = jnp.where(rows_iota > cols_iota, decay, 0.0)
    within = jnp.where(rows_iota >= cols_iota, decay, 0.0)
    key_key = jnp.einsum('nhid,nhjd->nhij', keys, keys, precision=highest)
    query_key = jnp.einsum('nhid,nhjd->nhij', query, keys, precision=highest)
    system = jnp.eye(size, dtype=jnp.float32) + beta[..., None] * key_key * strict
    start = jnp.exp(cumul)
    right = jnp.concatenate([beta[..., None] * values, (beta * start)[..., None] * keys], axis=-1)
    solved = jax.scipy.linalg.solve_triangular(system, right, lower=True, unit_diagonal=True)
    upd_values = solved[..., :width]
    upd_keys = solved[..., width:]
    tail_keys = jnp.exp(cumul[..., -1:] - cumul)[..., None] * keys
    last = jnp.exp(cumul[..., -1])
    return (upd_values, upd_keys, query_key * within, start, tail_keys, last, query)

def block_step(state, block):
    upd_values, upd_keys, attn, start, tail_keys, last, query = block
    highest = lax.Precision.HIGHEST
    corrected = upd_values - jnp.einsum('hik,hvk->hiv', upd_keys, state, precision=highest)
    output = start[..., None] * jnp.einsum('hik,hvk->hiv', query, state, precision=highest)
    output = output + jnp.einsum('hij,hjv->hiv', attn, corrected, precision=highest)
    new_state = last[:, None, None] * state + jnp.einsum('hiv,hik->hvk', corrected, tail_keys, precision=highest)
    return (new_state, output)

def unblock(outputs):
    count, heads, size, width = outputs.shape
    return jnp.swapaxes(outputs, 1, 2).reshape(count * size, heads, width)

def reference(tokens, span_lengths, state_slots, expert_ids, state_pool, attn_gain, w_query, w_key, w_value, w_zgate, w_heads, decay_rate, head_gain, w_output, moe_gain, router, w_expert_in, w_expert_out):
    ratio = HV // HK

    def one_prompt(item):
        rows_in, length, slot, chosen_ids = item
        live = (lax.broadcasted_iota(jnp.int32, (SPAN,), 0) < length).astype(jnp.float32)
        normed = rms_scale(rows_in.astype(jnp.float32), attn_gain).astype(jnp.bfloat16)
        query = jnp.dot(normed.astype(jnp.float32), w_query.astype(jnp.float32), preferred_element_type=jnp.float32).reshape(SPAN, HK, DH)
        keys = jnp.dot(normed.astype(jnp.float32), w_key.astype(jnp.float32), preferred_element_type=jnp.float32).reshape(SPAN, HK, DH)
        values = jnp.dot(normed.astype(jnp.float32), w_value.astype(jnp.float32), preferred_element_type=jnp.float32).reshape(SPAN, HV, DH)
        zgate = jnp.dot(normed.astype(jnp.float32), w_zgate.astype(jnp.float32), preferred_element_type=jnp.float32).reshape(SPAN, HV, DH)
        head_logits = jnp.dot(normed.astype(jnp.float32), w_heads.reshape(D, 2 * HV).astype(jnp.float32), preferred_element_type=jnp.float32).reshape(SPAN, 2, HV)
        query = jnp.repeat(unit_rows(query) * DH ** (-0.5), ratio, axis=1)
        keys = jnp.repeat(unit_rows(keys), ratio, axis=1)
        beta = jax.nn.sigmoid(head_logits[:, 1, :]) * live[:, None]
        logdec = -decay_rate[None, :] * jax.nn.softplus(head_logits[:, 0, :]) * live[:, None]
        state = lax.dynamic_index_in_dim(state_pool, slot, 0, keepdims=False)
        prepared = block_prepare(query, keys, values, beta, logdec, BLK)
        final, outputs = lax.scan(block_step, state, prepared)
        heads = unblock(outputs)
        gated = (rms_scale(heads, head_gain) * jax.nn.silu(zgate)).astype(jnp.bfloat16).reshape(SPAN, HV * DH)
        summed = jnp.dot(gated.astype(jnp.float32), w_output.astype(jnp.float32), preferred_element_type=jnp.float32)
        attended = (summed * live[:, None]).astype(jnp.bfloat16)
        residual = rows_in.astype(jnp.float32) + attended.astype(jnp.float32)
        moe_input = rms_scale(residual, moe_gain).astype(jnp.bfloat16)
        logits = jnp.dot(moe_input.astype(jnp.float32), router.astype(jnp.float32), preferred_element_type=jnp.float32)
        picked = jnp.take_along_axis(logits, chosen_ids, axis=-1)
        weights = jax.nn.softmax(picked, axis=-1) * live[:, None]
        return (attended, moe_input, weights, final)
    attended, moe_input, weights, new_states = lax.map(one_prompt, (tokens, span_lengths, state_slots, expert_ids))
    flat_input = moe_input.reshape(PROMPTS * SPAN, D)
    flat_ids = expert_ids.reshape(PROMPTS * SPAN, TOP)
    flat_weights = weights.reshape(PROMPTS * SPAN, TOP)
    bound = N_PROMPT * N_SEQ * CAP

    def one_expert(total, expert):
        member = flat_ids == expert
        weight = lax.optimization_barrier(jnp.sum(jnp.where(member, flat_weights, 0.0), axis=-1))
        order = jnp.argsort(jnp.where(jnp.any(member, axis=-1), 0, 1).astype(jnp.int32), stable=True)[:bound]
        picked_rows = flat_input[order]
        pair = jnp.dot(picked_rows.astype(jnp.float32), w_expert_in[expert].astype(jnp.float32), preferred_element_type=jnp.float32)
        inner = (jax.nn.silu(pair[:, :FFE]) * pair[:, FFE:]).astype(jnp.bfloat16)
        result = jnp.dot(inner.astype(jnp.float32), w_expert_out[expert].astype(jnp.float32), preferred_element_type=jnp.float32).astype(jnp.bfloat16)
        return (total.at[order].add(weight[order][:, None] * result.astype(jnp.float32)), None)
    total, _ = lax.scan(one_expert, jnp.zeros((PROMPTS * SPAN, D), jnp.float32), jnp.arange(EXPERTS, dtype=jnp.int32))
    expert_out = total.astype(jnp.bfloat16).reshape(PROMPTS, SPAN, D)
    return (attended, expert_out, new_states)
```

```python
import functools
import jax
import jax.numpy as jnp
from jax import lax
from jax.sharding import PartitionSpec as P
from jax.experimental import pallas as pl
from jax.experimental.pallas import tpu as pltpu

EPS = 1e-06
CH = 128
F32 = jnp.float32
BF16 = jnp.bfloat16


def mm(a, b):
    return jnp.dot(a, b, preferred_element_type=F32)


def halves(a):
    high = a.astype(BF16)
    return high, (a - high.astype(F32)).astype(BF16)


def mm3(a, b):
    a_high, a_low = halves(a)
    b_high, b_low = halves(b)
    wide = mm(jnp.concatenate([a_high, a_low], axis=1), jnp.concatenate([b_high, b_high], axis=0))
    return wide + mm(a_high, b_low)


def unit_lower_inverse(lows, rows, cols):
    eye = jnp.where(rows == cols, 1.0, 0.0)
    inverses = [eye - jnp.where(rows // 2 == cols // 2, low, 0.0) for low in lows]
    size = 2
    while size < CH:
        mask = (rows // (2 * size) == cols // (2 * size)) & (rows // size != cols // size)
        inner = [mm3(jnp.where(mask, low, 0.0), inv) for low, inv in zip(lows, inverses)]
        inverses = [inv - mm3(inv, part) for inv, part in zip(inverses, inner)]
        size *= 2
    return inverses


def delta_body(tile, base, length, proj, rate, gain, state):
    rows = lax.broadcasted_iota(jnp.int32, (CH, CH), 0)
    cols = lax.broadcasted_iota(jnp.int32, (CH, CH), 1)
    tri = jnp.where(rows >= cols, 1.0, 0.0)
    chunks = tile // CH
    prep = []
    lows = []
    for c in range(chunks):
        part = proj[c * CH : (c + 1) * CH]
        q, k = part[:, 0:128], part[:, 128:256]
        q = q * (lax.rsqrt(jnp.sum(q * q, axis=-1, keepdims=True) + EPS) * 128 ** (-0.5))
        k = k * lax.rsqrt(jnp.sum(k * k, axis=-1, keepdims=True) + EPS)
        logits = part[:, 768:896]
        live = jnp.where(base + c * CH + rows < length, 1.0, 0.0)
        softplus = jnp.maximum(logits, 0.0) + jnp.log1p(jnp.exp(-jnp.abs(logits)))
        logdec = -rate * softplus * live
        beta2 = live / (1.0 + jnp.exp(-logits))
        cumul = jnp.dot(tri, logdec, preferred_element_type=F32, precision=lax.Precision.HIGHEST)
        cumul_t = cumul.T
        q_b, k_b = q.astype(BF16), k.astype(BF16)
        kt_b = k.T.astype(BF16)
        both = mm(jnp.concatenate([k_b, q_b], axis=0), kt_b)
        kk, qk = both[:CH], both[CH:]
        per_head = []
        for h in range(2):
            g = cumul[:, h : h + 1]
            decay = jnp.exp(jnp.minimum(g - cumul_t[h : h + 1, :], 0.0))
            beta = beta2[:, 2 + h : 3 + h]
            lows.append(jnp.where(rows > cols, beta * kk * decay, 0.0))
            attn = jnp.where(rows >= cols, qk * decay, 0.0).astype(BF16)
            start = jnp.exp(g)
            value = part[:, 256 + 128 * h : 384 + 128 * h]
            right = jnp.concatenate([beta * value, (beta * start) * k], axis=1).astype(BF16)
            last = cumul[CH - 1 : CH, h : h + 1]
            tail = jnp.exp(last - g)
            per_head.append((attn, start, right, tail, jnp.exp(last)))
        prep.append((q_b, kt_b, per_head))
    inverses = unit_lower_inverse(lows, rows, cols)
    solved = []
    for c in range(chunks):
        for h in range(2):
            high, low = halves(inverses[2 * c + h])
            right = prep[c][2][h][2]
            solved.append(mm(jnp.concatenate([high, low], axis=1), jnp.concatenate([right, right], axis=0)))
    gated = []
    state = list(state)
    for c in range(chunks):
        q_b, kt_b, per_head = prep[c]
        outs = []
        for h in range(2):
            attn, start, _, tail, last = per_head[h]
            upd = solved[2 * c + h]
            left = jnp.concatenate([upd[:, 128:].astype(BF16), q_b], axis=0)
            s_high, s_low = halves(state[h])
            got = mm(jnp.concatenate([left, left], axis=1), jnp.concatenate([s_high, s_low], axis=0))
            corrected = upd[:, :128] - got[:CH]
            out = start * got[CH:] + mm(attn, corrected.astype(BF16))
            t_high, t_low = halves(tail * corrected)
            state[h] = last * state[h] + mm(
                jnp.concatenate([kt_b, kt_b], axis=1), jnp.concatenate([t_high, t_low], axis=0)
            )
            z = proj[c * CH : (c + 1) * CH, 512 + 128 * h : 640 + 128 * h]
            scale = lax.rsqrt(jnp.mean(out * out, axis=-1, keepdims=True) + EPS)
            outs.append((out * scale * gain * (z / (1.0 + jnp.exp(-z)))).astype(BF16))
        gated.append(jnp.concatenate(outs, axis=1))
    return state, jnp.concatenate(gated, axis=0)


def delta_kernel(tile, length_ref, piece_ref, w_ref, rate_ref, gain_ref, wo_ref, first_ref, out_ref, final_ref, state_ref):
    step = pl.program_id(0)

    @pl.when(step == 0)
    def _():
        for h in range(2):
            state_ref[h] = first_ref[h].T

    proj = mm(piece_ref[...], w_ref[...])
    state, gated = delta_body(
        tile, step * tile, length_ref[0], proj, rate_ref[...], gain_ref[...], [state_ref[0], state_ref[1]]
    )
    for h in range(2):
        state_ref[h] = state[h]
    out_ref[...] = mm(gated, wo_ref[...]).astype(BF16)

    @pl.when(step == pl.num_programs(0) - 1)
    def _():
        for h in range(2):
            final_ref[h] = state_ref[h].T


def delta(length, piece, weights, rate, gain, w_output, first, tile=256):
    span, width = piece.shape
    total = weights.shape[1]
    const = lambda *shape: pl.BlockSpec(shape, lambda i: (0,) * len(shape))
    return pl.pallas_call(
        functools.partial(delta_kernel, tile),
        grid=(span // tile,),
        in_specs=[
            pl.BlockSpec(memory_space=pltpu.SMEM),
            pl.BlockSpec((tile, width), lambda i: (i, 0)),
            const(width, total),
            const(1, 128),
            const(1, 128),
            const(*w_output.shape),
            const(2, 128, 128),
        ],
        out_specs=[pl.BlockSpec((tile, w_output.shape[1]), lambda i: (i, 0)), const(2, 128, 128)],
        out_shape=[
            jax.ShapeDtypeStruct((span, w_output.shape[1]), BF16),
            jax.ShapeDtypeStruct((2, 128, 128), F32),
        ],
        scratch_shapes=[pltpu.VMEM((2, 128, 128), F32)],
        compiler_params=pltpu.CompilerParams(vmem_limit_bytes=50 * 2**20),
    )(length, piece, weights, rate, gain, w_output, first)


CAP = 8


def rms_scale(values, gain):
    mean = jnp.mean(values * values, axis=-1, keepdims=True)
    return values * lax.rsqrt(mean + EPS) * gain


def routing(chosen_ids, experts):
    tokens = chosen_ids.shape[0]
    table = lax.broadcasted_iota(jnp.int32, (1, 1, experts), 2)
    member = jnp.any(chosen_ids[:, :, None] == table, axis=1)
    rows = lax.broadcasted_iota(jnp.int32, (tokens, tokens), 0)
    cols = lax.broadcasted_iota(jnp.int32, (tokens, tokens), 1)
    earlier = (rows > cols).astype(BF16)
    before = jnp.dot(earlier, member.astype(BF16), preferred_element_type=F32)
    place = jnp.where(member, before, -1.0).T
    slots = lax.broadcasted_iota(jnp.int32, (1, CAP, 1), 1).astype(F32)
    onehot = (place[:, None, :] == slots).reshape(experts * CAP, tokens)
    return onehot, member


def shards(
    tokens,
    span_lengths,
    state_slots,
    expert_ids,
    state_pool,
    attn_gain,
    w_query,
    w_key,
    w_value,
    w_zgate,
    w_heads,
    decay_rate,
    head_gain,
    w_output,
    moe_gain,
    router,
    w_expert_in,
    w_expert_out,
):
    local_rows, width = tokens.shape[1:]
    length = span_lengths[0]
    own_rows = tokens[0]
    normed = rms_scale(own_rows.astype(F32), attn_gain).astype(BF16)
    head_weights = jnp.pad(w_heads.reshape(width, 4), ((0, 0), (0, 124)))
    weights_all = jnp.concatenate([w_query, w_key, w_value, w_zgate, head_weights], axis=1)
    piece = lax.all_gather(normed, "seq", axis=0, tiled=True)
    first = lax.dynamic_index_in_dim(state_pool, state_slots[0], 0, keepdims=False)
    rate = jnp.pad(decay_rate, (0, 126)).reshape(1, 128)
    partial, final = delta(span_lengths, piece, weights_all, rate, head_gain.reshape(1, 128), w_output, first)
    summed = lax.psum_scatter(partial, "seq", scatter_dimension=0, tiled=True).astype(F32)
    own_positions = lax.axis_index("seq") * local_rows + lax.broadcasted_iota(jnp.int32, (local_rows, 1), 0)
    own_live = (own_positions < length).astype(F32)
    attended = (summed * own_live).astype(BF16)
    residual = own_rows.astype(F32) + attended.astype(F32)
    moe_input = rms_scale(residual, moe_gain).astype(BF16)
    logits = jnp.dot(moe_input, router, preferred_element_type=F32)
    experts_all = router.shape[1]
    onehot, member = routing(expert_ids[0], experts_all)
    top = jnp.max(jnp.where(member, logits, -jnp.inf), axis=-1, keepdims=True)
    powers = jnp.where(member, jnp.exp(logits - top), 0.0)
    weights = powers / jnp.sum(powers, axis=-1, keepdims=True) * own_live
    spread = jnp.broadcast_to(weights.T[:, None, :], (experts_all, CAP, local_rows)).reshape(onehot.shape)
    combine = jnp.where(onehot, spread, 0.0).astype(BF16)
    outgoing = jnp.dot(onehot.astype(BF16), moe_input, preferred_element_type=F32).astype(BF16)
    local_experts = w_expert_in.shape[0]
    owners = experts_all // local_experts
    arrived = lax.all_to_all(
        outgoing.reshape(owners, local_experts, CAP, width),
        ("prompt", "seq"),
        split_axis=0,
        concat_axis=0,
        tiled=True,
    )
    pair = jnp.einsum("necd,edf->necf", arrived, w_expert_in, preferred_element_type=F32)
    inner_width = w_expert_out.shape[1]
    inner = (jax.nn.silu(pair[..., :inner_width]) * pair[..., inner_width:]).astype(BF16)
    result = jnp.einsum("necf,efd->necd", inner, w_expert_out, preferred_element_type=F32).astype(BF16)
    returned = lax.all_to_all(result, ("prompt", "seq"), split_axis=0, concat_axis=0, tiled=True)
    expert_out = lax.dot_general(
        combine,
        returned.reshape(experts_all * CAP, width),
        (((0,), (0,)), ((), ())),
        preferred_element_type=F32,
    ).astype(BF16)
    return (attended[None], expert_out[None], final[None])


def solution(mesh):
    return jax.shard_map(
        shards,
        mesh=mesh,
        in_specs=(
            P("prompt", "seq", None),
            P("prompt"),
            P("prompt"),
            P("prompt", "seq", None),
            P(None, "seq", None, None),
            P(),
            P(None, "seq"),
            P(None, "seq"),
            P(None, "seq"),
            P(None, "seq"),
            P(None, None, "seq"),
            P("seq"),
            P(),
            P("seq", None),
            P(),
            P(),
            P(("prompt", "seq"), None, None),
            P(("prompt", "seq"), None, None),
        ),
        out_specs=(
            P("prompt", "seq", None),
            P("prompt", "seq", None),
            P("prompt", "seq", None, None),
        ),
        check_vma=False,
    )
```

```python
import functools
import jax
import jax.numpy as jnp
from jax import lax
from jax.experimental import pallas as pl
from jax.experimental.pallas import tpu as pltpu
from jax.sharding import PartitionSpec as P

EPS = 1e-06
CH = 128
RING = 4
SEQ = RING * RING
HEADS = 2
F32 = jnp.float32
BF16 = jnp.bfloat16
MESH = pl.DeviceIdType.MESH


def mm(a, b):
    return jnp.dot(a, b, preferred_element_type=F32)


def halves(a):
    high = a.astype(BF16)
    return high, (a - high.astype(F32)).astype(BF16)


def mm3(a, b):
    a_high, a_low = halves(a)
    b_high, b_low = halves(b)
    wide = mm(jnp.concatenate([a_high, a_low], axis=1), jnp.concatenate([b_high, b_high], axis=0))
    return wide + mm(a_high, b_low)


def unit_lower_inverse(lows, rows, cols):
    eye = jnp.where(rows == cols, 1.0, 0.0)
    inverses = [eye - jnp.where(rows // 2 == cols // 2, low, 0.0) for low in lows]
    size = 2
    while size < CH:
        mask = (rows // (2 * size) == cols // (2 * size)) & (rows // size != cols // size)
        inner = [mm3(jnp.where(mask, low, 0.0), inv) for low, inv in zip(lows, inverses)]
        inverses = [inv - mm3(inv, part) for inv, part in zip(inverses, inner)]
        size *= 2
    return inverses


def prepare(blocks, length, tok, w_ref, rate, gain, store):
    left_ref, kt_ref, attn_ref, upd_ref, last_ref, gate_ref = store
    rows = lax.broadcasted_iota(jnp.int32, (CH, CH), 0)
    cols = lax.broadcasted_iota(jnp.int32, (CH, CH), 1)
    tri = jnp.where(rows >= cols, 1.0, 0.0)
    proj_all = mm(jnp.concatenate([tok[b] for b in blocks], axis=0), w_ref[...])
    lows = []
    rights = []
    for n, block in enumerate(blocks):
        part = proj_all[n * CH : (n + 1) * CH]
        q, k = part[:, 0:128], part[:, 128:256]
        q = q * (lax.rsqrt(jnp.sum(q * q, axis=-1, keepdims=True) + EPS) * 128 ** (-0.5))
        k = k * lax.rsqrt(jnp.sum(k * k, axis=-1, keepdims=True) + EPS)
        logits = part[:, 768:896]
        live = jnp.where(block * CH + rows < length, 1.0, 0.0)
        softplus = jnp.maximum(logits, 0.0) + jnp.log1p(jnp.exp(-jnp.abs(logits)))
        logdec = -rate * softplus * live
        beta2 = live / (1.0 + jnp.exp(-logits))
        cumul = jnp.dot(tri, logdec, preferred_element_type=F32, precision=lax.Precision.HIGHEST)
        cumul_t = cumul.T
        both = mm(jnp.concatenate([k.astype(BF16), q.astype(BF16)], axis=0), k.T.astype(BF16))
        kk, qk = both[:CH], both[CH:]
        for h in range(HEADS):
            g = cumul[:, h : h + 1]
            decay = jnp.exp(jnp.minimum(g - cumul_t[h : h + 1, :], 0.0))
            beta = beta2[:, 2 + h : 3 + h]
            lows.append(jnp.where(rows > cols, beta * kk * decay, 0.0))
            attn_ref[block, h] = jnp.where(rows >= cols, qk * decay, 0.0).astype(BF16)
            start = jnp.exp(g)
            value = part[:, 256 + 128 * h : 384 + 128 * h]
            rights.append(jnp.concatenate([beta * value, (beta * start) * k], axis=1).astype(BF16))
            last = cumul[CH - 1 : CH, h : h + 1]
            left_ref[block, h, CH:, :] = (start * q).astype(BF16)
            kt_ref[block, h] = (jnp.exp(last - g) * k).T.astype(BF16)
            last_ref[block, h] = jnp.broadcast_to(jnp.exp(last), (8, CH))
            z = part[:, 512 + 128 * h : 640 + 128 * h]
            gate_ref[block, h] = gain * (z / (1.0 + jnp.exp(-z)))
    for n, inverse in enumerate(unit_lower_inverse(lows, rows, cols)):
        block, h = blocks[n // HEADS], n % HEADS
        high, low = halves(inverse)
        got = mm(jnp.concatenate([high, low], axis=1), jnp.concatenate([rights[n], rights[n]], axis=0))
        upd_ref[block, h] = got[:, :CH]
        left_ref[block, h, :CH, :] = got[:, CH:].astype(BF16)


def advance(block, state_ref, store):
    left_ref, kt_ref, attn_ref, upd_ref, last_ref, gate_ref = store
    outs = []
    for h in range(HEADS):
        state = state_ref[h]
        left = left_ref[block, h]
        high, low = halves(state)
        got = mm(jnp.concatenate([left, left], axis=1), jnp.concatenate([high, low], axis=0))
        corrected = upd_ref[block, h] - got[:CH]
        high, low = halves(corrected)
        kt = kt_ref[block, h]
        state_ref[h] = last_ref[block, h, 0:1, :] * state + mm(
            jnp.concatenate([kt, kt], axis=1), jnp.concatenate([high, low], axis=0)
        )
        out = got[CH:] + mm(attn_ref[block, h], high)
        scale = lax.rsqrt(jnp.mean(out * out, axis=-1, keepdims=True) + EPS)
        outs.append((out * scale * gate_ref[block, h]).astype(BF16))
    return jnp.concatenate(outs, axis=1)


def attention_kernel(
    length_ref,
    own_ref,
    wo_ref,
    w_ref,
    rate_ref,
    gain_ref,
    first_ref,
    out_ref,
    final_ref,
    tok,
    wall,
    got,
    gout,
    left_ref,
    kt_ref,
    attn_ref,
    upd_ref,
    last_ref,
    gate_ref,
    state_ref,
    ring_send,
    ring_recv,
    z_send,
    z_recv,
    mate_send,
    mate_recv,
    got_send,
    got_recv,
):
    store = (left_ref, kt_ref, attn_ref, upd_ref, last_ref, gate_ref)
    p = lax.axis_index("prompt")
    s = lax.axis_index("seq")
    z, c = p // 2, p % 2
    x, y = s // RING, s % RING
    parity = z % 2
    length = length_ref[0]
    tcols = tok.shape[2] // 2

    def spot(half, df, dg):
        dx, dy = (dg, df) if half == 0 else (df, dg)
        return ((x + dx + 2 * RING) % RING) * RING + (y + dy + 2 * RING) % RING

    def depth(step):
        return ((z + step + RING) % RING) * 2 + c

    mate = z * 2 + (1 - c)

    def at(chan, half, owner, first, count, side=None, par=None):
        if chan == 0:
            return tok.at[owner, pl.ds(first, count), pl.ds(half * tcols, tcols)]
        row = pl.multiple_of(owner * 256 + half * 128 + first, 64)
        return wall.at[c if side is None else side, parity if par is None else par, pl.ds(row, count), :]

    FULL, LOW, HIGH = (0, 128), (0, 64), (64, 64)

    def ring(chan, half, df, dg, span, tf, tg):
        kf, kg = (df - tf) % RING, (dg - tg) % RING
        slot = ((kf * RING + kg) * 2) + (1 if span is HIGH else 0)
        piece = at(chan, half, spot(half, df, dg), *span)
        return pltpu.make_async_remote_copy(
            src_ref=piece,
            dst_ref=piece,
            send_sem=ring_send.at[chan, half, slot],
            recv_sem=ring_recv.at[chan, half, slot],
            device_id=(p, spot(half, tf, tg)),
            device_id_type=MESH,
        )

    started = []

    def send(*args):
        copy = ring(*args)
        copy.start()
        started.append(copy)

    def arrive(chan, half, df, dg, span):
        slot = ((df % RING * RING + dg % RING) * 2) + (1 if span is HIGH else 0)
        piece = at(chan, half, spot(half, df, dg), *span)
        pltpu.make_async_remote_copy(
            src_ref=piece,
            dst_ref=piece,
            send_sem=ring_send.at[chan, half, slot],
            recv_sem=ring_recv.at[chan, half, slot],
            device_id=(p, spot(half, 1, 0)),
            device_id_type=MESH,
        ).wait_recv()

    passed = []

    def hand_on(half, df, dg):
        owner = spot(half, df, dg)
        slot = (df % RING) * RING + dg % RING
        piece = at(1, half, owner, *FULL)
        copy = pltpu.make_async_remote_copy(
            src_ref=piece,
            dst_ref=piece,
            send_sem=z_send.at[half, slot],
            recv_sem=z_recv.at[half, slot],
            device_id=(depth(1 if half == 0 else -1), s),
            device_id_type=MESH,
        )
        copy.start()
        started.append(copy)
        copy = to_mate(half, df, dg, parity, 0)
        copy.start()
        started.append(copy)
        passed.append((half, df, dg))

    def to_mate(half, df, dg, par, kind):
        slot = (df % RING) * RING + dg % RING
        piece = at(1, half, spot(half, df, dg), *FULL, par=par)
        return pltpu.make_async_remote_copy(
            src_ref=piece,
            dst_ref=piece,
            send_sem=mate_send.at[kind, half, slot],
            recv_sem=mate_recv.at[kind, half, slot],
            device_id=(mate, s),
            device_id_type=MESH,
        )

    def from_z(half, df, dg):
        owner = spot(half, df, dg)
        slot = (df % RING) * RING + dg % RING
        piece = at(1, half, owner, *FULL, par=1 - parity)
        pltpu.make_async_remote_copy(
            src_ref=piece,
            dst_ref=piece,
            send_sem=z_send.at[half, slot],
            recv_sem=z_recv.at[half, slot],
            device_id=(depth(1), s),
            device_id_type=MESH,
        ).wait_recv()
        copy = to_mate(half, df, dg, 1 - parity, 1)
        copy.start()
        started.append(copy)

    def from_mate(half, df, dg):
        slot = (df % RING) * RING + dg % RING
        for kind in (0, 1):
            piece = at(1, half, spot(half, df, dg), *FULL, side=1 - c, par=parity if kind == 0 else 1 - parity)
            pltpu.make_async_remote_copy(
                src_ref=piece,
                dst_ref=piece,
                send_sem=mate_send.at[kind, half, slot],
                recv_sem=mate_recv.at[kind, half, slot],
                device_id=(mate, s),
                device_id_type=MESH,
            ).wait_recv()

    def begin(chan):
        for half in (0, 1):
            for step in (1, -1):
                send(chan, half, 0, 0, FULL, step, 0)
        for half in (0, 1):
            for step in (1, -1):
                send(chan, half, 0, 0, FULL, 0, step)

    def both(chan, event):
        for half in (0, 1):
            event(chan, half)

    def first_near(chan, half):
        for df, span in ((-1, LOW), (1, HIGH)):
            arrive(chan, half, df, 0, FULL)
            send(chan, half, df, 0, span, -df, 0)
        if chan == 1:
            hand_on(half, -1, 0)
            hand_on(half, 1, 0)

    def second_near(chan, half):
        for dg, span in ((-1, LOW), (1, HIGH)):
            arrive(chan, half, 0, dg, FULL)
            send(chan, half, 0, dg, span, 0, -dg)
        if chan == 1:
            hand_on(half, 0, -1)
            hand_on(half, 0, 1)
        for df in (-1, 1):
            for step in (1, -1):
                send(chan, half, df, 0, FULL, 0, step)

    def first_far(chan, half):
        arrive(chan, half, 2, 0, LOW)
        arrive(chan, half, 2, 0, HIGH)
        for step in (1, -1):
            send(chan, half, 2, 0, FULL, 0, step)
        if chan == 1:
            hand_on(half, 2, 0)

    def second_far(chan, half, df=0):
        arrive(chan, half, df, 2, LOW)
        arrive(chan, half, df, 2, HIGH)
        if chan == 1:
            hand_on(half, df, 2)

    def corner(chan, half, dfs=(-1, 1)):
        for df in dfs:
            for dg, span in ((-1, LOW), (1, HIGH)):
                arrive(chan, half, df, dg, FULL)
                send(chan, half, df, dg, span, 0, -dg)
                if chan == 1:
                    hand_on(half, df, dg)

    def block_of(dx, dy):
        return spot(1, dx, dy)

    def compute(offsets):
        prepare(
            [block_of(*offset) for offset in offsets], length, tok, w_ref, rate_ref[...], gain_ref[...], store
        )

    barrier = pltpu.get_barrier_semaphore()

    def greet(step, carry):
        pl.semaphore_signal(barrier, 1, device_id=(p, (s + step) % SEQ), device_id_type=MESH)
        return carry

    lax.fori_loop(1, SEQ, greet, 0)
    for other in (mate, depth(1), depth(-1)):
        pl.semaphore_signal(barrier, 1, device_id=(other, s), device_id_type=MESH)
    tok[s] = own_ref[...]
    for side in (0, 1):
        for par in (0, 1):
            first = (2 * side + par) * 512
            wall[side, par, pl.ds(pl.multiple_of(s * 256, 256), 256), :] = wo_ref[:, first : first + 512]
    for h in range(HEADS):
        state_ref[h] = first_ref[h].T
    pl.semaphore_wait(barrier, SEQ + 2)

    begin(0)
    compute([(0, 0)])
    both(0, first_near)
    both(0, second_near)
    compute([(0, 1), (0, -1), (1, 0), (-1, 0)])
    both(0, first_far)
    both(0, second_far)
    begin(1)
    compute([(0, 2), (2, 0)])
    both(0, corner)
    both(1, first_near)
    compute([(1, 1), (1, -1), (-1, 1), (-1, -1)])
    for half in (0, 1):
        corner(0, half, (2,))
    both(1, second_near)
    for half in (0, 1):
        second_far(0, half, -1)
        second_far(0, half, 1)
        second_far(0, half, 2)
    compute([(1, 2), (-1, 2), (2, 1), (2, -1), (2, 2)])
    both(1, first_far)
    both(1, second_far)

    def give(index):
        here = gout.at[index]
        there = got.at[:, pl.ds(pl.multiple_of(s * 256, 256), 256)]
        return pltpu.make_async_remote_copy(
            src_ref=here,
            dst_ref=there,
            send_sem=got_send.at[index],
            recv_sem=got_recv.at[s],
            device_id=(p, index),
            device_id_type=MESH,
        )

    def scan(index, carry):
        gated = advance(index, state_ref, store)

        @pl.when(index != s)
        def _():
            gout[index] = gated
            give(index).start()

        @pl.when(index == s)
        def _():
            got[:, pl.ds(pl.multiple_of(s * 256, 256), 256)] = gated

        return carry

    lax.fori_loop(0, 8, scan, 0)
    both(1, corner)
    lax.fori_loop(8, SEQ, scan, 0)
    for half in (0, 1):
        corner(1, half, (2,))
    for half in (0, 1):
        second_far(1, half, -1)
        second_far(1, half, 1)
        second_far(1, half, 2)
    for h in range(HEADS):
        final_ref[h] = state_ref[h].T
    for item in passed:
        from_z(*item)

    def receive(step, carry):
        source = (s + step) % SEQ
        there = got.at[:, pl.ds(pl.multiple_of(source * 256, 256), 256)]
        pltpu.make_async_remote_copy(
            src_ref=gout.at[source],
            dst_ref=there,
            send_sem=got_send.at[source],
            recv_sem=got_recv.at[source],
            device_id=(p, source),
            device_id_type=MESH,
        ).wait()
        return carry

    lax.fori_loop(1, SEQ, receive, 0)
    for item in passed:
        from_mate(*item)
    for copy in started:
        copy.wait_send()
    for side in (0, 1):
        for par in (0, 1):
            first = (2 * side + par) * 512
            out_ref[:, first : first + 512] = mm(got[...], wall[side, par])


def attention(length, own, w_output, weights, rate, gain, first):
    rows, width = own.shape
    vmem = pl.BlockSpec(memory_space=pltpu.VMEM)
    dma = pltpu.SemaphoreType.DMA
    return pl.pallas_call(
        attention_kernel,
        in_specs=[pl.BlockSpec(memory_space=pltpu.SMEM)] + [vmem] * 6,
        out_specs=[vmem, vmem],
        out_shape=[
            jax.ShapeDtypeStruct((rows, width), F32),
            jax.ShapeDtypeStruct((HEADS, 128, 128), F32),
        ],
        scratch_shapes=[
            pltpu.VMEM((SEQ, rows, width), BF16),
            pltpu.VMEM((2, 2, SEQ * 256, 512), BF16),
            pltpu.VMEM((rows, SEQ * 256), BF16),
            pltpu.VMEM((SEQ, rows, 256), BF16),
            pltpu.VMEM((SEQ, HEADS, 2 * CH, 128), BF16),
            pltpu.VMEM((SEQ, HEADS, 128, CH), BF16),
            pltpu.VMEM((SEQ, HEADS, CH, CH), BF16),
            pltpu.VMEM((SEQ, HEADS, CH, 128), F32),
            pltpu.VMEM((SEQ, HEADS, 8, CH), F32),
            pltpu.VMEM((SEQ, HEADS, CH, 128), F32),
            pltpu.VMEM((HEADS, 128, 128), F32),
            dma((2, 2, 32)),
            dma((2, 2, 32)),
            dma((2, 16)),
            dma((2, 16)),
            dma((2, 2, 16)),
            dma((2, 2, 16)),
            dma((SEQ,)),
            dma((SEQ,)),
        ],
        compiler_params=pltpu.CompilerParams(
            collective_id=0, has_side_effects=True, vmem_limit_bytes=56 * 2**20
        ),
    )(length, own, w_output, weights, rate, gain, first)


CAP = 8


def rms_scale(values, gain):
    mean = jnp.mean(values * values, axis=-1, keepdims=True)
    return values * lax.rsqrt(mean + EPS) * gain


def routing(chosen_ids, experts):
    tokens = chosen_ids.shape[0]
    table = lax.broadcasted_iota(jnp.int32, (1, 1, experts), 2)
    member = jnp.any(chosen_ids[:, :, None] == table, axis=1)
    rows = lax.broadcasted_iota(jnp.int32, (tokens, tokens), 0)
    cols = lax.broadcasted_iota(jnp.int32, (tokens, tokens), 1)
    earlier = (rows > cols).astype(BF16)
    before = jnp.dot(earlier, member.astype(BF16), preferred_element_type=F32)
    place = jnp.where(member, before, -1.0).T
    slots = lax.broadcasted_iota(jnp.int32, (1, CAP, 1), 1).astype(F32)
    onehot = (place[:, None, :] == slots).reshape(experts * CAP, tokens)
    return onehot, member


def shards(
    tokens,
    span_lengths,
    state_slots,
    expert_ids,
    state_pool,
    attn_gain,
    w_query,
    w_key,
    w_value,
    w_zgate,
    w_heads,
    decay_rate,
    head_gain,
    w_output,
    moe_gain,
    router,
    w_expert_in,
    w_expert_out,
):
    local_rows, width = tokens.shape[1:]
    length = span_lengths[0]
    own_rows = tokens[0]
    normed = rms_scale(own_rows.astype(F32), attn_gain).astype(BF16)
    head_weights = jnp.pad(w_heads.reshape(width, 4), ((0, 0), (0, 124)))
    weights_all = jnp.concatenate([w_query, w_key, w_value, w_zgate, head_weights], axis=1)
    first = lax.dynamic_index_in_dim(state_pool, state_slots[0], 0, keepdims=False)
    rate = jnp.pad(decay_rate, (0, 126)).reshape(1, 128)
    summed, final = attention(
        span_lengths, normed, w_output, weights_all, rate, head_gain.reshape(1, 128), first
    )
    own_positions = lax.axis_index("seq") * local_rows + lax.broadcasted_iota(jnp.int32, (local_rows, 1), 0)
    own_live = (own_positions < length).astype(F32)
    attended = (summed * own_live).astype(BF16)
    residual = own_rows.astype(F32) + attended.astype(F32)
    moe_input = rms_scale(residual, moe_gain).astype(BF16)
    logits = jnp.dot(moe_input, router, preferred_element_type=F32)
    experts_all = router.shape[1]
    onehot, member = routing(expert_ids[0], experts_all)
    top = jnp.max(jnp.where(member, logits, -jnp.inf), axis=-1, keepdims=True)
    powers = jnp.where(member, jnp.exp(logits - top), 0.0)
    weights = powers / jnp.sum(powers, axis=-1, keepdims=True) * own_live
    spread = jnp.broadcast_to(weights.T[:, None, :], (experts_all, CAP, local_rows)).reshape(onehot.shape)
    combine = jnp.where(onehot, spread, 0.0).astype(BF16)
    outgoing = jnp.dot(onehot.astype(BF16), moe_input, preferred_element_type=F32).astype(BF16)
    local_experts = w_expert_in.shape[0]
    owners = experts_all // local_experts
    arrived = lax.all_to_all(
        outgoing.reshape(owners, local_experts, CAP, width),
        ("prompt", "seq"),
        split_axis=0,
        concat_axis=0,
        tiled=True,
    )
    pair = jnp.einsum("necd,edf->necf", arrived, w_expert_in, preferred_element_type=F32)
    inner_width = w_expert_out.shape[1]
    inner = (jax.nn.silu(pair[..., :inner_width]) * pair[..., inner_width:]).astype(BF16)
    result = jnp.einsum("necf,efd->necd", inner, w_expert_out, preferred_element_type=F32).astype(BF16)
    returned = lax.all_to_all(result, ("prompt", "seq"), split_axis=0, concat_axis=0, tiled=True)
    expert_out = lax.dot_general(
        combine,
        returned.reshape(experts_all * CAP, width),
        (((0,), (0,)), ((), ())),
        preferred_element_type=F32,
    ).astype(BF16)
    return (attended[None], expert_out[None], final[None])


def solution(mesh):
    return jax.shard_map(
        shards,
        mesh=mesh,
        in_specs=(
            P("prompt", "seq", None),
            P("prompt"),
            P("prompt"),
            P("prompt", "seq", None),
            P(None, "seq", None, None),
            P(),
            P(None, "seq"),
            P(None, "seq"),
            P(None, "seq"),
            P(None, "seq"),
            P(None, None, "seq"),
            P("seq"),
            P(),
            P("seq", None),
            P(),
            P(),
            P(("prompt", "seq"), None, None),
            P(("prompt", "seq"), None, None),
        ),
        out_specs=(
            P("prompt", "seq", None),
            P("prompt", "seq", None),
            P("prompt", "seq", None, None),
        ),
        check_vma=False,
    )
```

```python
import functools
import jax
import jax.numpy as jnp
from jax import lax
from jax.experimental import pallas as pl
from jax.experimental.pallas import tpu as pltpu
from jax.sharding import PartitionSpec as P

EPS = 1e-06
CH = 128
RING = 4
SEQ = RING * RING
HEADS = 2
F32 = jnp.float32
BF16 = jnp.bfloat16
MESH = pl.DeviceIdType.MESH


def mm(a, b):
    return jnp.dot(a, b, preferred_element_type=F32)


def halves(a):
    high = a.astype(BF16)
    return high, (a - high.astype(F32)).astype(BF16)


def mm3(a, b):
    a_high, a_low = halves(a)
    b_high, b_low = halves(b)
    wide = mm(jnp.concatenate([a_high, a_low], axis=1), jnp.concatenate([b_high, b_high], axis=0))
    return wide + mm(a_high, b_low)


def unit_lower_inverse(lows, rows, cols):
    eye = jnp.where(rows == cols, 1.0, 0.0)
    inverses = [eye - jnp.where(rows // 2 == cols // 2, low, 0.0) for low in lows]
    size = 2
    while size < CH:
        mask = (rows // (2 * size) == cols // (2 * size)) & (rows // size != cols // size)
        inner = [mm3(jnp.where(mask, low, 0.0), inv) for low, inv in zip(lows, inverses)]
        inverses = [inv - mm3(inv, part) for inv, part in zip(inverses, inner)]
        size *= 2
    return inverses


def prepare(blocks, length, tok, w_ref, rate, gain, store):
    left_ref, kt_ref, attn_ref, upd_ref, last_ref, gate_ref = store
    rows = lax.broadcasted_iota(jnp.int32, (CH, CH), 0)
    cols = lax.broadcasted_iota(jnp.int32, (CH, CH), 1)
    tri = jnp.where(rows >= cols, 1.0, 0.0)
    proj_all = mm(jnp.concatenate([tok[b] for b in blocks], axis=0), w_ref[...])
    lows = []
    rights = []
    for n, block in enumerate(blocks):
        part = proj_all[n * CH : (n + 1) * CH]
        q, k = part[:, 0:128], part[:, 128:256]
        q = q * (lax.rsqrt(jnp.sum(q * q, axis=-1, keepdims=True) + EPS) * 128 ** (-0.5))
        k = k * lax.rsqrt(jnp.sum(k * k, axis=-1, keepdims=True) + EPS)
        logits = part[:, 768:896]
        live = jnp.where(block * CH + rows < length, 1.0, 0.0)
        softplus = jnp.maximum(logits, 0.0) + jnp.log1p(jnp.exp(-jnp.abs(logits)))
        logdec = -rate * softplus * live
        beta2 = live / (1.0 + jnp.exp(-logits))
        cumul = jnp.dot(tri, logdec, preferred_element_type=F32, precision=lax.Precision.HIGHEST)
        cumul_t = cumul.T
        both = mm(jnp.concatenate([k.astype(BF16), q.astype(BF16)], axis=0), k.T.astype(BF16))
        kk, qk = both[:CH], both[CH:]
        for h in range(HEADS):
            g = cumul[:, h : h + 1]
            decay = jnp.exp(jnp.minimum(g - cumul_t[h : h + 1, :], 0.0))
            beta = beta2[:, 2 + h : 3 + h]
            lows.append(jnp.where(rows > cols, beta * kk * decay, 0.0))
            attn_ref[block, h] = jnp.where(rows >= cols, qk * decay, 0.0).astype(BF16)
            start = jnp.exp(g)
            value = part[:, 256 + 128 * h : 384 + 128 * h]
            rights.append(jnp.concatenate([beta * value, (beta * start) * k], axis=1).astype(BF16))
            last = cumul[CH - 1 : CH, h : h + 1]
            left_ref[block, h, CH:, :] = (start * q).astype(BF16)
            kt_ref[block, h] = (jnp.exp(last - g) * k).T.astype(BF16)
            last_ref[block, h] = jnp.broadcast_to(jnp.exp(last), (8, CH))
            z = part[:, 512 + 128 * h : 640 + 128 * h]
            gate_ref[block, h] = gain * (z / (1.0 + jnp.exp(-z)))
    for n, inverse in enumerate(unit_lower_inverse(lows, rows, cols)):
        block, h = blocks[n // HEADS], n % HEADS
        high, low = halves(inverse)
        got = mm(jnp.concatenate([high, low], axis=1), jnp.concatenate([rights[n], rights[n]], axis=0))
        upd_ref[block, h] = got[:, :CH]
        left_ref[block, h, :CH, :] = got[:, CH:].astype(BF16)


def advance(block, state_ref, store):
    left_ref, kt_ref, attn_ref, upd_ref, last_ref, gate_ref = store
    outs = []
    for h in range(HEADS):
        state = state_ref[h]
        left = left_ref[block, h]
        high, low = halves(state)
        got = mm(jnp.concatenate([left, left], axis=1), jnp.concatenate([high, low], axis=0))
        corrected = upd_ref[block, h] - got[:CH]
        high, low = halves(corrected)
        kt = kt_ref[block, h]
        state_ref[h] = last_ref[block, h, 0:1, :] * state + mm(
            jnp.concatenate([kt, kt], axis=1), jnp.concatenate([high, low], axis=0)
        )
        out = got[CH:] + mm(attn_ref[block, h], high)
        scale = lax.rsqrt(jnp.mean(out * out, axis=-1, keepdims=True) + EPS)
        outs.append((out * scale * gate_ref[block, h]).astype(BF16))
    return jnp.concatenate(outs, axis=1)


def ring_spot(s, half, df, dg):
    dx, dy = (dg, df) if half == 0 else (df, dg)
    x, y = s // RING, s % RING
    return ((x + dx + 2 * RING) % RING) * RING + (y + dy + 2 * RING) % RING


FULL, LOW, HIGH = (0, 128), (0, 64), (64, 64)


class Rings:
    def __init__(self, p, s, at, send_sem, recv_sem, hook=None):
        self.p, self.s, self.at = p, s, at
        self.send_sem, self.recv_sem = send_sem, recv_sem
        self.hook = hook or (lambda half, df, dg: None)
        self.started = []

    def copy(self, half, df, dg, span, tf, tg):
        slot = ((df - tf) % RING * RING + (dg - tg) % RING) * 2 + (1 if span is HIGH else 0)
        piece = self.at(half, ring_spot(self.s, half, df, dg), *span)
        return pltpu.make_async_remote_copy(
            src_ref=piece,
            dst_ref=piece,
            send_sem=self.send_sem.at[half, slot],
            recv_sem=self.recv_sem.at[half, slot],
            device_id=(self.p, ring_spot(self.s, half, tf, tg)),
            device_id_type=MESH,
        )

    def send(self, *args):
        copy = self.copy(*args)
        copy.start()
        self.started.append(copy)

    def arrive(self, half, df, dg, span=FULL):
        slot = (df % RING * RING + dg % RING) * 2 + (1 if span is HIGH else 0)
        piece = self.at(half, ring_spot(self.s, half, df, dg), *span)
        pltpu.make_async_remote_copy(
            src_ref=piece,
            dst_ref=piece,
            send_sem=self.send_sem.at[half, slot],
            recv_sem=self.recv_sem.at[half, slot],
            device_id=(self.p, ring_spot(self.s, half, 1, 0)),
            device_id_type=MESH,
        ).wait_recv()

    def begin(self):
        for half in (0, 1):
            for step in (1, -1):
                self.send(half, 0, 0, FULL, step, 0)
        for half in (0, 1):
            for step in (1, -1):
                self.send(half, 0, 0, FULL, 0, step)

    def first_near(self):
        for half in (0, 1):
            for df, span in ((-1, LOW), (1, HIGH)):
                self.arrive(half, df, 0)
                self.send(half, df, 0, span, -df, 0)
            self.hook(half, -1, 0)
            self.hook(half, 1, 0)

    def second_near(self):
        for half in (0, 1):
            for dg, span in ((-1, LOW), (1, HIGH)):
                self.arrive(half, 0, dg)
                self.send(half, 0, dg, span, 0, -dg)
            self.hook(half, 0, -1)
            self.hook(half, 0, 1)
            for df in (-1, 1):
                for step in (1, -1):
                    self.send(half, df, 0, FULL, 0, step)

    def near(self):
        self.first_near()
        self.second_near()

    def far(self):
        for half in (0, 1):
            self.arrive(half, 2, 0, LOW)
            self.arrive(half, 2, 0, HIGH)
            for step in (1, -1):
                self.send(half, 2, 0, FULL, 0, step)
            self.hook(half, 2, 0)
        self.second_far((0,))

    def second_far(self, dfs):
        for half in (0, 1):
            for df in dfs:
                self.arrive(half, df, 2, LOW)
                self.arrive(half, df, 2, HIGH)
                self.hook(half, df, 2)

    def corners(self, dfs=(-1, 1)):
        for half in (0, 1):
            for df in dfs:
                for dg, span in ((-1, LOW), (1, HIGH)):
                    self.arrive(half, df, dg)
                    self.send(half, df, dg, span, 0, -dg)
                    self.hook(half, df, dg)

    def far_corners(self):
        self.corners((2,))

    def last(self):
        self.second_far((-1, 1, 2))


def attention_kernel(
    length_ref,
    own_ref,
    wo_ref,
    w_ref,
    rate_ref,
    gain_ref,
    first_ref,
    out_ref,
    final_ref,
    tok,
    wall,
    got,
    gout,
    left_ref,
    kt_ref,
    attn_ref,
    upd_ref,
    last_ref,
    gate_ref,
    state_ref,
    ring_send,
    ring_recv,
    z_send,
    z_recv,
    mate_send,
    mate_recv,
    got_send,
    got_recv,
):
    store = (left_ref, kt_ref, attn_ref, upd_ref, last_ref, gate_ref)
    p = lax.axis_index("prompt")
    s = lax.axis_index("seq")
    z, c = p // 2, p % 2
    x, y = s // RING, s % RING
    parity = z % 2
    length = length_ref[0]
    tcols = tok.shape[2] // 2

    def spot(half, df, dg):
        return ring_spot(s, half, df, dg)

    def depth(step):
        return ((z + step + RING) % RING) * 2 + c

    mate = z * 2 + (1 - c)

    def at(chan, half, owner, first, count, side=None, par=None):
        if chan == 0:
            return tok.at[owner, pl.ds(first, count), pl.ds(half * tcols, tcols)]
        row = pl.multiple_of(owner * 256 + half * 128 + first, 64)
        return wall.at[c if side is None else side, parity if par is None else par, pl.ds(row, count), :]

    started = []
    passed = []

    def hand_on(half, df, dg):
        owner = spot(half, df, dg)
        slot = (df % RING) * RING + dg % RING
        piece = at(1, half, owner, *FULL)
        copy = pltpu.make_async_remote_copy(
            src_ref=piece,
            dst_ref=piece,
            send_sem=z_send.at[half, slot],
            recv_sem=z_recv.at[half, slot],
            device_id=(depth(1 if half == 0 else -1), s),
            device_id_type=MESH,
        )
        copy.start()
        started.append(copy)
        copy = to_mate(half, df, dg, parity, 0)
        copy.start()
        started.append(copy)
        passed.append((half, df, dg))

    def to_mate(half, df, dg, par, kind):
        slot = (df % RING) * RING + dg % RING
        piece = at(1, half, spot(half, df, dg), *FULL, par=par)
        return pltpu.make_async_remote_copy(
            src_ref=piece,
            dst_ref=piece,
            send_sem=mate_send.at[kind, half, slot],
            recv_sem=mate_recv.at[kind, half, slot],
            device_id=(mate, s),
            device_id_type=MESH,
        )

    def from_z(half, df, dg):
        owner = spot(half, df, dg)
        slot = (df % RING) * RING + dg % RING
        piece = at(1, half, owner, *FULL, par=1 - parity)
        pltpu.make_async_remote_copy(
            src_ref=piece,
            dst_ref=piece,
            send_sem=z_send.at[half, slot],
            recv_sem=z_recv.at[half, slot],
            device_id=(depth(1), s),
            device_id_type=MESH,
        ).wait_recv()
        copy = to_mate(half, df, dg, 1 - parity, 1)
        copy.start()
        started.append(copy)

    def from_mate(half, df, dg):
        slot = (df % RING) * RING + dg % RING
        for kind in (0, 1):
            piece = at(1, half, spot(half, df, dg), *FULL, side=1 - c, par=parity if kind == 0 else 1 - parity)
            pltpu.make_async_remote_copy(
                src_ref=piece,
                dst_ref=piece,
                send_sem=mate_send.at[kind, half, slot],
                recv_sem=mate_recv.at[kind, half, slot],
                device_id=(mate, s),
                device_id_type=MESH,
            ).wait_recv()

    tokens = Rings(p, s, functools.partial(at, 0), ring_send.at[0], ring_recv.at[0])
    others = Rings(p, s, functools.partial(at, 1), ring_send.at[1], ring_recv.at[1], hand_on)

    def block_of(dx, dy):
        return spot(1, dx, dy)

    def compute(offsets):
        prepare(
            [block_of(*offset) for offset in offsets], length, tok, w_ref, rate_ref[...], gain_ref[...], store
        )

    barrier = pltpu.get_barrier_semaphore()

    def greet(step, carry):
        pl.semaphore_signal(barrier, 1, device_id=(p, (s + step) % SEQ), device_id_type=MESH)
        return carry

    lax.fori_loop(1, SEQ, greet, 0)
    for other in (mate, depth(1), depth(-1)):
        pl.semaphore_signal(barrier, 1, device_id=(other, s), device_id_type=MESH)
    tok[s] = own_ref[...]
    for side in (0, 1):
        for par in (0, 1):
            first = (2 * side + par) * 512
            wall[side, par, pl.ds(pl.multiple_of(s * 256, 256), 256), :] = wo_ref[:, first : first + 512]
    for h in range(HEADS):
        state_ref[h] = first_ref[h].T
    pl.semaphore_wait(barrier, SEQ + 2)

    tokens.begin()
    others.begin()
    compute([(0, 0)])
    tokens.near()
    others.near()
    compute([(0, 1), (0, -1), (1, 0), (-1, 0)])
    tokens.far()
    others.far()
    compute([(0, 2), (2, 0)])
    tokens.corners()
    others.corners()
    compute([(1, 1), (1, -1), (-1, 1), (-1, -1)])
    tokens.far_corners()
    others.far_corners()
    tokens.last()
    compute([(1, 2), (-1, 2), (2, 1), (2, -1), (2, 2)])
    others.last()

    def give(index):
        here = gout.at[index]
        there = got.at[:, pl.ds(pl.multiple_of(s * 256, 256), 256)]
        return pltpu.make_async_remote_copy(
            src_ref=here,
            dst_ref=there,
            send_sem=got_send.at[index],
            recv_sem=got_recv.at[s],
            device_id=(p, index),
            device_id_type=MESH,
        )

    def scan(index, carry):
        gated = advance(index, state_ref, store)

        @pl.when(index != s)
        def _():
            gout[index] = gated
            give(index).start()

        @pl.when(index == s)
        def _():
            got[:, pl.ds(pl.multiple_of(s * 256, 256), 256)] = gated

        return carry

    lax.fori_loop(0, 8, scan, 0)
    for item in passed[:16]:
        from_z(*item)
    lax.fori_loop(8, SEQ, scan, 0)
    for h in range(HEADS):
        final_ref[h] = state_ref[h].T
    for item in passed[16:]:
        from_z(*item)

    def receive(step, carry):
        source = (s + step) % SEQ
        there = got.at[:, pl.ds(pl.multiple_of(source * 256, 256), 256)]
        pltpu.make_async_remote_copy(
            src_ref=gout.at[source],
            dst_ref=there,
            send_sem=got_send.at[source],
            recv_sem=got_recv.at[source],
            device_id=(p, source),
            device_id_type=MESH,
        ).wait()
        return carry

    lax.fori_loop(1, SEQ, receive, 0)
    for item in passed:
        from_mate(*item)
    for copy in started + tokens.started + others.started:
        copy.wait_send()
    for side in (0, 1):
        for par in (0, 1):
            first = (2 * side + par) * 512
            out_ref[:, first : first + 512] = mm(got[...], wall[side, par])


def attention(length, own, w_output, weights, rate, gain, first):
    rows, width = own.shape
    vmem = pl.BlockSpec(memory_space=pltpu.VMEM)
    dma = pltpu.SemaphoreType.DMA
    return pl.pallas_call(
        attention_kernel,
        in_specs=[pl.BlockSpec(memory_space=pltpu.SMEM)] + [vmem] * 6,
        out_specs=[vmem, vmem],
        out_shape=[
            jax.ShapeDtypeStruct((rows, width), F32),
            jax.ShapeDtypeStruct((HEADS, 128, 128), F32),
        ],
        scratch_shapes=[
            pltpu.VMEM((SEQ, rows, width), BF16),
            pltpu.VMEM((2, 2, SEQ * 256, 512), BF16),
            pltpu.VMEM((rows, SEQ * 256), BF16),
            pltpu.VMEM((SEQ, rows, 256), BF16),
            pltpu.VMEM((SEQ, HEADS, 2 * CH, 128), BF16),
            pltpu.VMEM((SEQ, HEADS, 128, CH), BF16),
            pltpu.VMEM((SEQ, HEADS, CH, CH), BF16),
            pltpu.VMEM((SEQ, HEADS, CH, 128), F32),
            pltpu.VMEM((SEQ, HEADS, 8, CH), F32),
            pltpu.VMEM((SEQ, HEADS, CH, 128), F32),
            pltpu.VMEM((HEADS, 128, 128), F32),
            dma((2, 2, 32)),
            dma((2, 2, 32)),
            dma((2, 16)),
            dma((2, 16)),
            dma((2, 2, 16)),
            dma((2, 2, 16)),
            dma((SEQ,)),
            dma((SEQ,)),
        ],
        compiler_params=pltpu.CompilerParams(
            collective_id=0, has_side_effects=True, vmem_limit_bytes=56 * 2**20
        ),
    )(length, own, w_output, weights, rate, gain, first)


CAP = 8
ROWS = 2 * CAP
TOP = 10
PCOLS = 1280
QCOLS = 768


def select(slots, meta):
    hit = slots == meta[0:1, :]
    for j in range(1, TOP):
        hit = hit | (slots == meta[j : j + 1, :])
    return jnp.where(hit, 1.0, 0.0).astype(BF16)


def expert_kernel(
    own_ref,
    meta_ref,
    win_hbm,
    wout_hbm,
    out_ref,
    ptok,
    qtok,
    pmeta,
    qmeta,
    pout,
    qout,
    arr,
    win,
    wout,
    ring_send,
    ring_recv,
    z_send,
    z_recv,
    meta_send,
    meta_recv,
    p_send,
    p_recv,
    q_send,
    q_recv,
    local_sem,
):
    p = lax.axis_index("prompt")
    s = lax.axis_index("seq")
    z, c = p // 2, p % 2
    depths = 4

    def depth(step):
        return ((z + step + depths) % depths) * 2 + c

    loads = [
        pltpu.make_async_copy(win_hbm, win, local_sem.at[0]),
        pltpu.make_async_copy(wout_hbm, wout, local_sem.at[1]),
    ]
    for load in loads:
        load.start()
    barrier = pltpu.get_barrier_semaphore()

    def greet_plane(step, carry):
        for core in (0, 1):
            pl.semaphore_signal(
                barrier, 1, device_id=(2 * z + core, (s + step) % SEQ), device_id_type=MESH
            )
        return carry

    lax.fori_loop(1, SEQ, greet_plane, 0)

    def greet_column(step, carry):
        pl.semaphore_signal(barrier, 1, device_id=((p + step) % (2 * depths), s), device_id_type=MESH)
        return carry

    lax.fori_loop(1, 2 * depths, greet_column, 0)
    ptok[s] = own_ref[:, :PCOLS]
    qtok[z] = own_ref[:, PCOLS:]
    pmeta[s] = meta_ref[...]
    qmeta[z] = meta_ref[...]
    pl.semaphore_wait(barrier, 2 * (SEQ - 1) + 2 * depths - 1)

    def plane_meta(step):
        there = (s + step) % SEQ
        return pltpu.make_async_remote_copy(
            src_ref=meta_ref,
            dst_ref=pmeta.at[s],
            send_sem=meta_send.at[step],
            recv_sem=meta_recv.at[s],
            device_id=(p, there),
            device_id_type=MESH,
        )

    def plane_meta_from(step):
        source = (s + step) % SEQ
        return pltpu.make_async_remote_copy(
            src_ref=meta_ref,
            dst_ref=pmeta.at[source],
            send_sem=meta_send.at[step],
            recv_sem=meta_recv.at[source],
            device_id=(p, source),
            device_id_type=MESH,
        )

    def depth_meta(step):
        return pltpu.make_async_remote_copy(
            src_ref=meta_ref,
            dst_ref=qmeta.at[z],
            send_sem=meta_send.at[SEQ + step],
            recv_sem=meta_recv.at[SEQ + z],
            device_id=(depth(step), s),
            device_id_type=MESH,
        )

    def depth_meta_from(step):
        source = (z + step) % depths
        return pltpu.make_async_remote_copy(
            src_ref=meta_ref,
            dst_ref=qmeta.at[source],
            send_sem=meta_send.at[SEQ + step],
            recv_sem=meta_recv.at[SEQ + source],
            device_id=(depth(step), s),
            device_id_type=MESH,
        )

    def start_plane_meta(step, carry):
        plane_meta(step).start()
        return carry

    lax.fori_loop(1, SEQ, start_plane_meta, 0)
    for step in (1, 2, 3):
        depth_meta(step).start()

    def at(half, owner, first, count):
        return ptok.at[owner, pl.ds(first, count), pl.ds(half * (PCOLS // 2), PCOLS // 2)]

    rings = Rings(p, s, at, ring_send, ring_recv)

    def z_copy(source, span, step, slot):
        piece = qtok.at[source, pl.ds(*span), :]
        return pltpu.make_async_remote_copy(
            src_ref=piece,
            dst_ref=piece,
            send_sem=z_send.at[slot],
            recv_sem=z_recv.at[slot],
            device_id=(depth(step), s),
            device_id_type=MESH,
        )

    z_copies = [z_copy(z, FULL, 1, 0), z_copy(z, FULL, -1, 1)]
    for copy in z_copies:
        copy.start()
    rings.begin()

    rows = lax.broadcasted_iota(jnp.int32, (8 * ROWS, 128), 0)
    p_slots = ((rows // ROWS) * (SEQ * ROWS) + s * ROWS + rows % ROWS).astype(F32)

    def p_copy(source, there):
        return pltpu.make_async_remote_copy(
            src_ref=pout.at[source, there],
            dst_ref=arr.at[z, c, source, :, pl.ds(0, PCOLS)],
            send_sem=p_send.at[source, there],
            recv_sem=p_recv.at[p, source],
            device_id=(there, s),
            device_id_type=MESH,
        )

    def p_hand(source):
        picked = mm(select(p_slots, pmeta[source]), ptok[source]).astype(BF16)
        pout[source] = picked.reshape(8, ROWS, PCOLS)

        def go(step, carry):
            p_copy(source, (p + step) % 8).start()
            return carry

        lax.fori_loop(1, 8, go, 0)
        arr[z, c, source, :, 0:PCOLS] = pout[source, p]

    def p_hands(offsets):
        for dx, dy in offsets:
            source = ring_spot(s, 1, dx, dy)
            step = ((dx % RING) * RING + dy % RING)
            pltpu.make_async_remote_copy(
                src_ref=meta_ref,
                dst_ref=pmeta.at[source],
                send_sem=meta_send.at[0],
                recv_sem=meta_recv.at[source],
                device_id=(p, source),
                device_id_type=MESH,
            ).wait_recv()
            p_hand(source)

    def q_copy(there):
        return pltpu.make_async_remote_copy(
            src_ref=qout.at[:, there],
            dst_ref=arr.at[:, c, s, :, pl.ds(PCOLS, QCOLS)],
            send_sem=q_send.at[there],
            recv_sem=q_recv.at[c, s],
            device_id=(2 * z + there // SEQ, there % SEQ),
            device_id_type=MESH,
        )

    def q_hand(source):
        slots = (z * (2 * SEQ * ROWS) + lax.broadcasted_iota(jnp.int32, (2 * SEQ * ROWS, 128), 0)).astype(F32)
        picked = mm(select(slots, qmeta[source]), qtok[source]).astype(BF16)
        qout[source] = picked.reshape(2 * SEQ, ROWS, QCOLS)

    p_hand(s)
    q_hand(z)
    z_copy((z + 3) % depths, FULL, 1, 0).wait_recv()
    z_copy((z + 1) % depths, FULL, -1, 1).wait_recv()
    z_copies.append(z_copy((z + 3) % depths, LOW, 1, 2))
    z_copies.append(z_copy((z + 1) % depths, HIGH, -1, 3))
    z_copies[2].start()
    z_copies[3].start()
    for step in (1, 3):
        depth_meta_from(step).wait_recv()
        q_hand((z + step) % depths)
    rings.near()
    p_hands([(0, 1), (0, -1), (1, 0), (-1, 0)])
    depth_meta_from(2).wait_recv()
    z_copy((z + 2) % depths, LOW, 1, 2).wait_recv()
    z_copy((z + 2) % depths, HIGH, -1, 3).wait_recv()
    q_hand((z + 2) % depths)
    here = c * SEQ + s

    def q_go(step, carry):
        q_copy((here + step) % (2 * SEQ)).start()
        return carry

    rings.far()
    p_hands([(0, 2), (2, 0)])
    rings.corners()
    p_hands([(1, 1), (1, -1), (-1, 1), (-1, -1)])
    rings.far_corners()
    rings.last()
    lax.fori_loop(1, 2 * SEQ, q_go, 0)
    arr[:, c, s, :, PCOLS:] = qout[:, here]
    p_hands([(1, 2), (-1, 2), (2, 1), (2, -1), (2, 2)])

    def p_wait(step, carry):
        source, back = step // 8, step % 8

        @pl.when(back != p)
        def _():
            pltpu.make_async_remote_copy(
                src_ref=pout.at[source, back],
                dst_ref=arr.at[back // 2, back % 2, source, :, pl.ds(0, PCOLS)],
                send_sem=p_send.at[source, back],
                recv_sem=p_recv.at[back, source],
                device_id=(back, s),
                device_id_type=MESH,
            ).wait()

        return carry

    lax.fori_loop(0, 8 * SEQ, p_wait, 0)

    def q_wait(step, carry):
        back = (here + step) % (2 * SEQ)
        pltpu.make_async_remote_copy(
            src_ref=qout.at[:, back],
            dst_ref=arr.at[:, back // SEQ, back % SEQ, :, pl.ds(PCOLS, QCOLS)],
            send_sem=q_send.at[back],
            recv_sem=q_recv.at[back // SEQ, back % SEQ],
            device_id=(2 * z + back // SEQ, back % SEQ),
            device_id_type=MESH,
        ).wait()
        return carry

    lax.fori_loop(1, 2 * SEQ, q_wait, 0)
    for load in loads:
        load.wait()

    def experts(step, carry):
        sources = arr[step]
        width = sources.shape[-1]
        wide = sources.reshape(2 * SEQ, ROWS, width).astype(F32)
        results = []
        for e in range(2):
            mine = wide[:, e * CAP : (e + 1) * CAP, :].reshape(2 * SEQ * CAP, width).astype(BF16)
            pair = mm(mine, win[e])
            inner_width = wout.shape[1]
            gate = pair[:, :inner_width]
            inner = (gate / (1.0 + jnp.exp(-gate)) * pair[:, inner_width:]).astype(BF16)
            results.append(mm(inner, wout[e]).reshape(2 * SEQ, CAP, width))
        result = jnp.concatenate(results, axis=1).astype(BF16)
        arr[step] = result.reshape(sources.shape)
        pltpu.make_async_copy(arr.at[step], out_ref.at[step], local_sem.at[2 + step]).start()
        return carry

    lax.fori_loop(0, depths, experts, 0)
    for step in range(depths):
        pltpu.make_async_copy(arr.at[step], out_ref.at[step], local_sem.at[2 + step]).wait()
    for copy in rings.started + z_copies:
        copy.wait_send()

    def meta_wait(step, carry):
        plane_meta(step).wait_send()
        return carry

    lax.fori_loop(1, SEQ, meta_wait, 0)
    for step in (1, 2, 3):
        depth_meta(step).wait_send()


def run_experts(own, meta, w_in, w_out):
    rows, width = own.shape
    vmem = pl.BlockSpec(memory_space=pltpu.VMEM)
    hbm = pl.BlockSpec(memory_space=pl.ANY)
    dma = pltpu.SemaphoreType.DMA
    return pl.pallas_call(
        expert_kernel,
        in_specs=[vmem, vmem, hbm, hbm],
        out_specs=hbm,
        out_shape=jax.ShapeDtypeStruct((4, 2, SEQ, ROWS, width), BF16),
        scratch_shapes=[
            pltpu.VMEM((SEQ, rows, PCOLS), BF16),
            pltpu.VMEM((4, rows, QCOLS), BF16),
            pltpu.VMEM((SEQ, 16, rows), F32),
            pltpu.VMEM((4, 16, rows), F32),
            pltpu.VMEM((SEQ, 8, ROWS, PCOLS), BF16),
            pltpu.VMEM((4, 2 * SEQ, ROWS, QCOLS), BF16),
            pltpu.VMEM((4, 2, SEQ, ROWS, width), BF16),
            pltpu.VMEM(w_in.shape, BF16),
            pltpu.VMEM(w_out.shape, BF16),
            dma((2, 32)),
            dma((2, 32)),
            dma((4,)),
            dma((4,)),
            dma((SEQ + 4,)),
            dma((SEQ + 4,)),
            dma((SEQ, 8)),
            dma((8, SEQ)),
            dma((2 * SEQ,)),
            dma((2, SEQ)),
            dma((6,)),
        ],
        compiler_params=pltpu.CompilerParams(
            collective_id=1, has_side_effects=True, vmem_limit_bytes=58 * 2**20
        ),
    )(own, meta, w_in, w_out)


def rms_scale(values, gain):
    mean = jnp.mean(values * values, axis=-1, keepdims=True)
    return values * lax.rsqrt(mean + EPS) * gain


def routing(chosen_ids, experts):
    tokens = chosen_ids.shape[0]
    table = lax.broadcasted_iota(jnp.int32, (1, 1, experts), 2)
    match = chosen_ids[:, :, None] == table
    member = jnp.any(match, axis=1)
    rows = lax.broadcasted_iota(jnp.int32, (tokens, tokens), 0)
    cols = lax.broadcasted_iota(jnp.int32, (tokens, tokens), 1)
    earlier = (rows > cols).astype(BF16)
    before = jnp.dot(earlier, member.astype(BF16), preferred_element_type=F32)
    place = jnp.sum(jnp.where(match, before[:, None, :], 0.0), axis=-1)
    return member, before, chosen_ids.astype(F32) * CAP + place


def shards(
    tokens,
    span_lengths,
    state_slots,
    expert_ids,
    state_pool,
    attn_gain,
    w_query,
    w_key,
    w_value,
    w_zgate,
    w_heads,
    decay_rate,
    head_gain,
    w_output,
    moe_gain,
    router,
    w_expert_in,
    w_expert_out,
):
    local_rows, width = tokens.shape[1:]
    length = span_lengths[0]
    own_rows = tokens[0]
    normed = rms_scale(own_rows.astype(F32), attn_gain).astype(BF16)
    head_weights = jnp.pad(w_heads.reshape(width, 4), ((0, 0), (0, 124)))
    weights_all = jnp.concatenate([w_query, w_key, w_value, w_zgate, head_weights], axis=1)
    first = lax.dynamic_index_in_dim(state_pool, state_slots[0], 0, keepdims=False)
    rate = jnp.pad(decay_rate, (0, 126)).reshape(1, 128)
    summed, final = attention(
        span_lengths, normed, w_output, weights_all, rate, head_gain.reshape(1, 128), first
    )
    own_positions = lax.axis_index("seq") * local_rows + lax.broadcasted_iota(jnp.int32, (local_rows, 1), 0)
    own_live = (own_positions < length).astype(F32)
    attended = (summed * own_live).astype(BF16)
    residual = own_rows.astype(F32) + attended.astype(F32)
    moe_input = rms_scale(residual, moe_gain).astype(BF16)
    logits = jnp.dot(moe_input, router, preferred_element_type=F32)
    experts_all = router.shape[1]
    member, before, target = routing(expert_ids[0], experts_all)
    top = jnp.max(jnp.where(member, logits, -jnp.inf), axis=-1, keepdims=True)
    powers = jnp.where(member, jnp.exp(logits - top), 0.0)
    weights = powers / jnp.sum(powers, axis=-1, keepdims=True) * own_live
    slots = lax.broadcasted_iota(jnp.int32, (1, CAP, 1), 1).astype(F32)
    place = jnp.where(member, before, -1.0).T
    combine = jnp.where(place[:, None, :] == slots, weights.T[:, None, :], 0.0)
    combine = combine.reshape(experts_all * CAP, local_rows).astype(BF16)
    meta = jnp.pad(target.T, ((0, 16 - TOP), (0, 0)), constant_values=-1.0)
    result = run_experts(moe_input, meta, w_expert_in, w_expert_out)
    result = result.reshape(-1, ROWS, width)
    returned = lax.all_to_all(result, ("prompt", "seq"), split_axis=0, concat_axis=0, tiled=True)
    expert_out = lax.dot_general(
        combine,
        returned.reshape(experts_all * CAP, width),
        (((0,), (0,)), ((), ())),
        preferred_element_type=F32,
    ).astype(BF16)
    return (attended[None], expert_out[None], final[None])


def solution(mesh):
    return jax.shard_map(
        shards,
        mesh=mesh,
        in_specs=(
            P("prompt", "seq", None),
            P("prompt"),
            P("prompt"),
            P("prompt", "seq", None),
            P(None, "seq", None, None),
            P(),
            P(None, "seq"),
            P(None, "seq"),
            P(None, "seq"),
            P(None, "seq"),
            P(None, None, "seq"),
            P("seq"),
            P(),
            P("seq", None),
            P(),
            P(),
            P(("prompt", "seq"), None, None),
            P(("prompt", "seq"), None, None),
        ),
        out_specs=(
            P("prompt", "seq", None),
            P("prompt", "seq", None),
            P("prompt", "seq", None, None),
        ),
        check_vma=False,
    )
```

```python
import functools
import jax
import jax.numpy as jnp
from jax import lax
from jax.experimental import pallas as pl
from jax.experimental.pallas import tpu as pltpu
from jax.sharding import PartitionSpec as P

EPS = 1e-06
CH = 128
RING = 4
SEQ = RING * RING
HEADS = 2
F32 = jnp.float32
BF16 = jnp.bfloat16
MESH = pl.DeviceIdType.MESH


def mm(a, b):
    return jnp.dot(a, b, preferred_element_type=F32)


def halves(a):
    high = a.astype(BF16)
    return high, (a - high.astype(F32)).astype(BF16)


def mm3(a, b):
    a_high, a_low = halves(a)
    b_high, b_low = halves(b)
    wide = mm(jnp.concatenate([a_high, a_low], axis=1), jnp.concatenate([b_high, b_high], axis=0))
    return wide + mm(a_high, b_low)


def unit_lower_inverse(lows, rows, cols):
    eye = jnp.where(rows == cols, 1.0, 0.0)
    inverses = [eye - jnp.where(rows // 2 == cols // 2, low, 0.0) for low in lows]
    size = 2
    while size < CH:
        mask = (rows // (2 * size) == cols // (2 * size)) & (rows // size != cols // size)
        inner = [mm3(jnp.where(mask, low, 0.0), inv) for low, inv in zip(lows, inverses)]
        inverses = [inv - mm3(inv, part) for inv, part in zip(inverses, inner)]
        size *= 2
    return inverses


def prepare(blocks, length, tok, w_ref, rate, gain, store):
    left_ref, kt_ref, attn_ref, upd_ref, last_ref, gate_ref = store
    rows = lax.broadcasted_iota(jnp.int32, (CH, CH), 0)
    cols = lax.broadcasted_iota(jnp.int32, (CH, CH), 1)
    tri = jnp.where(rows >= cols, 1.0, 0.0)
    proj_all = mm(jnp.concatenate([tok[b] for b in blocks], axis=0), w_ref[...])
    lows = []
    rights = []
    for n, block in enumerate(blocks):
        part = proj_all[n * CH : (n + 1) * CH]
        q, k = part[:, 0:128], part[:, 128:256]
        q = q * (lax.rsqrt(jnp.sum(q * q, axis=-1, keepdims=True) + EPS) * 128 ** (-0.5))
        k = k * lax.rsqrt(jnp.sum(k * k, axis=-1, keepdims=True) + EPS)
        logits = part[:, 768:896]
        live = jnp.where(block * CH + rows < length, 1.0, 0.0)
        softplus = jnp.maximum(logits, 0.0) + jnp.log1p(jnp.exp(-jnp.abs(logits)))
        logdec = -rate * softplus * live
        beta2 = live / (1.0 + jnp.exp(-logits))
        cumul = jnp.dot(tri, logdec, preferred_element_type=F32, precision=lax.Precision.HIGHEST)
        cumul_t = cumul.T
        both = mm(jnp.concatenate([k.astype(BF16), q.astype(BF16)], axis=0), k.T.astype(BF16))
        kk, qk = both[:CH], both[CH:]
        for h in range(HEADS):
            g = cumul[:, h : h + 1]
            decay = jnp.exp(jnp.minimum(g - cumul_t[h : h + 1, :], 0.0))
            beta = beta2[:, 2 + h : 3 + h]
            lows.append(jnp.where(rows > cols, beta * kk * decay, 0.0))
            attn_ref[block, h] = jnp.where(rows >= cols, qk * decay, 0.0).astype(BF16)
            start = jnp.exp(g)
            value = part[:, 256 + 128 * h : 384 + 128 * h]
            rights.append(jnp.concatenate([beta * value, (beta * start) * k], axis=1).astype(BF16))
            last = cumul[CH - 1 : CH, h : h + 1]
            left_ref[block, h, CH:, :] = (start * q).astype(BF16)
            kt_ref[block, h] = (jnp.exp(last - g) * k).T.astype(BF16)
            last_ref[block, h] = jnp.broadcast_to(jnp.exp(last), (8, CH))
            z = part[:, 512 + 128 * h : 640 + 128 * h]
            gate_ref[block, h] = gain * (z / (1.0 + jnp.exp(-z)))
    for n, inverse in enumerate(unit_lower_inverse(lows, rows, cols)):
        block, h = blocks[n // HEADS], n % HEADS
        high, low = halves(inverse)
        got = mm(jnp.concatenate([high, low], axis=1), jnp.concatenate([rights[n], rights[n]], axis=0))
        upd_ref[block, h] = got[:, :CH]
        left_ref[block, h, :CH, :] = got[:, CH:].astype(BF16)


def advance(block, state_ref, store):
    left_ref, kt_ref, attn_ref, upd_ref, last_ref, gate_ref = store
    outs = []
    for h in range(HEADS):
        state = state_ref[h]
        left = left_ref[block, h]
        high, low = halves(state)
        got = mm(jnp.concatenate([left, left], axis=1), jnp.concatenate([high, low], axis=0))
        corrected = upd_ref[block, h] - got[:CH]
        high, low = halves(corrected)
        kt = kt_ref[block, h]
        state_ref[h] = last_ref[block, h, 0:1, :] * state + mm(
            jnp.concatenate([kt, kt], axis=1), jnp.concatenate([high, low], axis=0)
        )
        out = got[CH:] + mm(attn_ref[block, h], high)
        scale = lax.rsqrt(jnp.mean(out * out, axis=-1, keepdims=True) + EPS)
        outs.append((out * scale * gate_ref[block, h]).astype(BF16))
    return jnp.concatenate(outs, axis=1)


def ring_spot(s, half, df, dg):
    dx, dy = (dg, df) if half == 0 else (df, dg)
    x, y = s // RING, s % RING
    return ((x + dx + 2 * RING) % RING) * RING + (y + dy + 2 * RING) % RING


FULL, LOW, HIGH = (0, 128), (0, 64), (64, 64)


class Rings:
    def __init__(self, p, s, at, send_sem, recv_sem, hook=None):
        self.p, self.s, self.at = p, s, at
        self.send_sem, self.recv_sem = send_sem, recv_sem
        self.hook = hook or (lambda half, df, dg: None)
        self.started = []

    def copy(self, half, df, dg, span, tf, tg):
        slot = ((df - tf) % RING * RING + (dg - tg) % RING) * 2 + (1 if span is HIGH else 0)
        piece = self.at(half, ring_spot(self.s, half, df, dg), *span)
        return pltpu.make_async_remote_copy(
            src_ref=piece,
            dst_ref=piece,
            send_sem=self.send_sem.at[half, slot],
            recv_sem=self.recv_sem.at[half, slot],
            device_id=(self.p, ring_spot(self.s, half, tf, tg)),
            device_id_type=MESH,
        )

    def send(self, *args):
        copy = self.copy(*args)
        copy.start()
        self.started.append(copy)

    def arrive(self, half, df, dg, span=FULL):
        slot = (df % RING * RING + dg % RING) * 2 + (1 if span is HIGH else 0)
        piece = self.at(half, ring_spot(self.s, half, df, dg), *span)
        pltpu.make_async_remote_copy(
            src_ref=piece,
            dst_ref=piece,
            send_sem=self.send_sem.at[half, slot],
            recv_sem=self.recv_sem.at[half, slot],
            device_id=(self.p, ring_spot(self.s, half, 1, 0)),
            device_id_type=MESH,
        ).wait_recv()

    def begin(self):
        for half in (0, 1):
            for step in (1, -1):
                self.send(half, 0, 0, FULL, step, 0)
        for half in (0, 1):
            for step in (1, -1):
                self.send(half, 0, 0, FULL, 0, step)

    def first_near(self):
        for half in (0, 1):
            for df, span in ((-1, LOW), (1, HIGH)):
                self.arrive(half, df, 0)
                self.send(half, df, 0, span, -df, 0)
            self.hook(half, -1, 0)
            self.hook(half, 1, 0)

    def second_near(self):
        for half in (0, 1):
            for dg, span in ((-1, LOW), (1, HIGH)):
                self.arrive(half, 0, dg)
                self.send(half, 0, dg, span, 0, -dg)
            self.hook(half, 0, -1)
            self.hook(half, 0, 1)
            for df in (-1, 1):
                for step in (1, -1):
                    self.send(half, df, 0, FULL, 0, step)

    def near(self):
        self.first_near()
        self.second_near()

    def far(self):
        for half in (0, 1):
            self.arrive(half, 2, 0, LOW)
            self.arrive(half, 2, 0, HIGH)
            for step in (1, -1):
                self.send(half, 2, 0, FULL, 0, step)
            self.hook(half, 2, 0)
        self.second_far((0,))

    def second_far(self, dfs):
        for half in (0, 1):
            for df in dfs:
                self.arrive(half, df, 2, LOW)
                self.arrive(half, df, 2, HIGH)
                self.hook(half, df, 2)

    def corners(self, dfs=(-1, 1)):
        for half in (0, 1):
            for df in dfs:
                for dg, span in ((-1, LOW), (1, HIGH)):
                    self.arrive(half, df, dg)
                    self.send(half, df, dg, span, 0, -dg)
                    self.hook(half, df, dg)

    def far_corners(self):
        self.corners((2,))

    def last(self):
        self.second_far((-1, 1, 2))


def attention_kernel(
    length_ref,
    own_ref,
    wo_ref,
    w_ref,
    rate_ref,
    gain_ref,
    first_ref,
    out_ref,
    final_ref,
    tok,
    wall,
    got,
    gout,
    left_ref,
    kt_ref,
    attn_ref,
    upd_ref,
    last_ref,
    gate_ref,
    state_ref,
    ring_send,
    ring_recv,
    z_send,
    z_recv,
    mate_send,
    mate_recv,
    got_send,
    got_recv,
):
    store = (left_ref, kt_ref, attn_ref, upd_ref, last_ref, gate_ref)
    p = lax.axis_index("prompt")
    s = lax.axis_index("seq")
    z, c = p // 2, p % 2
    x, y = s // RING, s % RING
    parity = z % 2
    length = length_ref[0]
    tcols = tok.shape[2] // 2

    def spot(half, df, dg):
        return ring_spot(s, half, df, dg)

    def depth(step):
        return ((z + step + RING) % RING) * 2 + c

    mate = z * 2 + (1 - c)

    def at(chan, half, owner, first, count, side=None, par=None):
        if chan == 0:
            return tok.at[owner, pl.ds(first, count), pl.ds(half * tcols, tcols)]
        row = pl.multiple_of(owner * 256 + half * 128 + first, 64)
        return wall.at[c if side is None else side, parity if par is None else par, pl.ds(row, count), :]

    started = []
    passed = []

    def hand_on(half, df, dg):
        owner = spot(half, df, dg)
        slot = (df % RING) * RING + dg % RING
        piece = at(1, half, owner, *FULL)
        copy = pltpu.make_async_remote_copy(
            src_ref=piece,
            dst_ref=piece,
            send_sem=z_send.at[half, slot],
            recv_sem=z_recv.at[half, slot],
            device_id=(depth(1 if half == 0 else -1), s),
            device_id_type=MESH,
        )
        copy.start()
        started.append(copy)
        copy = to_mate(half, df, dg, parity, 0)
        copy.start()
        started.append(copy)
        passed.append((half, df, dg))

    def to_mate(half, df, dg, par, kind):
        slot = (df % RING) * RING + dg % RING
        piece = at(1, half, spot(half, df, dg), *FULL, par=par)
        return pltpu.make_async_remote_copy(
            src_ref=piece,
            dst_ref=piece,
            send_sem=mate_send.at[kind, half, slot],
            recv_sem=mate_recv.at[kind, half, slot],
            device_id=(mate, s),
            device_id_type=MESH,
        )

    def from_z(half, df, dg):
        owner = spot(half, df, dg)
        slot = (df % RING) * RING + dg % RING
        piece = at(1, half, owner, *FULL, par=1 - parity)
        pltpu.make_async_remote_copy(
            src_ref=piece,
            dst_ref=piece,
            send_sem=z_send.at[half, slot],
            recv_sem=z_recv.at[half, slot],
            device_id=(depth(1), s),
            device_id_type=MESH,
        ).wait_recv()
        copy = to_mate(half, df, dg, 1 - parity, 1)
        copy.start()
        started.append(copy)

    def from_mate(half, df, dg):
        slot = (df % RING) * RING + dg % RING
        for kind in (0, 1):
            piece = at(1, half, spot(half, df, dg), *FULL, side=1 - c, par=parity if kind == 0 else 1 - parity)
            pltpu.make_async_remote_copy(
                src_ref=piece,
                dst_ref=piece,
                send_sem=mate_send.at[kind, half, slot],
                recv_sem=mate_recv.at[kind, half, slot],
                device_id=(mate, s),
                device_id_type=MESH,
            ).wait_recv()

    tokens = Rings(p, s, functools.partial(at, 0), ring_send.at[0], ring_recv.at[0])
    others = Rings(p, s, functools.partial(at, 1), ring_send.at[1], ring_recv.at[1], hand_on)

    def block_of(dx, dy):
        return spot(1, dx, dy)

    def compute(offsets):
        prepare(
            [block_of(*offset) for offset in offsets], length, tok, w_ref, rate_ref[...], gain_ref[...], store
        )

    barrier = pltpu.get_barrier_semaphore()

    def greet(step, carry):
        pl.semaphore_signal(barrier, 1, device_id=(p, (s + step) % SEQ), device_id_type=MESH)
        return carry

    lax.fori_loop(1, SEQ, greet, 0)
    for other in (mate, depth(1), depth(-1)):
        pl.semaphore_signal(barrier, 1, device_id=(other, s), device_id_type=MESH)
    tok[s] = own_ref[...]
    for side in (0, 1):
        for par in (0, 1):
            first = (2 * side + par) * 512
            wall[side, par, pl.ds(pl.multiple_of(s * 256, 256), 256), :] = wo_ref[:, first : first + 512]
    for h in range(HEADS):
        state_ref[h] = first_ref[h].T
    pl.semaphore_wait(barrier, SEQ + 2)

    tokens.begin()
    others.begin()
    compute([(0, 0)])
    tokens.near()
    others.near()
    compute([(0, 1), (0, -1), (1, 0), (-1, 0)])
    tokens.far()
    others.far()
    compute([(0, 2), (2, 0)])
    tokens.corners()
    others.corners()
    compute([(1, 1), (1, -1), (-1, 1), (-1, -1)])
    tokens.far_corners()
    others.far_corners()
    tokens.last()
    compute([(1, 2), (-1, 2), (2, 1), (2, -1), (2, 2)])
    others.last()

    def give(index):
        here = gout.at[index]
        there = got.at[:, pl.ds(pl.multiple_of(s * 256, 256), 256)]
        return pltpu.make_async_remote_copy(
            src_ref=here,
            dst_ref=there,
            send_sem=got_send.at[index],
            recv_sem=got_recv.at[s],
            device_id=(p, index),
            device_id_type=MESH,
        )

    def scan(index, carry):
        gated = advance(index, state_ref, store)

        @pl.when(index != s)
        def _():
            gout[index] = gated
            give(index).start()

        @pl.when(index == s)
        def _():
            got[:, pl.ds(pl.multiple_of(s * 256, 256), 256)] = gated

        return carry

    lax.fori_loop(0, 8, scan, 0)
    for item in passed[:16]:
        from_z(*item)
    lax.fori_loop(8, SEQ, scan, 0)
    for h in range(HEADS):
        final_ref[h] = state_ref[h].T
    for item in passed[16:]:
        from_z(*item)

    def receive(step, carry):
        source = (s + step) % SEQ
        there = got.at[:, pl.ds(pl.multiple_of(source * 256, 256), 256)]
        pltpu.make_async_remote_copy(
            src_ref=gout.at[source],
            dst_ref=there,
            send_sem=got_send.at[source],
            recv_sem=got_recv.at[source],
            device_id=(p, source),
            device_id_type=MESH,
        ).wait()
        return carry

    lax.fori_loop(1, SEQ, receive, 0)
    for item in passed:
        from_mate(*item)
    for copy in started + tokens.started + others.started:
        copy.wait_send()
    for side in (0, 1):
        for par in (0, 1):
            first = (2 * side + par) * 512
            out_ref[:, first : first + 512] = mm(got[...], wall[side, par])


def attention(length, own, w_output, weights, rate, gain, first):
    rows, width = own.shape
    vmem = pl.BlockSpec(memory_space=pltpu.VMEM)
    dma = pltpu.SemaphoreType.DMA
    return pl.pallas_call(
        attention_kernel,
        in_specs=[pl.BlockSpec(memory_space=pltpu.SMEM)] + [vmem] * 6,
        out_specs=[vmem, vmem],
        out_shape=[
            jax.ShapeDtypeStruct((rows, width), F32),
            jax.ShapeDtypeStruct((HEADS, 128, 128), F32),
        ],
        scratch_shapes=[
            pltpu.VMEM((SEQ, rows, width), BF16),
            pltpu.VMEM((2, 2, SEQ * 256, 512), BF16),
            pltpu.VMEM((rows, SEQ * 256), BF16),
            pltpu.VMEM((SEQ, rows, 256), BF16),
            pltpu.VMEM((SEQ, HEADS, 2 * CH, 128), BF16),
            pltpu.VMEM((SEQ, HEADS, 128, CH), BF16),
            pltpu.VMEM((SEQ, HEADS, CH, CH), BF16),
            pltpu.VMEM((SEQ, HEADS, CH, 128), F32),
            pltpu.VMEM((SEQ, HEADS, 8, CH), F32),
            pltpu.VMEM((SEQ, HEADS, CH, 128), F32),
            pltpu.VMEM((HEADS, 128, 128), F32),
            dma((2, 2, 32)),
            dma((2, 2, 32)),
            dma((2, 16)),
            dma((2, 16)),
            dma((2, 2, 16)),
            dma((2, 2, 16)),
            dma((SEQ,)),
            dma((SEQ,)),
        ],
        compiler_params=pltpu.CompilerParams(
            collective_id=0, has_side_effects=True, vmem_limit_bytes=56 * 2**20
        ),
    )(length, own, w_output, weights, rate, gain, first)


CAP = 8
ROWS = 2 * CAP
TOP = 10
PCOLS = 1280
QCOLS = 768


def select(slots, meta):
    hit = slots == meta[0:1, :]
    for j in range(1, TOP):
        hit = hit | (slots == meta[j : j + 1, :])
    return jnp.where(hit, 1.0, 0.0).astype(BF16)


def mix(slots, meta):
    share = jnp.where(slots == meta[0:1, :], meta[16:17, :], 0.0)
    for j in range(1, TOP):
        share = share + jnp.where(slots == meta[j : j + 1, :], meta[16 + j : 17 + j, :], 0.0)
    return share.T.astype(BF16)


def expert_kernel(
    own_ref,
    meta_ref,
    win_hbm,
    wout_hbm,
    out_ref,
    ptok,
    qtok,
    pmeta,
    qmeta,
    pout,
    qout,
    arr,
    win,
    wout,
    ring_send,
    ring_recv,
    z_send,
    z_recv,
    meta_send,
    meta_recv,
    p_send,
    p_recv,
    q_send,
    q_recv,
    local_sem,
    retp,
    retq,
    rs_a,
    rs_b,
    rs_c,
    rs_d,
    rs_q,
    r_send,
    r_recv,
    rq_send,
    rq_recv,
    rs_send,
    rs_recv,
    rsq_send,
    rsq_recv,
):
    p = lax.axis_index("prompt")
    s = lax.axis_index("seq")
    z, c = p // 2, p % 2
    depths = 4

    def depth(step):
        return ((z + step + depths) % depths) * 2 + c

    loads = [
        pltpu.make_async_copy(win_hbm, win, local_sem.at[0]),
        pltpu.make_async_copy(wout_hbm, wout, local_sem.at[1]),
    ]
    for load in loads:
        load.start()
    barrier = pltpu.get_barrier_semaphore()

    def greet_plane(step, carry):
        for core in (0, 1):
            pl.semaphore_signal(
                barrier, 1, device_id=(2 * z + core, (s + step) % SEQ), device_id_type=MESH
            )
        return carry

    lax.fori_loop(1, SEQ, greet_plane, 0)

    def greet_column(step, carry):
        pl.semaphore_signal(barrier, 1, device_id=((p + step) % (2 * depths), s), device_id_type=MESH)
        return carry

    lax.fori_loop(1, 2 * depths, greet_column, 0)
    ptok[s] = own_ref[:, :PCOLS]
    qtok[z] = own_ref[:, PCOLS:]
    pmeta[s] = meta_ref[...]
    qmeta[z] = meta_ref[...]
    pl.semaphore_wait(barrier, 2 * (SEQ - 1) + 2 * depths - 1)

    def plane_meta(step):
        there = (s + step) % SEQ
        return pltpu.make_async_remote_copy(
            src_ref=meta_ref,
            dst_ref=pmeta.at[s],
            send_sem=meta_send.at[step],
            recv_sem=meta_recv.at[s],
            device_id=(p, there),
            device_id_type=MESH,
        )

    def plane_meta_from(step):
        source = (s + step) % SEQ
        return pltpu.make_async_remote_copy(
            src_ref=meta_ref,
            dst_ref=pmeta.at[source],
            send_sem=meta_send.at[step],
            recv_sem=meta_recv.at[source],
            device_id=(p, source),
            device_id_type=MESH,
        )

    def depth_meta(step):
        return pltpu.make_async_remote_copy(
            src_ref=meta_ref,
            dst_ref=qmeta.at[z],
            send_sem=meta_send.at[SEQ + step],
            recv_sem=meta_recv.at[SEQ + z],
            device_id=(depth(step), s),
            device_id_type=MESH,
        )

    def depth_meta_from(step):
        source = (z + step) % depths
        return pltpu.make_async_remote_copy(
            src_ref=meta_ref,
            dst_ref=qmeta.at[source],
            send_sem=meta_send.at[SEQ + step],
            recv_sem=meta_recv.at[SEQ + source],
            device_id=(depth(step), s),
            device_id_type=MESH,
        )

    def start_plane_meta(step, carry):
        plane_meta(step).start()
        return carry

    lax.fori_loop(1, SEQ, start_plane_meta, 0)
    for step in (1, 2, 3):
        depth_meta(step).start()

    def at(half, owner, first, count):
        return ptok.at[owner, pl.ds(first, count), pl.ds(half * (PCOLS // 2), PCOLS // 2)]

    rings = Rings(p, s, at, ring_send, ring_recv)

    def z_copy(source, span, step, slot):
        piece = qtok.at[source, pl.ds(*span), :]
        return pltpu.make_async_remote_copy(
            src_ref=piece,
            dst_ref=piece,
            send_sem=z_send.at[slot],
            recv_sem=z_recv.at[slot],
            device_id=(depth(step), s),
            device_id_type=MESH,
        )

    z_copies = [z_copy(z, FULL, 1, 0), z_copy(z, FULL, -1, 1)]
    for copy in z_copies:
        copy.start()
    rings.begin()

    rows = lax.broadcasted_iota(jnp.int32, (8 * ROWS, 128), 0)
    p_slots = ((rows // ROWS) * (SEQ * ROWS) + s * ROWS + rows % ROWS).astype(F32)

    def p_copy(source, there):
        return pltpu.make_async_remote_copy(
            src_ref=pout.at[source, there],
            dst_ref=arr.at[z, c, source, :, pl.ds(0, PCOLS)],
            send_sem=p_send.at[source, there],
            recv_sem=p_recv.at[p, source],
            device_id=(there, s),
            device_id_type=MESH,
        )

    def p_hand(source):
        picked = mm(select(p_slots, pmeta[source]), ptok[source]).astype(BF16)
        pout[source] = picked.reshape(8, ROWS, PCOLS)

        def go(step, carry):
            p_copy(source, (p + step) % 8).start()
            return carry

        lax.fori_loop(1, 8, go, 0)
        arr[z, c, source, :, 0:PCOLS] = pout[source, p]

    def p_hands(offsets):
        for dx, dy in offsets:
            source = ring_spot(s, 1, dx, dy)
            pltpu.make_async_remote_copy(
                src_ref=meta_ref,
                dst_ref=pmeta.at[source],
                send_sem=meta_send.at[0],
                recv_sem=meta_recv.at[source],
                device_id=(p, source),
                device_id_type=MESH,
            ).wait_recv()
            p_hand(source)

    def q_copy(there):
        return pltpu.make_async_remote_copy(
            src_ref=qout.at[:, there],
            dst_ref=arr.at[:, c, s, :, pl.ds(PCOLS, QCOLS)],
            send_sem=q_send.at[there],
            recv_sem=q_recv.at[c, s],
            device_id=(2 * z + there // SEQ, there % SEQ),
            device_id_type=MESH,
        )

    def q_hand(source):
        slots = (z * (2 * SEQ * ROWS) + lax.broadcasted_iota(jnp.int32, (2 * SEQ * ROWS, 128), 0)).astype(F32)
        picked = mm(select(slots, qmeta[source]), qtok[source]).astype(BF16)
        qout[source] = picked.reshape(2 * SEQ, ROWS, QCOLS)

    p_hand(s)
    q_hand(z)
    z_copy((z + 3) % depths, FULL, 1, 0).wait_recv()
    z_copy((z + 1) % depths, FULL, -1, 1).wait_recv()
    z_copies.append(z_copy((z + 3) % depths, LOW, 1, 2))
    z_copies.append(z_copy((z + 1) % depths, HIGH, -1, 3))
    z_copies[2].start()
    z_copies[3].start()
    for step in (1, 3):
        depth_meta_from(step).wait_recv()
        q_hand((z + step) % depths)
    rings.near()
    p_hands([(0, 1), (0, -1), (1, 0), (-1, 0)])
    depth_meta_from(2).wait_recv()
    z_copy((z + 2) % depths, LOW, 1, 2).wait_recv()
    z_copy((z + 2) % depths, HIGH, -1, 3).wait_recv()
    q_hand((z + 2) % depths)
    here = c * SEQ + s

    def q_go(step, carry):
        q_copy((here + step) % (2 * SEQ)).start()
        return carry

    rings.far()
    p_hands([(0, 2), (2, 0)])
    rings.corners()
    p_hands([(1, 1), (1, -1), (-1, 1), (-1, -1)])
    rings.far_corners()
    rings.last()
    lax.fori_loop(1, 2 * SEQ, q_go, 0)
    arr[:, c, s, :, PCOLS:] = qout[:, here]
    p_hands([(1, 2), (-1, 2), (2, 1), (2, -1), (2, 2)])

    def p_wait(step, carry):
        source, back = step // 8, step % 8

        @pl.when(back != p)
        def _():
            pltpu.make_async_remote_copy(
                src_ref=pout.at[source, back],
                dst_ref=arr.at[back // 2, back % 2, source, :, pl.ds(0, PCOLS)],
                send_sem=p_send.at[source, back],
                recv_sem=p_recv.at[back, source],
                device_id=(back, s),
                device_id_type=MESH,
            ).wait()

        return carry

    lax.fori_loop(0, 8 * SEQ, p_wait, 0)

    def q_wait(step, carry):
        back = (here + step) % (2 * SEQ)
        pltpu.make_async_remote_copy(
            src_ref=qout.at[:, back],
            dst_ref=arr.at[:, back // SEQ, back % SEQ, :, pl.ds(PCOLS, QCOLS)],
            send_sem=q_send.at[back],
            recv_sem=q_recv.at[back // SEQ, back % SEQ],
            device_id=(2 * z + back // SEQ, back % SEQ),
            device_id_type=MESH,
        ).wait()
        return carry

    lax.fori_loop(1, 2 * SEQ, q_wait, 0)
    for load in loads:
        load.wait()

    for copy in rings.started + z_copies:
        copy.wait_send()

    def r_copy(source, there):
        return pltpu.make_async_remote_copy(
            src_ref=arr.at[there // 2, there % 2, source, :, pl.ds(0, PCOLS)],
            dst_ref=retp.at[p, source],
            send_sem=r_send.at[source, there],
            recv_sem=r_recv.at[source, p],
            device_id=(there, s),
            device_id_type=MESH,
        )

    def r_copy_from(source, back):
        return pltpu.make_async_remote_copy(
            src_ref=arr.at[back // 2, back % 2, source, :, pl.ds(0, PCOLS)],
            dst_ref=retp.at[back, source],
            send_sem=r_send.at[source, back],
            recv_sem=r_recv.at[source, back],
            device_id=(back, s),
            device_id_type=MESH,
        )

    first_blocks = [(2, 2), (2, 1), (2, -1), (1, 2), (-1, 2)]
    middle_blocks = [(2, 0), (0, 2)]
    corner_blocks = [(1, 1), (1, -1), (-1, 1), (-1, -1)]
    near_blocks = [(1, 0), (-1, 0), (0, 1), (0, -1)]

    def experts(step, carry):
        group = (z + 1 + step) % depths
        sources = arr[group]
        width = sources.shape[-1]
        wide = sources.reshape(2 * SEQ, ROWS, width).astype(F32)
        results = []
        for e in range(2):
            mine = wide[:, e * CAP : (e + 1) * CAP, :].reshape(2 * SEQ * CAP, width).astype(BF16)
            pair = mm(mine, win[e])
            inner_width = wout.shape[1]
            gate = pair[:, :inner_width]
            inner = (gate / (1.0 + jnp.exp(-gate)) * pair[:, inner_width:]).astype(BF16)
            results.append(mm(inner, wout[e]).reshape(2 * SEQ, CAP, width))
        result = jnp.concatenate(results, axis=1).astype(BF16)
        arr[group] = result.reshape(sources.shape)
        for dx, dy in first_blocks:
            for core in (0, 1):
                there = group * 2 + core

                @pl.when(there != p)
                def _():
                    r_copy(ring_spot(s, 1, dx, dy), there).start()

        return carry

    lax.fori_loop(0, depths, experts, 0)

    def rq_copy(there):
        return pltpu.make_async_remote_copy(
            src_ref=arr.at[:, there // SEQ, there % SEQ, :, pl.ds(PCOLS, QCOLS)],
            dst_ref=retq.at[here],
            send_sem=rq_send.at[there],
            recv_sem=rq_recv.at[here],
            device_id=(2 * z + there // SEQ, there % SEQ),
            device_id_type=MESH,
        )

    def rq_go(step, carry):
        rq_copy((here + step) % (2 * SEQ)).start()
        return carry

    lax.fori_loop(1, 2 * SEQ, rq_go, 0)
    for dx, dy in middle_blocks + corner_blocks + near_blocks + [(0, 0)]:

        def r_go(step, carry):
            r_copy(ring_spot(s, 1, dx, dy), (p + step) % 8).start()
            return carry

        lax.fori_loop(1, 8, r_go, 0)
    retp[p] = arr[z, c, :, :, 0:PCOLS]
    retq[here] = arr[:, c, s, :, PCOLS:]

    def weigh(blocks):
        for dx, dy in blocks:
            source = ring_spot(s, 1, dx, dy)

            def r_wait(step, carry):
                r_copy_from(source, (p + step) % 8).wait_recv()
                return carry

            lax.fori_loop(1, 8, r_wait, 0)
            found = retp[:, source].reshape(8 * ROWS, PCOLS)
            ptok[source] = mm(mix(p_slots, pmeta[source]), found).astype(BF16)

    sums = []

    def pass_sum(half, piece, room, tf, tg, slot):
        copy = pltpu.make_async_remote_copy(
            src_ref=piece,
            dst_ref=room,
            send_sem=rs_send.at[half, slot],
            recv_sem=rs_recv.at[half, slot],
            device_id=(p, ring_spot(s, half, tf, tg)),
            device_id_type=MESH,
        )
        copy.start()
        sums.append(copy)

    def take(half, room, slot):
        pltpu.make_async_remote_copy(
            src_ref=room,
            dst_ref=room,
            send_sem=rs_send.at[half, slot],
            recv_sem=rs_recv.at[half, slot],
            device_id=(p, ring_spot(s, half, 1, 0)),
            device_id_type=MESH,
        ).wait_recv()
        return room[...].astype(F32)

    def block(half, df, dg, span=FULL):
        return at(half, ring_spot(s, half, df, dg), *span)

    def add_to(ref, *terms):
        total = ref[...].astype(F32)
        for term in terms:
            total = total + term
        ref[...] = total.astype(BF16)

    def far_sums(half, df):
        slot = 2 * (df % RING)
        pass_sum(half, block(half, df, 2, LOW), rs_a.at[half, df % RING, 0], 0, 1, slot)
        pass_sum(half, block(half, df, 2, HIGH), rs_a.at[half, df % RING, 1], 0, -1, slot + 1)

    def near_sums(half, df):
        k = df % RING
        add_to(block(half, df, 1, LOW), take(half, rs_a.at[half, k, 0], 2 * k))
        add_to(block(half, df, -1, HIGH), take(half, rs_a.at[half, k, 1], 2 * k + 1))
        pass_sum(half, block(half, df, 1), rs_b.at[half, k, 0], 0, 1, 8 + 2 * k)
        pass_sum(half, block(half, df, -1), rs_b.at[half, k, 1], 0, -1, 9 + 2 * k)

    def line_sum(half, df):
        k = df % RING
        add_to(
            block(half, df, 0),
            take(half, rs_b.at[half, k, 0], 8 + 2 * k),
            take(half, rs_b.at[half, k, 1], 9 + 2 * k),
        )

    def far_line(half):
        pass_sum(half, block(half, 2, 0, LOW), rs_c.at[half, 0], 1, 0, 16)
        pass_sum(half, block(half, 2, 0, HIGH), rs_c.at[half, 1], -1, 0, 17)

    def near_line(half):
        add_to(block(half, 1, 0, LOW), take(half, rs_c.at[half, 0], 16))
        add_to(block(half, -1, 0, HIGH), take(half, rs_c.at[half, 1], 17))
        pass_sum(half, block(half, 1, 0), rs_d.at[half, 0], 1, 0, 18)
        pass_sum(half, block(half, -1, 0), rs_d.at[half, 1], -1, 0, 19)

    weigh(first_blocks)
    for half in (0, 1):
        for df in (2, 1, -1):
            far_sums(half, df)
    weigh(middle_blocks)
    for half in (0, 1):
        far_sums(half, 0)
        near_sums(half, 2)
    weigh(corner_blocks)
    for half in (0, 1):
        near_sums(half, 1)
        near_sums(half, -1)
        line_sum(half, 2)
        far_line(half)
    weigh(near_blocks)
    for half in (0, 1):
        near_sums(half, 0)
        line_sum(half, 1)
        line_sum(half, -1)
        near_line(half)

    def rq_wait(step, carry):
        back = (here + step) % (2 * SEQ)
        pltpu.make_async_remote_copy(
            src_ref=arr.at[:, back // SEQ, back % SEQ, :, pl.ds(PCOLS, QCOLS)],
            dst_ref=retq.at[back],
            send_sem=rq_send.at[back],
            recv_sem=rq_recv.at[back],
            device_id=(2 * z + back // SEQ, back % SEQ),
            device_id_type=MESH,
        ).wait()
        return carry

    lax.fori_loop(1, 2 * SEQ, rq_wait, 0)
    q_rows = lax.broadcasted_iota(jnp.int32, (2 * SEQ * ROWS, 128), 0)
    q_slots = (z * (2 * SEQ * ROWS) + q_rows).astype(F32)

    def q_weigh(source):
        found = retq[:, source].reshape(2 * SEQ * ROWS, QCOLS)
        qtok[source] = mm(mix(q_slots, qmeta[source]), found).astype(BF16)

    def q_sum(step):
        there = (z + step) % depths
        return pltpu.make_async_remote_copy(
            src_ref=qtok.at[there],
            dst_ref=rs_q.at[z],
            send_sem=rsq_send.at[there],
            recv_sem=rsq_recv.at[z],
            device_id=(depth(step), s),
            device_id_type=MESH,
        )

    for step in (2, 1, 3):
        q_weigh((z + step) % depths)
        q_sum(step).start()
    q_weigh(z)
    weigh([(0, 0)])
    q_total = qtok[z].astype(F32)
    for step in (1, 2, 3):
        source = (z + step) % depths
        pltpu.make_async_remote_copy(
            src_ref=qtok.at[source],
            dst_ref=rs_q.at[source],
            send_sem=rsq_send.at[source],
            recv_sem=rsq_recv.at[source],
            device_id=(depth(step), s),
            device_id_type=MESH,
        ).wait()
        q_total = q_total + rs_q[source].astype(F32)
    out_ref[:, PCOLS:] = q_total.astype(BF16)
    for half in (0, 1):
        line_sum(half, 0)
        total = block(half, 0, 0)[...].astype(F32)
        total = total + take(half, rs_d.at[half, 0], 18) + take(half, rs_d.at[half, 1], 19)
        out_ref[:, half * (PCOLS // 2) : (half + 1) * (PCOLS // 2)] = total.astype(BF16)
    for copy in sums:
        copy.wait_send()

    def r_done(step, carry):
        source, back = step // 8, step % 8

        @pl.when(back != p)
        def _():
            r_copy(source, back).wait_send()

        return carry

    lax.fori_loop(0, 8 * SEQ, r_done, 0)

    def meta_wait(step, carry):
        plane_meta(step).wait_send()
        return carry

    lax.fori_loop(1, SEQ, meta_wait, 0)
    for step in (1, 2, 3):
        depth_meta(step).wait_send()


def run_experts(own, meta, w_in, w_out):
    rows, width = own.shape
    vmem = pl.BlockSpec(memory_space=pltpu.VMEM)
    hbm = pl.BlockSpec(memory_space=pl.ANY)
    dma = pltpu.SemaphoreType.DMA
    return pl.pallas_call(
        expert_kernel,
        in_specs=[vmem, vmem, hbm, hbm],
        out_specs=vmem,
        out_shape=jax.ShapeDtypeStruct((rows, width), BF16),
        scratch_shapes=[
            pltpu.VMEM((SEQ, rows, PCOLS), BF16),
            pltpu.VMEM((4, rows, QCOLS), BF16),
            pltpu.VMEM((SEQ, 32, rows), F32),
            pltpu.VMEM((4, 32, rows), F32),
            pltpu.VMEM((SEQ, 8, ROWS, PCOLS), BF16),
            pltpu.VMEM((4, 2 * SEQ, ROWS, QCOLS), BF16),
            pltpu.VMEM((4, 2, SEQ, ROWS, width), BF16),
            pltpu.VMEM(w_in.shape, BF16),
            pltpu.VMEM(w_out.shape, BF16),
            dma((2, 32)),
            dma((2, 32)),
            dma((4,)),
            dma((4,)),
            dma((SEQ + 4,)),
            dma((SEQ + 4,)),
            dma((SEQ, 8)),
            dma((8, SEQ)),
            dma((2 * SEQ,)),
            dma((2, SEQ)),
            dma((2,)),
            pltpu.VMEM((8, SEQ, ROWS, PCOLS), BF16),
            pltpu.VMEM((2 * SEQ, 4, ROWS, QCOLS), BF16),
            pltpu.VMEM((2, RING, 2, 64, PCOLS // 2), BF16),
            pltpu.VMEM((2, RING, 2, 128, PCOLS // 2), BF16),
            pltpu.VMEM((2, 2, 64, PCOLS // 2), BF16),
            pltpu.VMEM((2, 2, 128, PCOLS // 2), BF16),
            pltpu.VMEM((4, 128, QCOLS), BF16),
            dma((SEQ, 8)),
            dma((SEQ, 8)),
            dma((2 * SEQ,)),
            dma((2 * SEQ,)),
            dma((2, 20)),
            dma((2, 20)),
            dma((4,)),
            dma((4,)),
        ],
        compiler_params=pltpu.CompilerParams(
            collective_id=1, has_side_effects=True, vmem_limit_bytes=62 * 2**20
        ),
    )(own, meta, w_in, w_out)


def rms_scale(values, gain):
    mean = jnp.mean(values * values, axis=-1, keepdims=True)
    return values * lax.rsqrt(mean + EPS) * gain


def routing(chosen_ids, logits):
    tokens, experts = logits.shape
    table = lax.broadcasted_iota(jnp.int32, (1, 1, experts), 2)
    match = chosen_ids[:, :, None] == table
    member = jnp.any(match, axis=1)
    rows = lax.broadcasted_iota(jnp.int32, (tokens, tokens), 0)
    cols = lax.broadcasted_iota(jnp.int32, (tokens, tokens), 1)
    earlier = (rows > cols).astype(BF16)
    before = jnp.dot(earlier, member.astype(BF16), preferred_element_type=F32)
    place = jnp.sum(jnp.where(match, before[:, None, :], 0.0), axis=-1)
    picked = jnp.sum(jnp.where(match, logits[:, None, :], 0.0), axis=-1)
    return chosen_ids.astype(F32) * CAP + place, picked


def shards(
    tokens,
    span_lengths,
    state_slots,
    expert_ids,
    state_pool,
    attn_gain,
    w_query,
    w_key,
    w_value,
    w_zgate,
    w_heads,
    decay_rate,
    head_gain,
    w_output,
    moe_gain,
    router,
    w_expert_in,
    w_expert_out,
):
    local_rows, width = tokens.shape[1:]
    length = span_lengths[0]
    own_rows = tokens[0]
    normed = rms_scale(own_rows.astype(F32), attn_gain).astype(BF16)
    head_weights = jnp.pad(w_heads.reshape(width, 4), ((0, 0), (0, 124)))
    weights_all = jnp.concatenate([w_query, w_key, w_value, w_zgate, head_weights], axis=1)
    first = lax.dynamic_index_in_dim(state_pool, state_slots[0], 0, keepdims=False)
    rate = jnp.pad(decay_rate, (0, 126)).reshape(1, 128)
    summed, final = attention(
        span_lengths, normed, w_output, weights_all, rate, head_gain.reshape(1, 128), first
    )
    own_positions = lax.axis_index("seq") * local_rows + lax.broadcasted_iota(jnp.int32, (local_rows, 1), 0)
    own_live = (own_positions < length).astype(F32)
    attended = (summed * own_live).astype(BF16)
    residual = own_rows.astype(F32) + attended.astype(F32)
    moe_input = rms_scale(residual, moe_gain).astype(BF16)
    logits = jnp.dot(moe_input, router, preferred_element_type=F32)
    slots, picked = routing(expert_ids[0], logits)
    weights = jax.nn.softmax(picked, axis=-1) * own_live
    meta = jnp.concatenate(
        [
            jnp.pad(slots.T, ((0, 16 - TOP), (0, 0)), constant_values=-1.0),
            jnp.pad(weights.T, ((0, 16 - TOP), (0, 0))),
        ],
        axis=0,
    )
    expert_out = run_experts(moe_input, meta, w_expert_in, w_expert_out)
    return (attended[None], expert_out[None], final[None])


def solution(mesh):
    return jax.shard_map(
        shards,
        mesh=mesh,
        in_specs=(
            P("prompt", "seq", None),
            P("prompt"),
            P("prompt"),
            P("prompt", "seq", None),
            P(None, "seq", None, None),
            P(),
            P(None, "seq"),
            P(None, "seq"),
            P(None, "seq"),
            P(None, "seq"),
            P(None, None, "seq"),
            P("seq"),
            P(),
            P("seq", None),
            P(),
            P(),
            P(("prompt", "seq"), None, None),
            P(("prompt", "seq"), None, None),
        ),
        out_specs=(
            P("prompt", "seq", None),
            P("prompt", "seq", None),
            P("prompt", "seq", None, None),
        ),
        check_vma=False,
    )
```

```python
import functools
import jax
import jax.numpy as jnp
from jax import lax
from jax.experimental import pallas as pl
from jax.experimental.pallas import tpu as pltpu
from jax.sharding import PartitionSpec as P

EPS = 1e-06
CH = 128
RING = 4
SEQ = RING * RING
HEADS = 2
F32 = jnp.float32
BF16 = jnp.bfloat16
MESH = pl.DeviceIdType.MESH


def mm(a, b):
    return jnp.dot(a, b, preferred_element_type=F32)


def halves(a):
    high = a.astype(BF16)
    return high, (a - high.astype(F32)).astype(BF16)


def mm3(a, b):
    a_high, a_low = halves(a)
    b_high, b_low = halves(b)
    wide = mm(jnp.concatenate([a_high, a_low], axis=1), jnp.concatenate([b_high, b_high], axis=0))
    return wide + mm(a_high, b_low)


def unit_lower_inverse(lows, rows, cols):
    eye = jnp.where(rows == cols, 1.0, 0.0)
    inverses = [eye - jnp.where(rows // 2 == cols // 2, low, 0.0) for low in lows]
    size = 2
    while size < CH:
        mask = (rows // (2 * size) == cols // (2 * size)) & (rows // size != cols // size)
        inner = [mm3(jnp.where(mask, low, 0.0), inv) for low, inv in zip(lows, inverses)]
        inverses = [inv - mm3(inv, part) for inv, part in zip(inverses, inner)]
        size *= 2
    return inverses


def prepare(blocks, length, tok, w_ref, rate, gain, store):
    left_ref, kt_ref, attn_ref, upd_ref, last_ref, gate_ref = store
    rows = lax.broadcasted_iota(jnp.int32, (CH, CH), 0)
    cols = lax.broadcasted_iota(jnp.int32, (CH, CH), 1)
    tri = jnp.where(rows >= cols, 1.0, 0.0)
    proj_all = mm(jnp.concatenate([tok[b] for b in blocks], axis=0), w_ref[...])
    lows = []
    rights = []
    for n, block in enumerate(blocks):
        part = proj_all[n * CH : (n + 1) * CH]
        q, k = part[:, 0:128], part[:, 128:256]
        q = q * (lax.rsqrt(jnp.sum(q * q, axis=-1, keepdims=True) + EPS) * 128 ** (-0.5))
        k = k * lax.rsqrt(jnp.sum(k * k, axis=-1, keepdims=True) + EPS)
        logits = part[:, 768:896]
        live = jnp.where(block * CH + rows < length, 1.0, 0.0)
        softplus = jnp.maximum(logits, 0.0) + jnp.log1p(jnp.exp(-jnp.abs(logits)))
        logdec = -rate * softplus * live
        beta2 = live / (1.0 + jnp.exp(-logits))
        cumul = jnp.dot(tri, logdec, preferred_element_type=F32, precision=lax.Precision.HIGHEST)
        cumul_t = cumul.T
        both = mm(jnp.concatenate([k.astype(BF16), q.astype(BF16)], axis=0), k.T.astype(BF16))
        kk, qk = both[:CH], both[CH:]
        for h in range(HEADS):
            g = cumul[:, h : h + 1]
            decay = jnp.exp(jnp.minimum(g - cumul_t[h : h + 1, :], 0.0))
            beta = beta2[:, 2 + h : 3 + h]
            lows.append(jnp.where(rows > cols, beta * kk * decay, 0.0))
            attn_ref[block, h] = jnp.where(rows >= cols, qk * decay, 0.0).astype(BF16)
            start = jnp.exp(g)
            value = part[:, 256 + 128 * h : 384 + 128 * h]
            rights.append(jnp.concatenate([beta * value, (beta * start) * k], axis=1).astype(BF16))
            last = cumul[CH - 1 : CH, h : h + 1]
            left_ref[block, h, CH:, :] = (start * q).astype(BF16)
            kt_ref[block, h] = (jnp.exp(last - g) * k).T.astype(BF16)
            last_ref[block, h] = jnp.broadcast_to(jnp.exp(last), (8, CH))
            z = part[:, 512 + 128 * h : 640 + 128 * h]
            gate_ref[block, h] = gain * (z / (1.0 + jnp.exp(-z)))
    for n, inverse in enumerate(unit_lower_inverse(lows, rows, cols)):
        block, h = blocks[n // HEADS], n % HEADS
        high, low = halves(inverse)
        got = mm(jnp.concatenate([high, low], axis=1), jnp.concatenate([rights[n], rights[n]], axis=0))
        upd_ref[block, h] = got[:, :CH]
        left_ref[block, h, :CH, :] = got[:, CH:].astype(BF16)


def advance(block, state_ref, store):
    left_ref, kt_ref, attn_ref, upd_ref, last_ref, gate_ref = store
    outs = []
    for h in range(HEADS):
        state = state_ref[h]
        left = left_ref[block, h]
        high, low = halves(state)
        got = mm(jnp.concatenate([left, left], axis=1), jnp.concatenate([high, low], axis=0))
        corrected = upd_ref[block, h] - got[:CH]
        high, low = halves(corrected)
        kt = kt_ref[block, h]
        state_ref[h] = last_ref[block, h, 0:1, :] * state + mm(
            jnp.concatenate([kt, kt], axis=1), jnp.concatenate([high, low], axis=0)
        )
        out = got[CH:] + mm(attn_ref[block, h], high)
        scale = lax.rsqrt(jnp.mean(out * out, axis=-1, keepdims=True) + EPS)
        outs.append((out * scale * gate_ref[block, h]).astype(BF16))
    return jnp.concatenate(outs, axis=1)


def ring_spot(s, half, df, dg):
    dx, dy = (dg, df) if half == 0 else (df, dg)
    x, y = s // RING, s % RING
    return ((x + dx + 2 * RING) % RING) * RING + (y + dy + 2 * RING) % RING


FULL, LOW, HIGH = (0, 128), (0, 64), (64, 64)


class Rings:
    def __init__(self, p, s, at, send_sem, recv_sem, hook=None):
        self.p, self.s, self.at = p, s, at
        self.send_sem, self.recv_sem = send_sem, recv_sem
        self.hook = hook or (lambda half, df, dg: None)
        self.started = []

    def copy(self, half, df, dg, span, tf, tg):
        slot = ((df - tf) % RING * RING + (dg - tg) % RING) * 2 + (1 if span is HIGH else 0)
        piece = self.at(half, ring_spot(self.s, half, df, dg), *span)
        return pltpu.make_async_remote_copy(
            src_ref=piece,
            dst_ref=piece,
            send_sem=self.send_sem.at[half, slot],
            recv_sem=self.recv_sem.at[half, slot],
            device_id=(self.p, ring_spot(self.s, half, tf, tg)),
            device_id_type=MESH,
        )

    def send(self, *args):
        copy = self.copy(*args)
        copy.start()
        self.started.append(copy)

    def arrive(self, half, df, dg, span=FULL):
        slot = (df % RING * RING + dg % RING) * 2 + (1 if span is HIGH else 0)
        piece = self.at(half, ring_spot(self.s, half, df, dg), *span)
        pltpu.make_async_remote_copy(
            src_ref=piece,
            dst_ref=piece,
            send_sem=self.send_sem.at[half, slot],
            recv_sem=self.recv_sem.at[half, slot],
            device_id=(self.p, ring_spot(self.s, half, 1, 0)),
            device_id_type=MESH,
        ).wait_recv()

    def begin(self):
        for half in (0, 1):
            for step in (1, -1):
                self.send(half, 0, 0, FULL, step, 0)
        for half in (0, 1):
            for step in (1, -1):
                self.send(half, 0, 0, FULL, 0, step)

    def first_near(self):
        for half in (0, 1):
            for df, span in ((-1, LOW), (1, HIGH)):
                self.arrive(half, df, 0)
                self.send(half, df, 0, span, -df, 0)
            self.hook(half, -1, 0)
            self.hook(half, 1, 0)

    def second_near(self):
        for half in (0, 1):
            for dg, span in ((-1, LOW), (1, HIGH)):
                self.arrive(half, 0, dg)
                self.send(half, 0, dg, span, 0, -dg)
            self.hook(half, 0, -1)
            self.hook(half, 0, 1)
            for df in (-1, 1):
                for step in (1, -1):
                    self.send(half, df, 0, FULL, 0, step)

    def near(self):
        self.first_near()
        self.second_near()

    def far(self):
        for half in (0, 1):
            self.arrive(half, 2, 0, LOW)
            self.arrive(half, 2, 0, HIGH)
            for step in (1, -1):
                self.send(half, 2, 0, FULL, 0, step)
            self.hook(half, 2, 0)
        self.second_far((0,))

    def second_far(self, dfs):
        for half in (0, 1):
            for df in dfs:
                self.arrive(half, df, 2, LOW)
                self.arrive(half, df, 2, HIGH)
                self.hook(half, df, 2)

    def corners(self, dfs=(-1, 1)):
        for half in (0, 1):
            for df in dfs:
                for dg, span in ((-1, LOW), (1, HIGH)):
                    self.arrive(half, df, dg)
                    self.send(half, df, dg, span, 0, -dg)
                    self.hook(half, df, dg)

    def far_corners(self):
        self.corners((2,))

    def last(self):
        self.second_far((-1, 1, 2))


def attention_kernel(
    length_ref,
    rate_ref,
    own_ref,
    norm_ref,
    wo_ref,
    heads_ref,
    gain_ref,
    first_ref,
    query_hbm,
    key_hbm,
    value_hbm,
    zgate_hbm,
    out_ref,
    final_ref,
    w_ref,
    load_sem,
    tok,
    wall,
    got,
    gout,
    left_ref,
    kt_ref,
    attn_ref,
    upd_ref,
    last_ref,
    gate_ref,
    state_ref,
    ring_send,
    ring_recv,
    z_send,
    z_recv,
    mate_send,
    mate_recv,
    got_send,
    got_recv,
):
    store = (left_ref, kt_ref, attn_ref, upd_ref, last_ref, gate_ref)
    p = lax.axis_index("prompt")
    s = lax.axis_index("seq")
    z, c = p // 2, p % 2
    x, y = s // RING, s % RING
    parity = z % 2
    length = length_ref[0]
    tcols = tok.shape[2] // 2

    def spot(half, df, dg):
        return ring_spot(s, half, df, dg)

    def depth(step):
        return ((z + step + RING) % RING) * 2 + c

    mate = z * 2 + (1 - c)

    def at(chan, half, owner, first, count, side=None, par=None):
        if chan == 0:
            return tok.at[owner, pl.ds(first, count), pl.ds(half * tcols, tcols)]
        row = pl.multiple_of(owner * 256 + half * 128 + first, 64)
        return wall.at[c if side is None else side, parity if par is None else par, pl.ds(row, count), :]

    started = []
    passed = []

    def hand_on(half, df, dg):
        owner = spot(half, df, dg)
        slot = (df % RING) * RING + dg % RING
        piece = at(1, half, owner, *FULL)
        copy = pltpu.make_async_remote_copy(
            src_ref=piece,
            dst_ref=piece,
            send_sem=z_send.at[half, slot],
            recv_sem=z_recv.at[half, slot],
            device_id=(depth(1 if half == 0 else -1), s),
            device_id_type=MESH,
        )
        copy.start()
        started.append(copy)
        copy = to_mate(half, df, dg, parity, 0)
        copy.start()
        started.append(copy)
        passed.append((half, df, dg))

    def to_mate(half, df, dg, par, kind):
        slot = (df % RING) * RING + dg % RING
        piece = at(1, half, spot(half, df, dg), *FULL, par=par)
        return pltpu.make_async_remote_copy(
            src_ref=piece,
            dst_ref=piece,
            send_sem=mate_send.at[kind, half, slot],
            recv_sem=mate_recv.at[kind, half, slot],
            device_id=(mate, s),
            device_id_type=MESH,
        )

    def from_z(half, df, dg):
        owner = spot(half, df, dg)
        slot = (df % RING) * RING + dg % RING
        piece = at(1, half, owner, *FULL, par=1 - parity)
        pltpu.make_async_remote_copy(
            src_ref=piece,
            dst_ref=piece,
            send_sem=z_send.at[half, slot],
            recv_sem=z_recv.at[half, slot],
            device_id=(depth(1), s),
            device_id_type=MESH,
        ).wait_recv()
        copy = to_mate(half, df, dg, 1 - parity, 1)
        copy.start()
        started.append(copy)

    def from_mate(half, df, dg):
        slot = (df % RING) * RING + dg % RING
        for kind in (0, 1):
            piece = at(1, half, spot(half, df, dg), *FULL, side=1 - c, par=parity if kind == 0 else 1 - parity)
            pltpu.make_async_remote_copy(
                src_ref=piece,
                dst_ref=piece,
                send_sem=mate_send.at[kind, half, slot],
                recv_sem=mate_recv.at[kind, half, slot],
                device_id=(mate, s),
                device_id_type=MESH,
            ).wait_recv()

    tokens = Rings(p, s, functools.partial(at, 0), ring_send.at[0], ring_recv.at[0])
    others = Rings(p, s, functools.partial(at, 1), ring_send.at[1], ring_recv.at[1], hand_on)

    def block_of(dx, dy):
        return spot(1, dx, dy)

    def compute(offsets):
        prepare(
            [block_of(*offset) for offset in offsets], length, tok, w_ref, rate, gain_ref[...], store
        )

    loads = []
    column = 0
    for number, source in enumerate((query_hbm, key_hbm, value_hbm, zgate_hbm)):
        count = source.shape[1]
        loads.append(
            pltpu.make_async_copy(source, w_ref.at[:, pl.ds(column, count)], load_sem.at[number])
        )
        loads[-1].start()
        column += count
    barrier = pltpu.get_barrier_semaphore()

    def greet(step, carry):
        pl.semaphore_signal(barrier, 1, device_id=(p, (s + step) % SEQ), device_id_type=MESH)
        return carry

    lax.fori_loop(1, SEQ, greet, 0)
    for other in (mate, depth(1), depth(-1)):
        pl.semaphore_signal(barrier, 1, device_id=(other, s), device_id_type=MESH)
    own = own_ref[...].astype(F32)
    own_scale = lax.rsqrt(jnp.mean(own * own, axis=-1, keepdims=True) + EPS)
    tok[s] = (own * own_scale * norm_ref[...]).astype(BF16)
    w_ref[:, column:] = heads_ref[...]
    lane = lax.broadcasted_iota(jnp.int32, (1, 128), 1)
    rate = jnp.where(lane == 0, rate_ref[0], jnp.where(lane == 1, rate_ref[1], 0.0))
    for side in (0, 1):
        for par in (0, 1):
            first = (2 * side + par) * 512
            wall[side, par, pl.ds(pl.multiple_of(s * 256, 256), 256), :] = wo_ref[:, first : first + 512]
    for h in range(HEADS):
        state_ref[h] = first_ref[h].T
    pl.semaphore_wait(barrier, SEQ + 2)

    tokens.begin()
    others.begin()
    for load in loads:
        load.wait()
    compute([(0, 0)])
    tokens.near()
    others.near()
    compute([(0, 1), (0, -1), (1, 0), (-1, 0)])
    tokens.far()
    others.far()
    compute([(0, 2), (2, 0)])
    tokens.corners()
    others.corners()
    compute([(1, 1), (1, -1), (-1, 1), (-1, -1)])
    tokens.far_corners()
    others.far_corners()
    tokens.last()
    compute([(1, 2), (-1, 2), (2, 1), (2, -1), (2, 2)])
    others.last()

    def give(index):
        here = gout.at[index]
        there = got.at[:, pl.ds(pl.multiple_of(s * 256, 256), 256)]
        return pltpu.make_async_remote_copy(
            src_ref=here,
            dst_ref=there,
            send_sem=got_send.at[index],
            recv_sem=got_recv.at[s],
            device_id=(p, index),
            device_id_type=MESH,
        )

    def scan(index, carry):
        gated = advance(index, state_ref, store)

        @pl.when(index != s)
        def _():
            gout[index] = gated
            give(index).start()

        @pl.when(index == s)
        def _():
            got[:, pl.ds(pl.multiple_of(s * 256, 256), 256)] = gated

        return carry

    lax.fori_loop(0, 8, scan, 0)
    for item in passed[:16]:
        from_z(*item)
    lax.fori_loop(8, SEQ, scan, 0)
    for h in range(HEADS):
        final_ref[h] = state_ref[h].T
    for item in passed[16:]:
        from_z(*item)

    def receive(step, carry):
        source = (s + step) % SEQ
        there = got.at[:, pl.ds(pl.multiple_of(source * 256, 256), 256)]
        pltpu.make_async_remote_copy(
            src_ref=gout.at[source],
            dst_ref=there,
            send_sem=got_send.at[source],
            recv_sem=got_recv.at[source],
            device_id=(p, source),
            device_id_type=MESH,
        ).wait()
        return carry

    lax.fori_loop(1, SEQ, receive, 0)
    for item in passed:
        from_mate(*item)
    for copy in started + tokens.started + others.started:
        copy.wait_send()
    for side in (0, 1):
        for par in (0, 1):
            first = (2 * side + par) * 512
            out_ref[:, first : first + 512] = mm(got[...], wall[side, par])


def attention(length, rate, own, norm_gain, w_output, head_weights, gain, first, projections):
    rows, width = own.shape
    columns = sum(weight.shape[1] for weight in projections) + head_weights.shape[1]
    smem = pl.BlockSpec(memory_space=pltpu.SMEM)
    vmem = pl.BlockSpec(memory_space=pltpu.VMEM)
    dma = pltpu.SemaphoreType.DMA
    return pl.pallas_call(
        attention_kernel,
        in_specs=[smem, smem] + [vmem] * 6 + [pl.BlockSpec(memory_space=pl.ANY)] * len(projections),
        out_specs=[vmem, vmem],
        out_shape=[
            jax.ShapeDtypeStruct((rows, width), F32),
            jax.ShapeDtypeStruct((HEADS, 128, 128), F32),
        ],
        scratch_shapes=[
            pltpu.VMEM((width, columns), BF16),
            dma((4,)),
            pltpu.VMEM((SEQ, rows, width), BF16),
            pltpu.VMEM((2, 2, SEQ * 256, 512), BF16),
            pltpu.VMEM((rows, SEQ * 256), BF16),
            pltpu.VMEM((SEQ, rows, 256), BF16),
            pltpu.VMEM((SEQ, HEADS, 2 * CH, 128), BF16),
            pltpu.VMEM((SEQ, HEADS, 128, CH), BF16),
            pltpu.VMEM((SEQ, HEADS, CH, CH), BF16),
            pltpu.VMEM((SEQ, HEADS, CH, 128), F32),
            pltpu.VMEM((SEQ, HEADS, 8, CH), F32),
            pltpu.VMEM((SEQ, HEADS, CH, 128), F32),
            pltpu.VMEM((HEADS, 128, 128), F32),
            dma((2, 2, 32)),
            dma((2, 2, 32)),
            dma((2, 16)),
            dma((2, 16)),
            dma((2, 2, 16)),
            dma((2, 2, 16)),
            dma((SEQ,)),
            dma((SEQ,)),
        ],
        compiler_params=pltpu.CompilerParams(
            collective_id=0, has_side_effects=True, vmem_limit_bytes=56 * 2**20
        ),
    )(length, rate, own, norm_gain, w_output, head_weights, gain, first, *projections)


CAP = 8
ROWS = 2 * CAP
TOP = 10
PCOLS = 1280
QCOLS = 768


def select(slots, meta):
    hit = slots == meta[0:1, :]
    for j in range(1, TOP):
        hit = hit | (slots == meta[j : j + 1, :])
    return jnp.where(hit, 1.0, 0.0).astype(BF16)


def mix(slots, meta):
    share = jnp.where(slots == meta[0:1, :], meta[16:17, :], 0.0)
    for j in range(1, TOP):
        share = share + jnp.where(slots == meta[j : j + 1, :], meta[16 + j : 17 + j, :], 0.0)
    return share.T.astype(BF16)


def expert_kernel(
    own_ref,
    meta_ref,
    win_hbm,
    wout_hbm,
    out_ref,
    ptok,
    qtok,
    pmeta,
    qmeta,
    pout,
    qout,
    arr,
    win,
    wout,
    ring_send,
    ring_recv,
    z_send,
    z_recv,
    meta_send,
    meta_recv,
    p_send,
    p_recv,
    q_send,
    q_recv,
    local_sem,
    retp,
    retq,
    rs_a,
    rs_b,
    rs_c,
    rs_d,
    rs_q,
    r_send,
    r_recv,
    rq_send,
    rq_recv,
    rs_send,
    rs_recv,
    rsq_send,
    rsq_recv,
):
    p = lax.axis_index("prompt")
    s = lax.axis_index("seq")
    z, c = p // 2, p % 2
    depths = 4

    def depth(step):
        return ((z + step + depths) % depths) * 2 + c

    loads = [
        pltpu.make_async_copy(win_hbm, win, local_sem.at[0]),
        pltpu.make_async_copy(wout_hbm, wout, local_sem.at[1]),
    ]
    for load in loads:
        load.start()
    barrier = pltpu.get_barrier_semaphore()

    def greet_plane(step, carry):
        for core in (0, 1):
            pl.semaphore_signal(
                barrier, 1, device_id=(2 * z + core, (s + step) % SEQ), device_id_type=MESH
            )
        return carry

    lax.fori_loop(1, SEQ, greet_plane, 0)

    def greet_column(step, carry):
        pl.semaphore_signal(barrier, 1, device_id=((p + step) % (2 * depths), s), device_id_type=MESH)
        return carry

    lax.fori_loop(1, 2 * depths, greet_column, 0)
    ptok[s] = own_ref[:, :PCOLS]
    qtok[z] = own_ref[:, PCOLS:]
    pmeta[s] = meta_ref[...]
    qmeta[z] = meta_ref[...]
    pl.semaphore_wait(barrier, 2 * (SEQ - 1) + 2 * depths - 1)

    def plane_meta(step):
        there = (s + step) % SEQ
        return pltpu.make_async_remote_copy(
            src_ref=meta_ref,
            dst_ref=pmeta.at[s],
            send_sem=meta_send.at[step],
            recv_sem=meta_recv.at[s],
            device_id=(p, there),
            device_id_type=MESH,
        )

    def plane_meta_from(step):
        source = (s + step) % SEQ
        return pltpu.make_async_remote_copy(
            src_ref=meta_ref,
            dst_ref=pmeta.at[source],
            send_sem=meta_send.at[step],
            recv_sem=meta_recv.at[source],
            device_id=(p, source),
            device_id_type=MESH,
        )

    def depth_meta(step):
        return pltpu.make_async_remote_copy(
            src_ref=meta_ref,
            dst_ref=qmeta.at[z],
            send_sem=meta_send.at[SEQ + step],
            recv_sem=meta_recv.at[SEQ + z],
            device_id=(depth(step), s),
            device_id_type=MESH,
        )

    def depth_meta_from(step):
        source = (z + step) % depths
        return pltpu.make_async_remote_copy(
            src_ref=meta_ref,
            dst_ref=qmeta.at[source],
            send_sem=meta_send.at[SEQ + step],
            recv_sem=meta_recv.at[SEQ + source],
            device_id=(depth(step), s),
            device_id_type=MESH,
        )

    def start_plane_meta(step, carry):
        plane_meta(step).start()
        return carry

    lax.fori_loop(1, SEQ, start_plane_meta, 0)
    for step in (1, 2, 3):
        depth_meta(step).start()

    def at(half, owner, first, count):
        return ptok.at[owner, pl.ds(first, count), pl.ds(half * (PCOLS // 2), PCOLS // 2)]

    rings = Rings(p, s, at, ring_send, ring_recv)

    def z_copy(source, span, step, slot):
        piece = qtok.at[source, pl.ds(*span), :]
        return pltpu.make_async_remote_copy(
            src_ref=piece,
            dst_ref=piece,
            send_sem=z_send.at[slot],
            recv_sem=z_recv.at[slot],
            device_id=(depth(step), s),
            device_id_type=MESH,
        )

    z_copies = [z_copy(z, FULL, 1, 0), z_copy(z, FULL, -1, 1)]
    for copy in z_copies:
        copy.start()
    rings.begin()

    rows = lax.broadcasted_iota(jnp.int32, (8 * ROWS, 128), 0)
    p_slots = ((rows // ROWS) * (SEQ * ROWS) + s * ROWS + rows % ROWS).astype(F32)

    def p_copy(source, there):
        return pltpu.make_async_remote_copy(
            src_ref=pout.at[source, there],
            dst_ref=arr.at[z, c, source, :, pl.ds(0, PCOLS)],
            send_sem=p_send.at[source, there],
            recv_sem=p_recv.at[p, source],
            device_id=(there, s),
            device_id_type=MESH,
        )

    def p_hand(source):
        picked = mm(select(p_slots, pmeta[source]), ptok[source]).astype(BF16)
        pout[source] = picked.reshape(8, ROWS, PCOLS)

        def go(step, carry):
            p_copy(source, (p + step) % 8).start()
            return carry

        lax.fori_loop(1, 8, go, 0)
        arr[z, c, source, :, 0:PCOLS] = pout[source, p]

    def p_hands(offsets):
        for dx, dy in offsets:
            source = ring_spot(s, 1, dx, dy)
            pltpu.make_async_remote_copy(
                src_ref=meta_ref,
                dst_ref=pmeta.at[source],
                send_sem=meta_send.at[0],
                recv_sem=meta_recv.at[source],
                device_id=(p, source),
                device_id_type=MESH,
            ).wait_recv()
            p_hand(source)

    def q_copy(there):
        return pltpu.make_async_remote_copy(
            src_ref=qout.at[:, there],
            dst_ref=arr.at[:, c, s, :, pl.ds(PCOLS, QCOLS)],
            send_sem=q_send.at[there],
            recv_sem=q_recv.at[c, s],
            device_id=(2 * z + there // SEQ, there % SEQ),
            device_id_type=MESH,
        )

    def q_hand(source):
        slots = (z * (2 * SEQ * ROWS) + lax.broadcasted_iota(jnp.int32, (2 * SEQ * ROWS, 128), 0)).astype(F32)
        picked = mm(select(slots, qmeta[source]), qtok[source]).astype(BF16)
        qout[source] = picked.reshape(2 * SEQ, ROWS, QCOLS)

    p_hand(s)
    q_hand(z)
    z_copy((z + 3) % depths, FULL, 1, 0).wait_recv()
    z_copy((z + 1) % depths, FULL, -1, 1).wait_recv()
    z_copies.append(z_copy((z + 3) % depths, LOW, 1, 2))
    z_copies.append(z_copy((z + 1) % depths, HIGH, -1, 3))
    z_copies[2].start()
    z_copies[3].start()
    for step in (1, 3):
        depth_meta_from(step).wait_recv()
        q_hand((z + step) % depths)
    rings.near()
    p_hands([(0, 1), (0, -1), (1, 0), (-1, 0)])
    depth_meta_from(2).wait_recv()
    z_copy((z + 2) % depths, LOW, 1, 2).wait_recv()
    z_copy((z + 2) % depths, HIGH, -1, 3).wait_recv()
    q_hand((z + 2) % depths)
    here = c * SEQ + s

    def q_go(step, carry):
        q_copy((here + step) % (2 * SEQ)).start()
        return carry

    rings.far()
    p_hands([(0, 2), (2, 0)])
    rings.corners()
    p_hands([(1, 1), (1, -1), (-1, 1), (-1, -1)])
    rings.far_corners()
    rings.last()
    lax.fori_loop(1, 2 * SEQ, q_go, 0)
    arr[:, c, s, :, PCOLS:] = qout[:, here]
    p_hands([(1, 2), (-1, 2), (2, 1), (2, -1), (2, 2)])

    def p_wait(step, carry):
        source, back = step // 8, step % 8

        @pl.when(back != p)
        def _():
            pltpu.make_async_remote_copy(
                src_ref=pout.at[source, back],
                dst_ref=arr.at[back // 2, back % 2, source, :, pl.ds(0, PCOLS)],
                send_sem=p_send.at[source, back],
                recv_sem=p_recv.at[back, source],
                device_id=(back, s),
                device_id_type=MESH,
            ).wait()

        return carry

    lax.fori_loop(0, 8 * SEQ, p_wait, 0)

    def q_wait(step, carry):
        back = (here + step) % (2 * SEQ)
        pltpu.make_async_remote_copy(
            src_ref=qout.at[:, back],
            dst_ref=arr.at[:, back // SEQ, back % SEQ, :, pl.ds(PCOLS, QCOLS)],
            send_sem=q_send.at[back],
            recv_sem=q_recv.at[back // SEQ, back % SEQ],
            device_id=(2 * z + back // SEQ, back % SEQ),
            device_id_type=MESH,
        ).wait()
        return carry

    lax.fori_loop(1, 2 * SEQ, q_wait, 0)
    for load in loads:
        load.wait()

    for copy in rings.started + z_copies:
        copy.wait_send()

    def r_copy(source, there):
        return pltpu.make_async_remote_copy(
            src_ref=arr.at[there // 2, there % 2, source, :, pl.ds(0, PCOLS)],
            dst_ref=retp.at[p, source],
            send_sem=r_send.at[source, there],
            recv_sem=r_recv.at[source, p],
            device_id=(there, s),
            device_id_type=MESH,
        )

    def r_copy_from(source, back):
        return pltpu.make_async_remote_copy(
            src_ref=arr.at[back // 2, back % 2, source, :, pl.ds(0, PCOLS)],
            dst_ref=retp.at[back, source],
            send_sem=r_send.at[source, back],
            recv_sem=r_recv.at[source, back],
            device_id=(back, s),
            device_id_type=MESH,
        )

    first_blocks = [(2, 2), (2, 1), (2, -1), (1, 2), (-1, 2)]
    middle_blocks = [(2, 0), (0, 2)]
    corner_blocks = [(1, 1), (1, -1), (-1, 1), (-1, -1)]
    near_blocks = [(1, 0), (-1, 0), (0, 1), (0, -1)]

    def experts(step, carry):
        group = (z + 1 + step) % depths
        sources = arr[group]
        width = sources.shape[-1]
        wide = sources.reshape(2 * SEQ, ROWS, width).astype(F32)
        results = []
        for e in range(2):
            mine = wide[:, e * CAP : (e + 1) * CAP, :].reshape(2 * SEQ * CAP, width).astype(BF16)
            pair = mm(mine, win[e])
            inner_width = wout.shape[1]
            gate = pair[:, :inner_width]
            inner = (gate / (1.0 + jnp.exp(-gate)) * pair[:, inner_width:]).astype(BF16)
            results.append(mm(inner, wout[e]).reshape(2 * SEQ, CAP, width))
        result = jnp.concatenate(results, axis=1).astype(BF16)
        arr[group] = result.reshape(sources.shape)
        for dx, dy in first_blocks:
            for core in (0, 1):
                there = group * 2 + core

                @pl.when(there != p)
                def _():
                    r_copy(ring_spot(s, 1, dx, dy), there).start()

        return carry

    lax.fori_loop(0, depths, experts, 0)

    def rq_copy(there):
        return pltpu.make_async_remote_copy(
            src_ref=arr.at[:, there // SEQ, there % SEQ, :, pl.ds(PCOLS, QCOLS)],
            dst_ref=retq.at[here],
            send_sem=rq_send.at[there],
            recv_sem=rq_recv.at[here],
            device_id=(2 * z + there // SEQ, there % SEQ),
            device_id_type=MESH,
        )

    def rq_go(step, carry):
        rq_copy((here + step) % (2 * SEQ)).start()
        return carry

    lax.fori_loop(1, 2 * SEQ, rq_go, 0)
    for dx, dy in middle_blocks + corner_blocks + near_blocks + [(0, 0)]:

        def r_go(step, carry):
            r_copy(ring_spot(s, 1, dx, dy), (p + step) % 8).start()
            return carry

        lax.fori_loop(1, 8, r_go, 0)
    retp[p] = arr[z, c, :, :, 0:PCOLS]
    retq[here] = arr[:, c, s, :, PCOLS:]

    def weigh(blocks):
        for dx, dy in blocks:
            source = ring_spot(s, 1, dx, dy)

            def r_wait(step, carry):
                r_copy_from(source, (p + step) % 8).wait_recv()
                return carry

            lax.fori_loop(1, 8, r_wait, 0)
            found = retp[:, source].reshape(8 * ROWS, PCOLS)
            ptok[source] = mm(mix(p_slots, pmeta[source]), found).astype(BF16)

    sums = []

    def pass_sum(half, piece, room, tf, tg, slot):
        copy = pltpu.make_async_remote_copy(
            src_ref=piece,
            dst_ref=room,
            send_sem=rs_send.at[half, slot],
            recv_sem=rs_recv.at[half, slot],
            device_id=(p, ring_spot(s, half, tf, tg)),
            device_id_type=MESH,
        )
        copy.start()
        sums.append(copy)

    def take(half, room, slot):
        pltpu.make_async_remote_copy(
            src_ref=room,
            dst_ref=room,
            send_sem=rs_send.at[half, slot],
            recv_sem=rs_recv.at[half, slot],
            device_id=(p, ring_spot(s, half, 1, 0)),
            device_id_type=MESH,
        ).wait_recv()
        return room[...].astype(F32)

    def block(half, df, dg, span=FULL):
        return at(half, ring_spot(s, half, df, dg), *span)

    def add_to(ref, *terms):
        total = ref[...].astype(F32)
        for term in terms:
            total = total + term
        ref[...] = total.astype(BF16)

    def far_sums(half, df):
        slot = 2 * (df % RING)
        pass_sum(half, block(half, df, 2, LOW), rs_a.at[half, df % RING, 0], 0, 1, slot)
        pass_sum(half, block(half, df, 2, HIGH), rs_a.at[half, df % RING, 1], 0, -1, slot + 1)

    def near_sums(half, df):
        k = df % RING
        add_to(block(half, df, 1, LOW), take(half, rs_a.at[half, k, 0], 2 * k))
        add_to(block(half, df, -1, HIGH), take(half, rs_a.at[half, k, 1], 2 * k + 1))
        pass_sum(half, block(half, df, 1), rs_b.at[half, k, 0], 0, 1, 8 + 2 * k)
        pass_sum(half, block(half, df, -1), rs_b.at[half, k, 1], 0, -1, 9 + 2 * k)

    def line_sum(half, df):
        k = df % RING
        add_to(
            block(half, df, 0),
            take(half, rs_b.at[half, k, 0], 8 + 2 * k),
            take(half, rs_b.at[half, k, 1], 9 + 2 * k),
        )

    def far_line(half):
        pass_sum(half, block(half, 2, 0, LOW), rs_c.at[half, 0], 1, 0, 16)
        pass_sum(half, block(half, 2, 0, HIGH), rs_c.at[half, 1], -1, 0, 17)

    def near_line(half):
        add_to(block(half, 1, 0, LOW), take(half, rs_c.at[half, 0], 16))
        add_to(block(half, -1, 0, HIGH), take(half, rs_c.at[half, 1], 17))
        pass_sum(half, block(half, 1, 0), rs_d.at[half, 0], 1, 0, 18)
        pass_sum(half, block(half, -1, 0), rs_d.at[half, 1], -1, 0, 19)

    weigh(first_blocks)
    for half in (0, 1):
        for df in (2, 1, -1):
            far_sums(half, df)
    weigh(middle_blocks)
    for half in (0, 1):
        far_sums(half, 0)
        near_sums(half, 2)
    weigh(corner_blocks)
    for half in (0, 1):
        near_sums(half, 1)
        near_sums(half, -1)
        line_sum(half, 2)
        far_line(half)
    def rq_wait(step, carry):
        back = (here + step) % (2 * SEQ)
        pltpu.make_async_remote_copy(
            src_ref=arr.at[:, back // SEQ, back % SEQ, :, pl.ds(PCOLS, QCOLS)],
            dst_ref=retq.at[back],
            send_sem=rq_send.at[back],
            recv_sem=rq_recv.at[back],
            device_id=(2 * z + back // SEQ, back % SEQ),
            device_id_type=MESH,
        ).wait()
        return carry

    lax.fori_loop(1, 2 * SEQ, rq_wait, 0)
    q_rows = lax.broadcasted_iota(jnp.int32, (2 * SEQ * ROWS, 128), 0)
    q_slots = (z * (2 * SEQ * ROWS) + q_rows).astype(F32)

    def q_weigh(source):
        found = retq[:, source].reshape(2 * SEQ * ROWS, QCOLS)
        qtok[source] = mm(mix(q_slots, qmeta[source]), found).astype(BF16)

    def q_sum(step):
        there = (z + step) % depths
        return pltpu.make_async_remote_copy(
            src_ref=qtok.at[there],
            dst_ref=rs_q.at[z],
            send_sem=rsq_send.at[there],
            recv_sem=rsq_recv.at[z],
            device_id=(depth(step), s),
            device_id_type=MESH,
        )

    for step in (2, 1, 3):
        q_weigh((z + step) % depths)
        q_sum(step).start()
    q_weigh(z)
    weigh(near_blocks)
    for half in (0, 1):
        near_sums(half, 0)
        line_sum(half, 1)
        line_sum(half, -1)
        near_line(half)

    weigh([(0, 0)])
    q_total = qtok[z].astype(F32)
    for step in (1, 2, 3):
        source = (z + step) % depths
        pltpu.make_async_remote_copy(
            src_ref=qtok.at[source],
            dst_ref=rs_q.at[source],
            send_sem=rsq_send.at[source],
            recv_sem=rsq_recv.at[source],
            device_id=(depth(step), s),
            device_id_type=MESH,
        ).wait()
        q_total = q_total + rs_q[source].astype(F32)
    out_ref[:, PCOLS:] = q_total.astype(BF16)
    for half in (0, 1):
        line_sum(half, 0)
        total = block(half, 0, 0)[...].astype(F32)
        total = total + take(half, rs_d.at[half, 0], 18) + take(half, rs_d.at[half, 1], 19)
        out_ref[:, half * (PCOLS // 2) : (half + 1) * (PCOLS // 2)] = total.astype(BF16)
    for copy in sums:
        copy.wait_send()

    def r_done(step, carry):
        source, back = step // 8, step % 8

        @pl.when(back != p)
        def _():
            r_copy(source, back).wait_send()

        return carry

    lax.fori_loop(0, 8 * SEQ, r_done, 0)

    def meta_wait(step, carry):
        plane_meta(step).wait_send()
        return carry

    lax.fori_loop(1, SEQ, meta_wait, 0)
    for step in (1, 2, 3):
        depth_meta(step).wait_send()


def run_experts(own, meta, w_in, w_out):
    rows, width = own.shape
    vmem = pl.BlockSpec(memory_space=pltpu.VMEM)
    hbm = pl.BlockSpec(memory_space=pl.ANY)
    dma = pltpu.SemaphoreType.DMA
    return pl.pallas_call(
        expert_kernel,
        in_specs=[vmem, vmem, hbm, hbm],
        out_specs=vmem,
        out_shape=jax.ShapeDtypeStruct((rows, width), BF16),
        scratch_shapes=[
            pltpu.VMEM((SEQ, rows, PCOLS), BF16),
            pltpu.VMEM((4, rows, QCOLS), BF16),
            pltpu.VMEM((SEQ, 32, rows), F32),
            pltpu.VMEM((4, 32, rows), F32),
            pltpu.VMEM((SEQ, 8, ROWS, PCOLS), BF16),
            pltpu.VMEM((4, 2 * SEQ, ROWS, QCOLS), BF16),
            pltpu.VMEM((4, 2, SEQ, ROWS, width), BF16),
            pltpu.VMEM(w_in.shape, BF16),
            pltpu.VMEM(w_out.shape, BF16),
            dma((2, 32)),
            dma((2, 32)),
            dma((4,)),
            dma((4,)),
            dma((SEQ + 4,)),
            dma((SEQ + 4,)),
            dma((SEQ, 8)),
            dma((8, SEQ)),
            dma((2 * SEQ,)),
            dma((2, SEQ)),
            dma((2,)),
            pltpu.VMEM((8, SEQ, ROWS, PCOLS), BF16),
            pltpu.VMEM((2 * SEQ, 4, ROWS, QCOLS), BF16),
            pltpu.VMEM((2, RING, 2, 64, PCOLS // 2), BF16),
            pltpu.VMEM((2, RING, 2, 128, PCOLS // 2), BF16),
            pltpu.VMEM((2, 2, 64, PCOLS // 2), BF16),
            pltpu.VMEM((2, 2, 128, PCOLS // 2), BF16),
            pltpu.VMEM((4, 128, QCOLS), BF16),
            dma((SEQ, 8)),
            dma((SEQ, 8)),
            dma((2 * SEQ,)),
            dma((2 * SEQ,)),
            dma((2, 20)),
            dma((2, 20)),
            dma((4,)),
            dma((4,)),
        ],
        compiler_params=pltpu.CompilerParams(
            collective_id=1, has_side_effects=True, vmem_limit_bytes=62 * 2**20
        ),
    )(own, meta, w_in, w_out)


def rms_scale(values, gain):
    mean = jnp.mean(values * values, axis=-1, keepdims=True)
    return values * lax.rsqrt(mean + EPS) * gain


def routing(chosen_ids, logits):
    tokens, experts = logits.shape
    table = lax.broadcasted_iota(jnp.int32, (1, 1, experts), 2)
    match = chosen_ids[:, :, None] == table
    member = jnp.any(match, axis=1)
    rows = lax.broadcasted_iota(jnp.int32, (tokens, tokens), 0)
    cols = lax.broadcasted_iota(jnp.int32, (tokens, tokens), 1)
    earlier = (rows > cols).astype(BF16)
    before = jnp.dot(earlier, member.astype(BF16), preferred_element_type=F32)
    place = jnp.sum(jnp.where(match, before[:, None, :], 0.0), axis=-1)
    picked = jnp.sum(jnp.where(match, logits[:, None, :], 0.0), axis=-1)
    return chosen_ids.astype(F32) * CAP + place, picked


def shards(
    tokens,
    span_lengths,
    state_slots,
    expert_ids,
    state_pool,
    attn_gain,
    w_query,
    w_key,
    w_value,
    w_zgate,
    w_heads,
    decay_rate,
    head_gain,
    w_output,
    moe_gain,
    router,
    w_expert_in,
    w_expert_out,
):
    local_rows, width = tokens.shape[1:]
    length = span_lengths[0]
    own_rows = tokens[0]
    head_weights = jnp.pad(w_heads.reshape(width, 4), ((0, 0), (0, 124)))
    first = lax.dynamic_index_in_dim(state_pool, state_slots[0], 0, keepdims=False)
    summed, final = attention(
        span_lengths,
        decay_rate,
        own_rows,
        attn_gain.reshape(1, width),
        w_output,
        head_weights,
        head_gain.reshape(1, 128),
        first,
        (w_query, w_key, w_value, w_zgate),
    )
    own_positions = lax.axis_index("seq") * local_rows + lax.broadcasted_iota(jnp.int32, (local_rows, 1), 0)
    own_live = (own_positions < length).astype(F32)
    attended = (summed * own_live).astype(BF16)
    residual = own_rows.astype(F32) + attended.astype(F32)
    moe_input = rms_scale(residual, moe_gain).astype(BF16)
    logits = jnp.dot(moe_input, router, preferred_element_type=F32)
    slots, picked = routing(expert_ids[0], logits)
    weights = jax.nn.softmax(picked, axis=-1) * own_live
    meta = jnp.concatenate(
        [
            jnp.pad(slots.T, ((0, 16 - TOP), (0, 0)), constant_values=-1.0),
            jnp.pad(weights.T, ((0, 16 - TOP), (0, 0))),
        ],
        axis=0,
    )
    expert_out = run_experts(moe_input, meta, w_expert_in, w_expert_out)
    return (attended[None], expert_out[None], final[None])


def solution(mesh):
    return jax.shard_map(
        shards,
        mesh=mesh,
        in_specs=(
            P("prompt", "seq", None),
            P("prompt"),
            P("prompt"),
            P("prompt", "seq", None),
            P(None, "seq", None, None),
            P(),
            P(None, "seq"),
            P(None, "seq"),
            P(None, "seq"),
            P(None, "seq"),
            P(None, None, "seq"),
            P("seq"),
            P(),
            P("seq", None),
            P(),
            P(),
            P(("prompt", "seq"), None, None),
            P(("prompt", "seq"), None, None),
        ),
        out_specs=(
            P("prompt", "seq", None),
            P("prompt", "seq", None),
            P("prompt", "seq", None, None),
        ),
        check_vma=False,
    )
```

```python
import functools
import jax
import jax.numpy as jnp
from jax import lax
from jax.experimental import pallas as pl
from jax.experimental.pallas import tpu as pltpu
from jax.sharding import PartitionSpec as P

EPS = 1e-06
CH = 128
RING = 4
SEQ = RING * RING
HEADS = 2
F32 = jnp.float32
BF16 = jnp.bfloat16
MESH = pl.DeviceIdType.MESH


def mm(a, b):
    return jnp.dot(a, b, preferred_element_type=F32)


def halves(a):
    high = a.astype(BF16)
    return high, (a - high.astype(F32)).astype(BF16)


def mm3(a, b):
    a_high, a_low = halves(a)
    b_high, b_low = halves(b)
    wide = mm(jnp.concatenate([a_high, a_low], axis=1), jnp.concatenate([b_high, b_high], axis=0))
    return wide + mm(a_high, b_low)


def unit_lower_inverse(lows, rows, cols):
    eye = jnp.where(rows == cols, 1.0, 0.0)
    inverses = [eye - jnp.where(rows // 2 == cols // 2, low, 0.0) for low in lows]
    size = 2
    while size < CH:
        mask = (rows // (2 * size) == cols // (2 * size)) & (rows // size != cols // size)
        inner = [mm3(jnp.where(mask, low, 0.0), inv) for low, inv in zip(lows, inverses)]
        inverses = [inv - mm3(inv, part) for inv, part in zip(inverses, inner)]
        size *= 2
    return inverses


def prepare(blocks, length, tok, w_ref, rate, gain, store):
    left_ref, kt_ref, attn_ref, upd_ref, last_ref, gate_ref = store
    rows = lax.broadcasted_iota(jnp.int32, (CH, CH), 0)
    cols = lax.broadcasted_iota(jnp.int32, (CH, CH), 1)
    tri = jnp.where(rows >= cols, 1.0, 0.0)
    proj_all = mm(jnp.concatenate([tok[b] for b in blocks], axis=0), w_ref[...])
    lows = []
    rights = []
    for n, block in enumerate(blocks):
        part = proj_all[n * CH : (n + 1) * CH]
        q, k = part[:, 0:128], part[:, 128:256]
        q = q * (lax.rsqrt(jnp.sum(q * q, axis=-1, keepdims=True) + EPS) * 128 ** (-0.5))
        k = k * lax.rsqrt(jnp.sum(k * k, axis=-1, keepdims=True) + EPS)
        logits = part[:, 768:896]
        live = jnp.where(block * CH + rows < length, 1.0, 0.0)
        softplus = jnp.maximum(logits, 0.0) + jnp.log1p(jnp.exp(-jnp.abs(logits)))
        logdec = -rate * softplus * live
        beta2 = live / (1.0 + jnp.exp(-logits))
        cumul = jnp.dot(tri, logdec, preferred_element_type=F32, precision=lax.Precision.HIGHEST)
        cumul_t = cumul.T
        both = mm(jnp.concatenate([k.astype(BF16), q.astype(BF16)], axis=0), k.T.astype(BF16))
        kk, qk = both[:CH], both[CH:]
        for h in range(HEADS):
            g = cumul[:, h : h + 1]
            decay = jnp.exp(jnp.minimum(g - cumul_t[h : h + 1, :], 0.0))
            beta = beta2[:, 2 + h : 3 + h]
            lows.append(jnp.where(rows > cols, beta * kk * decay, 0.0))
            attn_ref[block, h] = jnp.where(rows >= cols, qk * decay, 0.0).astype(BF16)
            start = jnp.exp(g)
            value = part[:, 256 + 128 * h : 384 + 128 * h]
            rights.append(jnp.concatenate([beta * value, (beta * start) * k], axis=1).astype(BF16))
            last = cumul[CH - 1 : CH, h : h + 1]
            left_ref[block, h, CH:, :] = (start * q).astype(BF16)
            kt_ref[block, h] = (jnp.exp(last - g) * k).T.astype(BF16)
            last_ref[block, h] = jnp.broadcast_to(jnp.exp(last), (8, CH))
            z = part[:, 512 + 128 * h : 640 + 128 * h]
            gate_ref[block, h] = gain * (z / (1.0 + jnp.exp(-z)))
    for n, inverse in enumerate(unit_lower_inverse(lows, rows, cols)):
        block, h = blocks[n // HEADS], n % HEADS
        high, low = halves(inverse)
        got = mm(jnp.concatenate([high, low], axis=1), jnp.concatenate([rights[n], rights[n]], axis=0))
        upd_ref[block, h] = got[:, :CH]
        left_ref[block, h, :CH, :] = got[:, CH:].astype(BF16)


def advance(block, state_ref, store):
    left_ref, kt_ref, attn_ref, upd_ref, last_ref, gate_ref = store
    outs = []
    for h in range(HEADS):
        state = state_ref[h]
        left = left_ref[block, h]
        high, low = halves(state)
        got = mm(jnp.concatenate([left, left], axis=1), jnp.concatenate([high, low], axis=0))
        corrected = upd_ref[block, h] - got[:CH]
        high, low = halves(corrected)
        kt = kt_ref[block, h]
        state_ref[h] = last_ref[block, h, 0:1, :] * state + mm(
            jnp.concatenate([kt, kt], axis=1), jnp.concatenate([high, low], axis=0)
        )
        out = got[CH:] + mm(attn_ref[block, h], high)
        scale = lax.rsqrt(jnp.mean(out * out, axis=-1, keepdims=True) + EPS)
        outs.append((out * scale * gate_ref[block, h]).astype(BF16))
    return jnp.concatenate(outs, axis=1)


def ring_spot(s, half, df, dg):
    dx, dy = (dg, df) if half == 0 else (df, dg)
    x, y = s // RING, s % RING
    return ((x + dx + 2 * RING) % RING) * RING + (y + dy + 2 * RING) % RING


FULL, LOW, HIGH = (0, 128), (0, 64), (64, 64)


class Rings:
    def __init__(self, p, s, at, send_sem, recv_sem, hook=None):
        self.p, self.s, self.at = p, s, at
        self.send_sem, self.recv_sem = send_sem, recv_sem
        self.hook = hook or (lambda half, df, dg: None)
        self.started = []

    def copy(self, half, df, dg, span, tf, tg):
        slot = ((df - tf) % RING * RING + (dg - tg) % RING) * 2 + (1 if span is HIGH else 0)
        piece = self.at(half, ring_spot(self.s, half, df, dg), *span)
        return pltpu.make_async_remote_copy(
            src_ref=piece,
            dst_ref=piece,
            send_sem=self.send_sem.at[half, slot],
            recv_sem=self.recv_sem.at[half, slot],
            device_id=(self.p, ring_spot(self.s, half, tf, tg)),
            device_id_type=MESH,
        )

    def send(self, *args):
        copy = self.copy(*args)
        copy.start()
        self.started.append(copy)

    def arrive(self, half, df, dg, span=FULL):
        slot = (df % RING * RING + dg % RING) * 2 + (1 if span is HIGH else 0)
        piece = self.at(half, ring_spot(self.s, half, df, dg), *span)
        pltpu.make_async_remote_copy(
            src_ref=piece,
            dst_ref=piece,
            send_sem=self.send_sem.at[half, slot],
            recv_sem=self.recv_sem.at[half, slot],
            device_id=(self.p, ring_spot(self.s, half, 1, 0)),
            device_id_type=MESH,
        ).wait_recv()

    def begin(self):
        for half in (0, 1):
            for step in (1, -1):
                self.send(half, 0, 0, FULL, step, 0)
        for half in (0, 1):
            for step in (1, -1):
                self.send(half, 0, 0, FULL, 0, step)

    def first_near(self):
        for half in (0, 1):
            for df, span in ((-1, LOW), (1, HIGH)):
                self.arrive(half, df, 0)
                self.send(half, df, 0, span, -df, 0)
            self.hook(half, -1, 0)
            self.hook(half, 1, 0)

    def second_near(self):
        for half in (0, 1):
            for dg, span in ((-1, LOW), (1, HIGH)):
                self.arrive(half, 0, dg)
                self.send(half, 0, dg, span, 0, -dg)
            self.hook(half, 0, -1)
            self.hook(half, 0, 1)
            for df in (-1, 1):
                for step in (1, -1):
                    self.send(half, df, 0, FULL, 0, step)

    def near(self):
        self.first_near()
        self.second_near()

    def far(self):
        for half in (0, 1):
            self.arrive(half, 2, 0, LOW)
            self.arrive(half, 2, 0, HIGH)
            for step in (1, -1):
                self.send(half, 2, 0, FULL, 0, step)
            self.hook(half, 2, 0)
        self.second_far((0,))

    def second_far(self, dfs):
        for half in (0, 1):
            for df in dfs:
                self.arrive(half, df, 2, LOW)
                self.arrive(half, df, 2, HIGH)
                self.hook(half, df, 2)

    def corners(self, dfs=(-1, 1)):
        for half in (0, 1):
            for df in dfs:
                for dg, span in ((-1, LOW), (1, HIGH)):
                    self.arrive(half, df, dg)
                    self.send(half, df, dg, span, 0, -dg)
                    self.hook(half, df, dg)

    def far_corners(self):
        self.corners((2,))

    def last(self):
        self.second_far((-1, 1, 2))


def attention_kernel(
    length_ref,
    rate_ref,
    own_ref,
    norm_ref,
    wo_ref,
    heads_ref,
    gain_ref,
    first_ref,
    query_hbm,
    key_hbm,
    value_hbm,
    zgate_hbm,
    out_ref,
    final_ref,
    w_ref,
    load_sem,
    tok,
    wall,
    got,
    gout,
    left_ref,
    kt_ref,
    attn_ref,
    upd_ref,
    last_ref,
    gate_ref,
    state_ref,
    ring_send,
    ring_recv,
    z_send,
    z_recv,
    mate_send,
    mate_recv,
    got_send,
    got_recv,
):
    store = (left_ref, kt_ref, attn_ref, upd_ref, last_ref, gate_ref)
    p = lax.axis_index("prompt")
    s = lax.axis_index("seq")
    z, c = p // 2, p % 2
    x, y = s // RING, s % RING
    parity = z % 2
    length = length_ref[0]
    tcols = tok.shape[2] // 2

    def spot(half, df, dg):
        return ring_spot(s, half, df, dg)

    def depth(step):
        return ((z + step + RING) % RING) * 2 + c

    mate = z * 2 + (1 - c)

    def at(chan, half, owner, first, count, side=None, par=None):
        if chan == 0:
            return tok.at[owner, pl.ds(first, count), pl.ds(half * tcols, tcols)]
        row = pl.multiple_of(owner * 256 + half * 128 + first, 64)
        return wall.at[c if side is None else side, parity if par is None else par, pl.ds(row, count), :]

    started = []
    passed = []

    def hand_on(half, df, dg):
        owner = spot(half, df, dg)
        slot = (df % RING) * RING + dg % RING
        piece = at(1, half, owner, *FULL)
        copy = pltpu.make_async_remote_copy(
            src_ref=piece,
            dst_ref=piece,
            send_sem=z_send.at[half, slot],
            recv_sem=z_recv.at[half, slot],
            device_id=(depth(1 if half == 0 else -1), s),
            device_id_type=MESH,
        )
        copy.start()
        started.append(copy)
        copy = to_mate(half, df, dg, parity, 0)
        copy.start()
        started.append(copy)
        passed.append((half, df, dg))

    def to_mate(half, df, dg, par, kind):
        slot = (df % RING) * RING + dg % RING
        piece = at(1, half, spot(half, df, dg), *FULL, par=par)
        return pltpu.make_async_remote_copy(
            src_ref=piece,
            dst_ref=piece,
            send_sem=mate_send.at[kind, half, slot],
            recv_sem=mate_recv.at[kind, half, slot],
            device_id=(mate, s),
            device_id_type=MESH,
        )

    def from_z(half, df, dg):
        owner = spot(half, df, dg)
        slot = (df % RING) * RING + dg % RING
        piece = at(1, half, owner, *FULL, par=1 - parity)
        pltpu.make_async_remote_copy(
            src_ref=piece,
            dst_ref=piece,
            send_sem=z_send.at[half, slot],
            recv_sem=z_recv.at[half, slot],
            device_id=(depth(1), s),
            device_id_type=MESH,
        ).wait_recv()
        copy = to_mate(half, df, dg, 1 - parity, 1)
        copy.start()
        started.append(copy)

    def from_mate(half, df, dg):
        slot = (df % RING) * RING + dg % RING
        for kind in (0, 1):
            piece = at(1, half, spot(half, df, dg), *FULL, side=1 - c, par=parity if kind == 0 else 1 - parity)
            pltpu.make_async_remote_copy(
                src_ref=piece,
                dst_ref=piece,
                send_sem=mate_send.at[kind, half, slot],
                recv_sem=mate_recv.at[kind, half, slot],
                device_id=(mate, s),
                device_id_type=MESH,
            ).wait_recv()

    tokens = Rings(p, s, functools.partial(at, 0), ring_send.at[0], ring_recv.at[0])
    others = Rings(p, s, functools.partial(at, 1), ring_send.at[1], ring_recv.at[1], hand_on)

    def block_of(dx, dy):
        return spot(1, dx, dy)

    def compute(offsets):
        prepare(
            [block_of(*offset) for offset in offsets], length, tok, w_ref, rate, gain_ref[...], store
        )

    loads = []
    column = 0
    for number, source in enumerate((query_hbm, key_hbm, value_hbm, zgate_hbm)):
        count = source.shape[1]
        loads.append(
            pltpu.make_async_copy(source, w_ref.at[:, pl.ds(column, count)], load_sem.at[number])
        )
        loads[-1].start()
        column += count
    barrier = pltpu.get_barrier_semaphore()

    def greet(step, carry):
        pl.semaphore_signal(barrier, 1, device_id=(p, (s + step) % SEQ), device_id_type=MESH)
        return carry

    lax.fori_loop(1, SEQ, greet, 0)
    for other in (mate, depth(1), depth(-1)):
        pl.semaphore_signal(barrier, 1, device_id=(other, s), device_id_type=MESH)
    own = own_ref[...].astype(F32)
    own_scale = lax.rsqrt(jnp.mean(own * own, axis=-1, keepdims=True) + EPS)
    tok[s] = (own * own_scale * norm_ref[...]).astype(BF16)
    w_ref[:, column:] = heads_ref[...]
    lane = lax.broadcasted_iota(jnp.int32, (1, 128), 1)
    rate = jnp.where(lane == 0, rate_ref[0], jnp.where(lane == 1, rate_ref[1], 0.0))
    for side in (0, 1):
        for par in (0, 1):
            first = (2 * side + par) * 512
            wall[side, par, pl.ds(pl.multiple_of(s * 256, 256), 256), :] = wo_ref[:, first : first + 512]
    for h in range(HEADS):
        state_ref[h] = first_ref[h].T
    pl.semaphore_wait(barrier, SEQ + 2)

    tokens.begin()
    others.begin()
    for load in loads:
        load.wait()
    compute([(0, 0)])
    tokens.near()
    others.near()
    compute([(0, 1), (0, -1), (1, 0), (-1, 0)])
    tokens.far()
    others.far()
    compute([(0, 2), (2, 0)])
    tokens.corners()
    others.corners()
    compute([(1, 1), (1, -1), (-1, 1), (-1, -1)])
    tokens.far_corners()
    others.far_corners()
    tokens.last()
    compute([(1, 2), (-1, 2), (2, 1), (2, -1), (2, 2)])
    others.last()

    def give(index):
        here = gout.at[index]
        there = got.at[:, pl.ds(pl.multiple_of(s * 256, 256), 256)]
        return pltpu.make_async_remote_copy(
            src_ref=here,
            dst_ref=there,
            send_sem=got_send.at[index],
            recv_sem=got_recv.at[s],
            device_id=(p, index),
            device_id_type=MESH,
        )

    def scan(index, carry):
        gated = advance(index, state_ref, store)

        @pl.when(index != s)
        def _():
            gout[index] = gated
            give(index).start()

        @pl.when(index == s)
        def _():
            got[:, pl.ds(pl.multiple_of(s * 256, 256), 256)] = gated

        return carry

    lax.fori_loop(0, 8, scan, 0)
    for item in passed[:16]:
        from_z(*item)
    lax.fori_loop(8, SEQ, scan, 0)
    for h in range(HEADS):
        final_ref[h] = state_ref[h].T
    for item in passed[16:]:
        from_z(*item)

    def receive(step, carry):
        source = (s + step) % SEQ
        there = got.at[:, pl.ds(pl.multiple_of(source * 256, 256), 256)]
        pltpu.make_async_remote_copy(
            src_ref=gout.at[source],
            dst_ref=there,
            send_sem=got_send.at[source],
            recv_sem=got_recv.at[source],
            device_id=(p, source),
            device_id_type=MESH,
        ).wait()
        return carry

    lax.fori_loop(1, SEQ, receive, 0)
    for item in passed:
        from_mate(*item)
    for copy in started + tokens.started + others.started:
        copy.wait_send()
    for side in (0, 1):
        for par in (0, 1):
            first = (2 * side + par) * 512
            out_ref[:, first : first + 512] = mm(got[...], wall[side, par])


def attention(length, rate, own, norm_gain, w_output, head_weights, gain, first, projections):
    rows, width = own.shape
    columns = sum(weight.shape[1] for weight in projections) + head_weights.shape[1]
    smem = pl.BlockSpec(memory_space=pltpu.SMEM)
    vmem = pl.BlockSpec(memory_space=pltpu.VMEM)
    dma = pltpu.SemaphoreType.DMA
    return pl.pallas_call(
        attention_kernel,
        in_specs=[smem, smem] + [vmem] * 6 + [pl.BlockSpec(memory_space=pl.ANY)] * len(projections),
        out_specs=[vmem, vmem],
        out_shape=[
            jax.ShapeDtypeStruct((rows, width), F32),
            jax.ShapeDtypeStruct((HEADS, 128, 128), F32),
        ],
        scratch_shapes=[
            pltpu.VMEM((width, columns), BF16),
            dma((4,)),
            pltpu.VMEM((SEQ, rows, width), BF16),
            pltpu.VMEM((2, 2, SEQ * 256, 512), BF16),
            pltpu.VMEM((rows, SEQ * 256), BF16),
            pltpu.VMEM((SEQ, rows, 256), BF16),
            pltpu.VMEM((SEQ, HEADS, 2 * CH, 128), BF16),
            pltpu.VMEM((SEQ, HEADS, 128, CH), BF16),
            pltpu.VMEM((SEQ, HEADS, CH, CH), BF16),
            pltpu.VMEM((SEQ, HEADS, CH, 128), F32),
            pltpu.VMEM((SEQ, HEADS, 8, CH), F32),
            pltpu.VMEM((SEQ, HEADS, CH, 128), F32),
            pltpu.VMEM((HEADS, 128, 128), F32),
            dma((2, 2, 32)),
            dma((2, 2, 32)),
            dma((2, 16)),
            dma((2, 16)),
            dma((2, 2, 16)),
            dma((2, 2, 16)),
            dma((SEQ,)),
            dma((SEQ,)),
        ],
        compiler_params=pltpu.CompilerParams(
            collective_id=0, has_side_effects=True, vmem_limit_bytes=56 * 2**20
        ),
    )(length, rate, own, norm_gain, w_output, head_weights, gain, first, *projections)


CAP = 8
ROWS = 2 * CAP
TOP = 10
PCOLS = 1280
QCOLS = 768


def select(slots, meta):
    hit = slots == meta[0:1, :]
    for j in range(1, TOP):
        hit = hit | (slots == meta[j : j + 1, :])
    return jnp.where(hit, 1.0, 0.0).astype(BF16)


def mix(slots, meta):
    share = jnp.where(slots == meta[0:1, :], meta[16:17, :], 0.0)
    for j in range(1, TOP):
        share = share + jnp.where(slots == meta[j : j + 1, :], meta[16 + j : 17 + j, :], 0.0)
    return share.T.astype(BF16)


def expert_kernel(
    own_ref,
    meta_ref,
    win_hbm,
    wout_hbm,
    out_ref,
    ptok,
    qtok,
    pmeta,
    qmeta,
    pout,
    qout,
    arr,
    win,
    wout,
    ring_send,
    ring_recv,
    z_send,
    z_recv,
    meta_send,
    meta_recv,
    p_send,
    p_recv,
    q_send,
    q_recv,
    local_sem,
    retp,
    retq,
    rs_a,
    rs_b,
    rs_c,
    rs_d,
    rs_q,
    r_send,
    r_recv,
    rq_send,
    rq_recv,
    rs_send,
    rs_recv,
    rsq_send,
    rsq_recv,
):
    p = lax.axis_index("prompt")
    s = lax.axis_index("seq")
    z, c = p // 2, p % 2
    depths = 4

    def depth(step):
        return ((z + step + depths) % depths) * 2 + c

    loads = [
        pltpu.make_async_copy(win_hbm, win, local_sem.at[0]),
        pltpu.make_async_copy(wout_hbm, wout, local_sem.at[1]),
    ]
    for load in loads:
        load.start()
    barrier = pltpu.get_barrier_semaphore()

    def greet_plane(step, carry):
        for core in (0, 1):
            pl.semaphore_signal(
                barrier, 1, device_id=(2 * z + core, (s + step) % SEQ), device_id_type=MESH
            )
        return carry

    lax.fori_loop(1, SEQ, greet_plane, 0)

    def greet_column(step, carry):
        pl.semaphore_signal(barrier, 1, device_id=((p + step) % (2 * depths), s), device_id_type=MESH)
        return carry

    lax.fori_loop(1, 2 * depths, greet_column, 0)
    ptok[s] = own_ref[:, :PCOLS]
    qtok[z] = own_ref[:, PCOLS:]
    pmeta[s] = meta_ref[...]
    qmeta[z] = meta_ref[...]
    pl.semaphore_wait(barrier, 2 * (SEQ - 1) + 2 * depths - 1)

    def plane_meta(step):
        there = (s + step) % SEQ
        return pltpu.make_async_remote_copy(
            src_ref=meta_ref,
            dst_ref=pmeta.at[s],
            send_sem=meta_send.at[step],
            recv_sem=meta_recv.at[s],
            device_id=(p, there),
            device_id_type=MESH,
        )

    def plane_meta_from(step):
        source = (s + step) % SEQ
        return pltpu.make_async_remote_copy(
            src_ref=meta_ref,
            dst_ref=pmeta.at[source],
            send_sem=meta_send.at[step],
            recv_sem=meta_recv.at[source],
            device_id=(p, source),
            device_id_type=MESH,
        )

    def depth_meta(step):
        return pltpu.make_async_remote_copy(
            src_ref=meta_ref,
            dst_ref=qmeta.at[z],
            send_sem=meta_send.at[SEQ + step],
            recv_sem=meta_recv.at[SEQ + z],
            device_id=(depth(step), s),
            device_id_type=MESH,
        )

    def depth_meta_from(step):
        source = (z + step) % depths
        return pltpu.make_async_remote_copy(
            src_ref=meta_ref,
            dst_ref=qmeta.at[source],
            send_sem=meta_send.at[SEQ + step],
            recv_sem=meta_recv.at[SEQ + source],
            device_id=(depth(step), s),
            device_id_type=MESH,
        )

    def start_plane_meta(step, carry):
        plane_meta(step).start()
        return carry

    lax.fori_loop(1, SEQ, start_plane_meta, 0)
    for step in (1, 2, 3):
        depth_meta(step).start()

    def at(half, owner, first, count):
        return ptok.at[owner, pl.ds(first, count), pl.ds(half * (PCOLS // 2), PCOLS // 2)]

    rings = Rings(p, s, at, ring_send, ring_recv)

    def z_copy(source, span, step, slot):
        piece = qtok.at[source, pl.ds(*span), :]
        return pltpu.make_async_remote_copy(
            src_ref=piece,
            dst_ref=piece,
            send_sem=z_send.at[slot],
            recv_sem=z_recv.at[slot],
            device_id=(depth(step), s),
            device_id_type=MESH,
        )

    z_copies = [z_copy(z, FULL, 1, 0), z_copy(z, FULL, -1, 1)]
    for copy in z_copies:
        copy.start()
    rings.begin()

    rows = lax.broadcasted_iota(jnp.int32, (8 * ROWS, 128), 0)
    p_slots = ((rows // ROWS) * (SEQ * ROWS) + s * ROWS + rows % ROWS).astype(F32)

    def p_copy(source, there):
        return pltpu.make_async_remote_copy(
            src_ref=pout.at[source, there],
            dst_ref=arr.at[z, c, source, :, pl.ds(0, PCOLS)],
            send_sem=p_send.at[source, there],
            recv_sem=p_recv.at[p, source],
            device_id=(there, s),
            device_id_type=MESH,
        )

    def p_hand(source):
        picked = mm(select(p_slots, pmeta[source]), ptok[source]).astype(BF16)
        pout[source] = picked.reshape(8, ROWS, PCOLS)

        def go(step, carry):
            p_copy(source, (p + step) % 8).start()
            return carry

        lax.fori_loop(1, 8, go, 0)
        arr[z, c, source, :, 0:PCOLS] = pout[source, p]

    def p_hands(offsets):
        for dx, dy in offsets:
            source = ring_spot(s, 1, dx, dy)
            pltpu.make_async_remote_copy(
                src_ref=meta_ref,
                dst_ref=pmeta.at[source],
                send_sem=meta_send.at[0],
                recv_sem=meta_recv.at[source],
                device_id=(p, source),
                device_id_type=MESH,
            ).wait_recv()
            p_hand(source)

    def q_copy(there):
        return pltpu.make_async_remote_copy(
            src_ref=qout.at[:, there],
            dst_ref=arr.at[:, c, s, :, pl.ds(PCOLS, QCOLS)],
            send_sem=q_send.at[there],
            recv_sem=q_recv.at[c, s],
            device_id=(2 * z + there // SEQ, there % SEQ),
            device_id_type=MESH,
        )

    def q_hand(source):
        slots = (z * (2 * SEQ * ROWS) + lax.broadcasted_iota(jnp.int32, (2 * SEQ * ROWS, 128), 0)).astype(F32)
        picked = mm(select(slots, qmeta[source]), qtok[source]).astype(BF16)
        qout[source] = picked.reshape(2 * SEQ, ROWS, QCOLS)

    p_hand(s)
    q_hand(z)
    z_copy((z + 3) % depths, FULL, 1, 0).wait_recv()
    z_copy((z + 1) % depths, FULL, -1, 1).wait_recv()
    z_copies.append(z_copy((z + 3) % depths, LOW, 1, 2))
    z_copies.append(z_copy((z + 1) % depths, HIGH, -1, 3))
    z_copies[2].start()
    z_copies[3].start()
    for step in (1, 3):
        depth_meta_from(step).wait_recv()
        q_hand((z + step) % depths)
    rings.near()
    p_hands([(0, 1), (0, -1), (1, 0), (-1, 0)])
    depth_meta_from(2).wait_recv()
    z_copy((z + 2) % depths, LOW, 1, 2).wait_recv()
    z_copy((z + 2) % depths, HIGH, -1, 3).wait_recv()
    q_hand((z + 2) % depths)
    here = c * SEQ + s

    def q_go(step, carry):
        q_copy((here + step) % (2 * SEQ)).start()
        return carry

    rings.far()
    p_hands([(0, 2), (2, 0)])
    rings.corners()
    p_hands([(1, 1), (1, -1), (-1, 1), (-1, -1)])
    rings.far_corners()
    rings.last()
    lax.fori_loop(1, 2 * SEQ, q_go, 0)
    arr[:, c, s, :, PCOLS:] = qout[:, here]
    p_hands([(1, 2), (-1, 2), (2, 1), (2, -1), (2, 2)])

    def p_wait(step, carry):
        source, back = step // 8, step % 8

        @pl.when(back != p)
        def _():
            pltpu.make_async_remote_copy(
                src_ref=pout.at[source, back],
                dst_ref=arr.at[back // 2, back % 2, source, :, pl.ds(0, PCOLS)],
                send_sem=p_send.at[source, back],
                recv_sem=p_recv.at[back, source],
                device_id=(back, s),
                device_id_type=MESH,
            ).wait()

        return carry

    lax.fori_loop(0, 8 * SEQ, p_wait, 0)

    def q_wait(step, carry):
        back = (here + step) % (2 * SEQ)
        pltpu.make_async_remote_copy(
            src_ref=qout.at[:, back],
            dst_ref=arr.at[:, back // SEQ, back % SEQ, :, pl.ds(PCOLS, QCOLS)],
            send_sem=q_send.at[back],
            recv_sem=q_recv.at[back // SEQ, back % SEQ],
            device_id=(2 * z + back // SEQ, back % SEQ),
            device_id_type=MESH,
        ).wait()
        return carry

    lax.fori_loop(1, 2 * SEQ, q_wait, 0)
    for load in loads:
        load.wait()

    for copy in rings.started + z_copies:
        copy.wait_send()

    def r_copy(source, there):
        return pltpu.make_async_remote_copy(
            src_ref=arr.at[there // 2, there % 2, source, :, pl.ds(0, PCOLS)],
            dst_ref=retp.at[p, source],
            send_sem=r_send.at[source, there],
            recv_sem=r_recv.at[source, p],
            device_id=(there, s),
            device_id_type=MESH,
        )

    def r_copy_from(source, back):
        return pltpu.make_async_remote_copy(
            src_ref=arr.at[back // 2, back % 2, source, :, pl.ds(0, PCOLS)],
            dst_ref=retp.at[back, source],
            send_sem=r_send.at[source, back],
            recv_sem=r_recv.at[source, back],
            device_id=(back, s),
            device_id_type=MESH,
        )

    first_blocks = [(2, 2), (2, 1), (2, -1), (1, 2), (-1, 2)]
    middle_blocks = [(2, 0), (0, 2)]
    corner_blocks = [(1, 1), (1, -1), (-1, 1), (-1, -1)]
    near_blocks = [(1, 0), (-1, 0), (0, 1), (0, -1)]

    def rq_copy(there, group):
        return pltpu.make_async_remote_copy(
            src_ref=arr.at[group, there // SEQ, there % SEQ, :, pl.ds(PCOLS, QCOLS)],
            dst_ref=retq.at[here, group],
            send_sem=rq_send.at[there, group],
            recv_sem=rq_recv.at[here, group],
            device_id=(2 * z + there // SEQ, there % SEQ),
            device_id_type=MESH,
        )

    def experts(step, carry):
        group = (z + 1 + step) % depths
        sources = arr[group]
        width = sources.shape[-1]
        wide = sources.reshape(2 * SEQ, ROWS, width).astype(F32)
        results = []
        for e in range(2):
            mine = wide[:, e * CAP : (e + 1) * CAP, :].reshape(2 * SEQ * CAP, width).astype(BF16)
            pair = mm(mine, win[e])
            inner_width = wout.shape[1]
            gate = pair[:, :inner_width]
            inner = (gate / (1.0 + jnp.exp(-gate)) * pair[:, inner_width:]).astype(BF16)
            results.append(mm(inner, wout[e]).reshape(2 * SEQ, CAP, width))
        result = jnp.concatenate(results, axis=1).astype(BF16)
        arr[group] = result.reshape(sources.shape)
        for dx, dy in first_blocks:
            for core in (0, 1):
                there = group * 2 + core

                @pl.when(there != p)
                def _():
                    r_copy(ring_spot(s, 1, dx, dy), there).start()

        def rq_go(offset, carry):
            rq_copy((here + offset) % (2 * SEQ), group).start()
            return carry

        return lax.fori_loop(1, 2 * SEQ, rq_go, carry)

    lax.fori_loop(0, depths, experts, 0)

    for dx, dy in middle_blocks + corner_blocks + near_blocks + [(0, 0)]:

        def r_go(step, carry):
            r_copy(ring_spot(s, 1, dx, dy), (p + step) % 8).start()
            return carry

        lax.fori_loop(1, 8, r_go, 0)
    retp[p] = arr[z, c, :, :, 0:PCOLS]
    retq[here] = arr[:, c, s, :, PCOLS:]

    def weigh(blocks):
        for dx, dy in blocks:
            source = ring_spot(s, 1, dx, dy)

            def r_wait(step, carry):
                r_copy_from(source, (p + step) % 8).wait_recv()
                return carry

            lax.fori_loop(1, 8, r_wait, 0)
            found = retp[:, source].reshape(8 * ROWS, PCOLS)
            ptok[source] = mm(mix(p_slots, pmeta[source]), found).astype(BF16)

    sums = []

    def pass_sum(half, piece, room, tf, tg, slot):
        copy = pltpu.make_async_remote_copy(
            src_ref=piece,
            dst_ref=room,
            send_sem=rs_send.at[half, slot],
            recv_sem=rs_recv.at[half, slot],
            device_id=(p, ring_spot(s, half, tf, tg)),
            device_id_type=MESH,
        )
        copy.start()
        sums.append(copy)

    def take(half, room, slot):
        pltpu.make_async_remote_copy(
            src_ref=room,
            dst_ref=room,
            send_sem=rs_send.at[half, slot],
            recv_sem=rs_recv.at[half, slot],
            device_id=(p, ring_spot(s, half, 1, 0)),
            device_id_type=MESH,
        ).wait_recv()
        return room[...].astype(F32)

    def block(half, df, dg, span=FULL):
        return at(half, ring_spot(s, half, df, dg), *span)

    def add_to(ref, *terms):
        total = ref[...].astype(F32)
        for term in terms:
            total = total + term
        ref[...] = total.astype(BF16)

    def far_sums(half, df):
        slot = 2 * (df % RING)
        pass_sum(half, block(half, df, 2, LOW), rs_a.at[half, df % RING, 0], 0, 1, slot)
        pass_sum(half, block(half, df, 2, HIGH), rs_a.at[half, df % RING, 1], 0, -1, slot + 1)

    def near_sums(half, df):
        k = df % RING
        add_to(block(half, df, 1, LOW), take(half, rs_a.at[half, k, 0], 2 * k))
        add_to(block(half, df, -1, HIGH), take(half, rs_a.at[half, k, 1], 2 * k + 1))
        pass_sum(half, block(half, df, 1), rs_b.at[half, k, 0], 0, 1, 8 + 2 * k)
        pass_sum(half, block(half, df, -1), rs_b.at[half, k, 1], 0, -1, 9 + 2 * k)

    def line_sum(half, df):
        k = df % RING
        add_to(
            block(half, df, 0),
            take(half, rs_b.at[half, k, 0], 8 + 2 * k),
            take(half, rs_b.at[half, k, 1], 9 + 2 * k),
        )

    def far_line(half):
        pass_sum(half, block(half, 2, 0, LOW), rs_c.at[half, 0], 1, 0, 16)
        pass_sum(half, block(half, 2, 0, HIGH), rs_c.at[half, 1], -1, 0, 17)

    def near_line(half):
        add_to(block(half, 1, 0, LOW), take(half, rs_c.at[half, 0], 16))
        add_to(block(half, -1, 0, HIGH), take(half, rs_c.at[half, 1], 17))
        pass_sum(half, block(half, 1, 0), rs_d.at[half, 0], 1, 0, 18)
        pass_sum(half, block(half, -1, 0), rs_d.at[half, 1], -1, 0, 19)

    weigh(first_blocks)
    for half in (0, 1):
        for df in (2, 1, -1):
            far_sums(half, df)
    weigh(middle_blocks)
    for half in (0, 1):
        far_sums(half, 0)
        near_sums(half, 2)
    weigh(corner_blocks)
    for half in (0, 1):
        near_sums(half, 1)
        near_sums(half, -1)
        line_sum(half, 2)
        far_line(half)
    def rq_wait(step, carry):
        back, group = (here + step // depths) % (2 * SEQ), step % depths
        pltpu.make_async_remote_copy(
            src_ref=arr.at[group, back // SEQ, back % SEQ, :, pl.ds(PCOLS, QCOLS)],
            dst_ref=retq.at[back, group],
            send_sem=rq_send.at[back, group],
            recv_sem=rq_recv.at[back, group],
            device_id=(2 * z + back // SEQ, back % SEQ),
            device_id_type=MESH,
        ).wait()
        return carry

    lax.fori_loop(depths, depths * 2 * SEQ, rq_wait, 0)
    q_rows = lax.broadcasted_iota(jnp.int32, (2 * SEQ * ROWS, 128), 0)
    q_slots = (z * (2 * SEQ * ROWS) + q_rows).astype(F32)

    def q_weigh(source):
        found = retq[:, source].reshape(2 * SEQ * ROWS, QCOLS)
        qtok[source] = mm(mix(q_slots, qmeta[source]), found).astype(BF16)

    def q_sum(step):
        there = (z + step) % depths
        return pltpu.make_async_remote_copy(
            src_ref=qtok.at[there],
            dst_ref=rs_q.at[z],
            send_sem=rsq_send.at[there],
            recv_sem=rsq_recv.at[z],
            device_id=(depth(step), s),
            device_id_type=MESH,
        )

    for step in (2, 1, 3):
        q_weigh((z + step) % depths)
        q_sum(step).start()
    q_weigh(z)
    weigh(near_blocks)
    for half in (0, 1):
        near_sums(half, 0)
        line_sum(half, 1)
        line_sum(half, -1)
        near_line(half)

    weigh([(0, 0)])
    q_total = qtok[z].astype(F32)
    for step in (1, 2, 3):
        source = (z + step) % depths
        pltpu.make_async_remote_copy(
            src_ref=qtok.at[source],
            dst_ref=rs_q.at[source],
            send_sem=rsq_send.at[source],
            recv_sem=rsq_recv.at[source],
            device_id=(depth(step), s),
            device_id_type=MESH,
        ).wait()
        q_total = q_total + rs_q[source].astype(F32)
    out_ref[:, PCOLS:] = q_total.astype(BF16)
    for half in (0, 1):
        line_sum(half, 0)
        total = block(half, 0, 0)[...].astype(F32)
        total = total + take(half, rs_d.at[half, 0], 18) + take(half, rs_d.at[half, 1], 19)
        out_ref[:, half * (PCOLS // 2) : (half + 1) * (PCOLS // 2)] = total.astype(BF16)
    for copy in sums:
        copy.wait_send()

    def r_done(step, carry):
        source, back = step // 8, step % 8

        @pl.when(back != p)
        def _():
            r_copy(source, back).wait_send()

        return carry

    lax.fori_loop(0, 8 * SEQ, r_done, 0)

    def meta_wait(step, carry):
        plane_meta(step).wait_send()
        return carry

    lax.fori_loop(1, SEQ, meta_wait, 0)
    for step in (1, 2, 3):
        depth_meta(step).wait_send()


def run_experts(own, meta, w_in, w_out):
    rows, width = own.shape
    vmem = pl.BlockSpec(memory_space=pltpu.VMEM)
    hbm = pl.BlockSpec(memory_space=pl.ANY)
    dma = pltpu.SemaphoreType.DMA
    return pl.pallas_call(
        expert_kernel,
        in_specs=[vmem, vmem, hbm, hbm],
        out_specs=vmem,
        out_shape=jax.ShapeDtypeStruct((rows, width), BF16),
        scratch_shapes=[
            pltpu.VMEM((SEQ, rows, PCOLS), BF16),
            pltpu.VMEM((4, rows, QCOLS), BF16),
            pltpu.VMEM((SEQ, 32, rows), F32),
            pltpu.VMEM((4, 32, rows), F32),
            pltpu.VMEM((SEQ, 8, ROWS, PCOLS), BF16),
            pltpu.VMEM((4, 2 * SEQ, ROWS, QCOLS), BF16),
            pltpu.VMEM((4, 2, SEQ, ROWS, width), BF16),
            pltpu.VMEM(w_in.shape, BF16),
            pltpu.VMEM(w_out.shape, BF16),
            dma((2, 32)),
            dma((2, 32)),
            dma((4,)),
            dma((4,)),
            dma((SEQ + 4,)),
            dma((SEQ + 4,)),
            dma((SEQ, 8)),
            dma((8, SEQ)),
            dma((2 * SEQ,)),
            dma((2, SEQ)),
            dma((2,)),
            pltpu.VMEM((8, SEQ, ROWS, PCOLS), BF16),
            pltpu.VMEM((2 * SEQ, 4, ROWS, QCOLS), BF16),
            pltpu.VMEM((2, RING, 2, 64, PCOLS // 2), BF16),
            pltpu.VMEM((2, RING, 2, 128, PCOLS // 2), BF16),
            pltpu.VMEM((2, 2, 64, PCOLS // 2), BF16),
            pltpu.VMEM((2, 2, 128, PCOLS // 2), BF16),
            pltpu.VMEM((4, 128, QCOLS), BF16),
            dma((SEQ, 8)),
            dma((SEQ, 8)),
            dma((2 * SEQ, 4)),
            dma((2 * SEQ, 4)),
            dma((2, 20)),
            dma((2, 20)),
            dma((4,)),
            dma((4,)),
        ],
        compiler_params=pltpu.CompilerParams(
            collective_id=1, has_side_effects=True, vmem_limit_bytes=62 * 2**20
        ),
    )(own, meta, w_in, w_out)


def rms_scale(values, gain):
    mean = jnp.mean(values * values, axis=-1, keepdims=True)
    return values * lax.rsqrt(mean + EPS) * gain


def routing(chosen_ids, logits):
    tokens, experts = logits.shape
    table = lax.broadcasted_iota(jnp.int32, (1, 1, experts), 2)
    match = chosen_ids[:, :, None] == table
    member = jnp.any(match, axis=1)
    rows = lax.broadcasted_iota(jnp.int32, (tokens, tokens), 0)
    cols = lax.broadcasted_iota(jnp.int32, (tokens, tokens), 1)
    earlier = (rows > cols).astype(BF16)
    before = jnp.dot(earlier, member.astype(BF16), preferred_element_type=F32)
    place = jnp.sum(jnp.where(match, before[:, None, :], 0.0), axis=-1)
    picked = jnp.sum(jnp.where(match, logits[:, None, :], 0.0), axis=-1)
    return chosen_ids.astype(F32) * CAP + place, picked


def shards(
    tokens,
    span_lengths,
    state_slots,
    expert_ids,
    state_pool,
    attn_gain,
    w_query,
    w_key,
    w_value,
    w_zgate,
    w_heads,
    decay_rate,
    head_gain,
    w_output,
    moe_gain,
    router,
    w_expert_in,
    w_expert_out,
):
    local_rows, width = tokens.shape[1:]
    length = span_lengths[0]
    own_rows = tokens[0]
    head_weights = jnp.pad(w_heads.reshape(width, 4), ((0, 0), (0, 124)))
    first = lax.dynamic_index_in_dim(state_pool, state_slots[0], 0, keepdims=False)
    summed, final = attention(
        span_lengths,
        decay_rate,
        own_rows,
        attn_gain.reshape(1, width),
        w_output,
        head_weights,
        head_gain.reshape(1, 128),
        first,
        (w_query, w_key, w_value, w_zgate),
    )
    own_positions = lax.axis_index("seq") * local_rows + lax.broadcasted_iota(jnp.int32, (local_rows, 1), 0)
    own_live = (own_positions < length).astype(F32)
    attended = (summed * own_live).astype(BF16)
    residual = own_rows.astype(F32) + attended.astype(F32)
    moe_input = rms_scale(residual, moe_gain).astype(BF16)
    logits = jnp.dot(moe_input, router, preferred_element_type=F32)
    slots, picked = routing(expert_ids[0], logits)
    weights = jax.nn.softmax(picked, axis=-1) * own_live
    meta = jnp.concatenate(
        [
            jnp.pad(slots.T, ((0, 16 - TOP), (0, 0)), constant_values=-1.0),
            jnp.pad(weights.T, ((0, 16 - TOP), (0, 0))),
        ],
        axis=0,
    )
    expert_out = run_experts(moe_input, meta, w_expert_in, w_expert_out)
    return (attended[None], expert_out[None], final[None])


def solution(mesh):
    return jax.shard_map(
        shards,
        mesh=mesh,
        in_specs=(
            P("prompt", "seq", None),
            P("prompt"),
            P("prompt"),
            P("prompt", "seq", None),
            P(None, "seq", None, None),
            P(),
            P(None, "seq"),
            P(None, "seq"),
            P(None, "seq"),
            P(None, "seq"),
            P(None, None, "seq"),
            P("seq"),
            P(),
            P("seq", None),
            P(),
            P(),
            P(("prompt", "seq"), None, None),
            P(("prompt", "seq"), None, None),
        ),
        out_specs=(
            P("prompt", "seq", None),
            P("prompt", "seq", None),
            P("prompt", "seq", None, None),
        ),
        check_vma=False,
    )
```
